32 devices in a mesh: gx: 4 (over x, core), gy: 4 (over z), gz: 2 (over y).
Axes of the slice: x: 2, y: 2, z: 4, core: 2. Of those that a mesh axis runs over, the one named last changes fastest.
Arguments:
- probes: float32 [8, 32, 64, 512], P(None, 'gx', 'gy', 'gz'), may hold values from -0.011 to 0.011
- kappa2: float32 [32, 64, 512], P('gx', 'gy', 'gz'), may hold values from 0.25 to 4
- cotangents: float32 [5, 8], replicated, may hold values from -0.4375 to 0.4375
Outputs:
- kappa_grad: float32 [32, 64, 512], P('gx', 'gy', 'gz')
The draws below stay inside these ranges and needn't reach their ends.
All inputs are finite; a program needn't handle non-finite values.
Results may differ from the reference program's by a relative error of at most 0.02.
Values sent between devices are 32-bit elements; how exact they have to be, the bound alone decides.
No kernel may reach another device: no remote copies, remote signals or barrier semaphores. Data moves between devices by JAX's collectives and lax.ppermute only.
A program may use at most 64 MiB of HBM per device.

```python
import math
import jax
import jax.numpy as jnp
from jax import lax

P_SIZE = 8
NX = 32
NY = 64
NZ = 512


PROBE_SCALE = 0.00035


def draw_probes(key, part):
    first = jnp.arange(NX, dtype=jnp.float32) / max(NX - 1, 1)
    second = jnp.arange(NY, dtype=jnp.float32) / max(NY - 1, 1)
    third = jnp.arange(NZ, dtype=jnp.float32) / max(NZ - 1, 1)
    envelope = jnp.sqrt((1.0 + 2.0 * first)[:, None, None] * (1.0 + 2.0 * second)[None, :, None] * (1.0 + 2.0 * third)[None, None, :])
    values = jax.random.truncated_normal(key, -6.0, 6.0, (P_SIZE, NX, NY, NZ), jnp.float32)
    return (values * envelope[None] * PROBE_SCALE).astype(jnp.float32)


def steps_of(key, shape, pieces, smallest, top_value):
    level = 1.0
    for axis_at, blocks in pieces:
        steps = jax.random.uniform(jax.random.fold_in(jax.random.fold_in(key, 6), axis_at), (blocks,), jnp.float32, smallest / len(pieces), top_value / len(pieces))
        level = level * jnp.repeat(jnp.exp(steps), shape[axis_at] // blocks).reshape((-1,) + (1,) * (len(shape) - 1 - axis_at))
    return level


def scatter_about(rng, shape, width, most, kind=jnp.bfloat16):
    return jnp.clip(width * jax.random.normal(rng, shape, jnp.float32), -most, most).astype(kind)


def setup_inputs(seed: int = 0) -> dict:
    key_list = jax.random.split(jax.random.key(seed), 4)
    probes = draw_probes(jax.random.fold_in(key_list[3], 71), 0)
    kappa2 = jnp.clip(jnp.exp(math.log(4.0) - 2.7725887 * jax.random.uniform(key_list[1], (NX, NY, NZ), jnp.float32) ** steps_of(key_list[1], (NX, NY, NZ), ((0, 4), (1, 4), (2, 2)), -0.2, 0.2)), 0.25, 4.0)
    cotangents = scatter_about(key_list[2], (5, P_SIZE), 0.03, 0.4375, jnp.float32)
    return dict(probes=probes, kappa2=kappa2, cotangents=cotangents)


EPSILON = 1e-06

def stencil_apply(field, kappa2):
    padded = jnp.pad(field, 1)
    total = padded[2:, 1:-1, 1:-1] + padded[:-2, 1:-1, 1:-1]
    total = total + padded[1:-1, 2:, 1:-1] + padded[1:-1, :-2, 1:-1]
    total = total + padded[1:-1, 1:-1, 2:] + padded[1:-1, 1:-1, :-2]
    return (6.0 + kappa2) * field - total

def squared_apply(field, kappa2):
    return stencil_apply(stencil_apply(field, kappa2), kappa2)

def lanczos_loss(kappa2, probe, weights):
    first_basis = probe / jnp.sqrt(jnp.mean(probe * probe) + EPSILON)
    first_image = squared_apply(first_basis, kappa2)
    first_alpha = jnp.mean(first_basis * first_image)
    first_rest = first_image - first_alpha * first_basis
    first_beta = jnp.sqrt(jnp.mean(first_rest * first_rest) + EPSILON)
    second_basis = first_rest / first_beta
    second_image = squared_apply(second_basis, kappa2) - first_beta * first_basis
    second_alpha = jnp.mean(second_basis * second_image)
    second_rest = second_image - second_alpha * second_basis
    second_beta = jnp.sqrt(jnp.mean(second_rest * second_rest) + EPSILON)
    third_basis = second_rest / second_beta
    third_image = squared_apply(third_basis, kappa2) - second_beta * second_basis
    third_alpha = jnp.mean(third_basis * third_image)
    return weights[0] * first_alpha + weights[1] * second_alpha + weights[2] * third_alpha + weights[3] * first_beta + weights[4] * second_beta

def reference(probes, kappa2, cotangents):
    gradient_fn = jax.grad(lanczos_loss)

    def accumulate(index, total):
        return total + gradient_fn(kappa2, probes[index], cotangents[:, index])
    total = lax.fori_loop(0, P_SIZE, accumulate, jnp.zeros_like(kappa2))
    return total * float(NX * NY * NZ)
```

```python
import functools

import jax
import jax.numpy as jnp
from jax import lax
from jax.experimental import pallas as pl
from jax.experimental.pallas import tpu as pltpu
from jax.sharding import PartitionSpec as P

EPSILON = 1e-06
SHIFT = 64.0
DEPTH = 9
KAPPA_HALO = 8
MIB = 1024 * 1024


def loss_of_moments(moments, weights):
    m0, m1, m2, m3, m4, m5 = moments
    norm = m0 + EPSILON
    alpha1 = (m1 + SHIFT * m0) / norm
    e1 = SHIFT - alpha1
    rest1 = jnp.maximum(m2 + 2.0 * e1 * m1 + e1 * e1 * m0, 0.0)
    beta1_square = rest1 / norm + EPSILON
    beta1 = jnp.sqrt(beta1_square)
    scale = 1.0 / (norm * beta1_square)
    alpha2 = scale * (m3 + 2.0 * e1 * m2 + e1 * e1 * m1 + SHIFT * rest1) - (m1 + e1 * m0) / norm
    e2 = SHIFT - alpha2
    f1 = e1 + e2
    f0 = e1 * e2 - beta1_square
    g = f1 * f1 + 2.0 * f0
    rest2 = jnp.maximum(m4 + 2.0 * f1 * m3 + g * m2 + 2.0 * f1 * f0 * m1 + f0 * f0 * m0, 0.0)
    beta2_square = scale * rest2 + EPSILON
    beta2 = jnp.sqrt(beta2_square)
    image2 = m5 + 2.0 * f1 * m4 + g * m3 + 2.0 * f1 * f0 * m2 + f0 * f0 * m1
    cross = m3 + f1 * m2 + f0 * m1 + e1 * (m2 + f1 * m1 + f0 * m0)
    alpha3 = scale * ((image2 + SHIFT * rest2) / beta2_square - cross)
    return (
        weights[0] * alpha1
        + weights[1] * alpha2
        + weights[2] * alpha3
        + weights[3] * beta1
        + weights[4] * beta2
    )


def shifted(value, step, axis):
    tile = (8, 128)[axis]
    size = value.shape[axis]
    rolled = pltpu.roll(value, step % size, axis)
    at = 0 if step > 0 else size - tile
    edge = lax.slice_in_dim(rolled, at, at + tile, axis=axis)
    index = lax.broadcasted_iota(jnp.int32, edge.shape, axis)
    edge = jnp.where(index == (0 if step > 0 else tile - 1), 0.0, edge)
    if step > 0:
        parts = [edge, lax.slice_in_dim(rolled, tile, size, axis=axis)]
    else:
        parts = [lax.slice_in_dim(rolled, 0, size - tile, axis=axis), edge]
    return jnp.concatenate(parts, axis=axis)


def stencil_row(ref, at, diagonal):
    centre = ref[at]
    total = ref[at - 1] + ref[at + 1]
    total = total + shifted(centre, 1, 0) + shifted(centre, -1, 0)
    total = total + shifted(centre, 1, 1) + shifted(centre, -1, 1)
    return diagonal * centre - total


class Field:
    def __init__(self, ref, halo):
        self.ref = ref
        self.halo = halo

    def row(self, at):
        return self.ref[at + self.halo]

    def rows(self, own, halo):
        return self.ref.at[pl.ds(self.halo - halo, own + 2 * halo)]


def apply_steps(bounds_ref, own, target, source, diagonal, minus=None):
    halo = target.halo
    first = jnp.maximum(-halo, bounds_ref[0])
    last = jnp.minimum(own + halo, bounds_ref[1])
    if halo:
        zero = jnp.zeros(target.ref.shape[1:], jnp.float32)
        target.ref[halo - 1] = zero
        target.ref[halo + own] = zero

    def body(row, carry):
        value = stencil_row(source.ref, row + source.halo, diagonal.row(row))
        if minus is not None:
            value = value - SHIFT * minus.row(row)
        target.ref[row + halo] = value
        return carry

    lax.fori_loop(first, last, body, 0)


def tile_sum(value):
    total = None
    for x in range(0, value.shape[0], 8):
        for z in range(0, value.shape[1], 128):
            part = value[x : x + 8, z : z + 128]
            total = part if total is None else total + part
    return total


def column_copies(whole, columns, sem, inward):
    copies = []
    for index in range(columns.shape[0]):
        pair = (whole.at[:, pl.ds(index * 128, 128)], columns.at[index])
        source, target = pair if inward else pair[::-1]
        copies.append(pltpu.make_async_copy(source, target, sem.at[index]))
    return copies


def column_places(grid):
    nx, nz, bx, by, bz = grid
    for s in range(nx * nz):
        for column in range(bz // 128):
            z = (s % nz) * bz + column * 128
            yield s, column, pl.ds((s // nz) * bx, bx), pl.ds(z, 128)


def assemble_kernel(grid, blocks_ref, own_ref, low_ref, high_ref, columns_ref, sem):
    nx, nz, bx, by, bz = grid
    copies = column_copies(blocks_ref, columns_ref, sem, True)
    for copy in copies:
        copy.start()
    for copy in copies:
        copy.wait()
    for s, column, xs, zs in column_places(grid):
        for y in range(by):
            value = columns_ref[column, pl.ds(s * bx * by + y, bx, stride=by), :]
            own_ref[y, xs, zs] = value
            if y < DEPTH:
                low_ref[y, xs, zs] = value
            if y >= by - DEPTH:
                high_ref[y - (by - DEPTH), xs, zs] = value


def first_kernel(
    grid,
    bounds_ref, own_ref, low_ref, high_ref, kappa_ref,
    d0_out, c1_out, d1_out, c2_out, d2_out, diagonal_out, moments_ref,
    c0_ref, d0_ref, c1_ref, d1_ref, c2_ref, d2_ref, diagonal_ref, columns_ref,
    in_sem, out_sem, columns_sem,
):
    nx, nz, bx, by, bz = grid
    kappa_copies = column_copies(kappa_ref, columns_ref, columns_sem, True)
    for copy in kappa_copies:
        copy.start()
    arrivals = [
        pltpu.make_async_copy(low_ref, c0_ref.at[pl.ds(0, DEPTH)], in_sem.at[0]),
        pltpu.make_async_copy(own_ref, c0_ref.at[pl.ds(DEPTH, by)], in_sem.at[1]),
        pltpu.make_async_copy(high_ref, c0_ref.at[pl.ds(DEPTH + by, DEPTH)], in_sem.at[2]),
    ]
    for copy in arrivals:
        copy.start()
    ext = by + 2 * KAPPA_HALO

    def diagonal_row(y, carry):
        for s, column, xs, zs in column_places(grid):
            value = columns_ref[column, pl.ds(s * bx * ext + y, bx, stride=ext), :]
            diagonal_ref[y, xs, zs] = 6.0 + value
        return carry

    for copy in kappa_copies:
        copy.wait()
    lax.fori_loop(0, ext, diagonal_row, 0)
    c0 = Field(c0_ref, 9)
    d0 = Field(d0_ref, 8)
    c1 = Field(c1_ref, 7)
    d1 = Field(d1_ref, 6)
    c2 = Field(c2_ref, 5)
    d2 = Field(d2_ref, 4)
    diagonal = Field(diagonal_ref, KAPPA_HALO)
    departures = []

    def depart(field, halo, out):
        copy = pltpu.make_async_copy(field.rows(by, halo), out, out_sem.at[len(departures)])
        copy.start()
        departures.append(copy)

    depart(diagonal, 3, diagonal_out)
    for copy in arrivals:
        copy.wait()
    steps = functools.partial(apply_steps, bounds_ref, by)
    steps(d0, c0, diagonal)
    depart(d0, 0, d0_out)
    steps(c1, d0, diagonal, c0)
    depart(c1, 0, c1_out)
    steps(d1, c1, diagonal)
    depart(d1, 0, d1_out)
    steps(c2, d1, diagonal, c1)
    depart(c2, 3, c2_out)
    steps(d2, c2, diagonal)
    depart(d2, 4, d2_out)

    def moment_row(row, sums):
        a, b, c, d = c0.row(row), c1.row(row), c2.row(row), d2.row(row)
        pairs = ((a, a), (a, b), (b, b), (b, c), (c, c), (d, d))
        return tuple(total + tile_sum(u * v) for total, (u, v) in zip(sums, pairs))

    zero = jnp.zeros((8, 128), jnp.float32)
    sums = lax.fori_loop(0, by, moment_row, (zero,) * 6)
    for index, total in enumerate(sums):
        moments_ref[index] = total
    for copy in departures:
        copy.wait()


def second_kernel(
    grid, inverse_count, parts,
    bounds_ref, weights_ref, moments_ref,
    c0_in, d0_in, c1_in, d1_in, c2_in, d2_in, diagonal_in,
    out_ref,
    c0_ref, d0_ref, c1_ref, d1_ref, c2_ref, d2_ref, diagonal_ref,
    c3_ref, d3_ref, c4_ref, columns_ref, in_sem, out_sem,
):
    nx, nz, bx, by, bz = grid
    pairs = (
        (diagonal_in, diagonal_ref), (c2_in, c2_ref), (d2_in, d2_ref), (c0_in, c0_ref),
        (d0_in, d0_ref), (c1_in, c1_ref), (d1_in, d1_ref),
    )
    copies = [
        pltpu.make_async_copy(source, target, in_sem.at[index])
        for index, (source, target) in enumerate(pairs)
    ]
    for copy in copies:
        copy.start()
    raw = []
    for k in range(6):
        total = moments_ref[k]
        for part in range(1, parts):
            total = total + moments_ref[part * 6 + k]
        total = jnp.sum(jnp.sum(total, axis=0, keepdims=True), axis=1, keepdims=True)
        raw.append(jnp.broadcast_to(total * inverse_count, (8, 128)))
    moments = tuple(raw[:5]) + (raw[5] - SHIFT * raw[4],)
    weights = [weights_ref[k] for k in range(5)]
    value, pullback = jax.vjp(lambda m: loss_of_moments(m, weights), moments)
    (slopes,) = pullback(jnp.full((8, 128), 2.0, jnp.float32))
    slopes = [slope[0, 0] for slope in slopes]

    for copy in copies[:3]:
        copy.wait()
    c0, d0, c1, d1 = (Field(ref, 0) for ref in (c0_ref, d0_ref, c1_ref, d1_ref))
    c2 = Field(c2_ref, 3)
    d2 = Field(d2_ref, 4)
    c3 = Field(c3_ref, 3)
    d3 = Field(d3_ref, 2)
    c4 = Field(c4_ref, 1)
    diagonal = Field(diagonal_ref, 3)
    steps = functools.partial(apply_steps, bounds_ref, by)
    steps(c3, d2, diagonal, c2)
    steps(d3, c3, diagonal)
    steps(c4, d3, diagonal, c3)
    for copy in copies[3:]:
        copy.wait()

    def out_row(row, carry):
        d4 = stencil_row(c4.ref, row + 1, diagonal.row(row))
        cs = [field.row(row) for field in (c0, c1, c2, c3, c4)]
        ds = [field.row(row) for field in (d0, d1, d2, d3)] + [d4]
        total = None
        for i in range(5):
            inner = None
            for j in range(5 - i):
                term = slopes[i + j + 1] * ds[j]
                inner = term if inner is None else inner + term
            term = cs[i] * inner
            total = term if total is None else total + term
        for s, column, xs, zs in column_places(grid):
            part = total[xs.start : xs.start + bx, zs.start : zs.start + 128]
            columns_ref[column, pl.ds(s * bx * by + row, bx, stride=by), :] = part
        return carry

    lax.fori_loop(0, by, out_row, 0)
    copies = column_copies(out_ref, columns_ref, out_sem, False)
    for copy in copies:
        copy.start()
    for copy in copies:
        copy.wait()


def vmem():
    return pl.BlockSpec(memory_space=pltpu.VMEM)


def smem():
    return pl.BlockSpec(memory_space=pltpu.SMEM)


def anywhere():
    return pl.BlockSpec(memory_space=pl.ANY)


def f32(*shape):
    return jax.ShapeDtypeStruct(shape, jnp.float32)


def body(probes, kappa2, cotangents):
    nx, ny, nz = (lax.axis_size(axis) for axis in ("gx", "gy", "gz"))
    count, bx, by, bz = probes.shape
    group = nx * nz
    assert group % count == 0
    copies = group // count
    X, Z = nx * bx, nz * bz
    grid = (nx, nz, bx, by, bz)
    gy = lax.axis_index("gy")
    mine = (lax.axis_index("gx") * nz + lax.axis_index("gz")) % count
    up = [(i, i + 1) for i in range(ny - 1)]
    down = [(target, source) for source, target in up]

    def scratch(rows):
        return pltpu.VMEM((rows, X, Z), jnp.float32)

    def columns_of(rows):
        return pltpu.VMEM((bz // 128, rows, 128), jnp.float32)

    low = lax.ppermute(kappa2[:, by - KAPPA_HALO :], "gy", up)
    high = lax.ppermute(kappa2[:, :KAPPA_HALO], "gy", down)
    kappa = jnp.concatenate([low, kappa2, high], axis=1)
    kappa = lax.all_gather(kappa, ("gx", "gz"), axis=0, tiled=False)
    kappa = kappa.reshape(group * bx * (by + 2 * KAPPA_HALO), bz)

    blocks = jnp.concatenate([probes] * copies, axis=0) if copies > 1 else probes
    blocks = lax.all_to_all(blocks, ("gx", "gz"), 0, 0, tiled=True)
    own, first, last = pl.pallas_call(
        functools.partial(assemble_kernel, grid),
        out_shape=(f32(by, X, Z), f32(DEPTH, X, Z), f32(DEPTH, X, Z)),
        in_specs=[anywhere()],
        out_specs=(vmem(),) * 3,
        scratch_shapes=[columns_of(group * bx * by), pltpu.SemaphoreType.DMA((bz // 128,))],
        compiler_params=pltpu.CompilerParams(vmem_limit_bytes=24 * MIB),
        name="assemble",
    )(blocks.reshape(group * bx * by, bz))
    low = lax.ppermute(last, "gy", up)
    high = lax.ppermute(first, "gy", down)

    bounds = jnp.stack(
        [jnp.where(gy == 0, 0, -DEPTH), jnp.where(gy == ny - 1, by, by + DEPTH)]
    ).astype(jnp.int32)

    d0, c1, d1, c2, d2, diagonal, moments = pl.pallas_call(
        functools.partial(first_kernel, grid),
        out_shape=(
            f32(by, X, Z), f32(by, X, Z), f32(by, X, Z), f32(by + 6, X, Z), f32(by + 8, X, Z),
            f32(by + 6, X, Z), f32(6, 8, 128),
        ),
        in_specs=[smem()] + [anywhere()] * 4,
        out_specs=(anywhere(),) * 6 + (vmem(),),
        scratch_shapes=[scratch(by + 2 * halo) for halo in (9, 8, 7, 6, 5, 4, KAPPA_HALO)]
        + [
            columns_of(group * bx * (by + 2 * KAPPA_HALO)),
            pltpu.SemaphoreType.DMA((3,)),
            pltpu.SemaphoreType.DMA((6,)),
            pltpu.SemaphoreType.DMA((bz // 128,)),
        ],
        compiler_params=pltpu.CompilerParams(vmem_limit_bytes=48 * MIB),
        name="first_steps",
    )(bounds, own, low, high, kappa)

    shares = [moments]
    for step in range(1, ny):
        shares.append(lax.ppermute(moments, "gy", [(i, (i + step) % ny) for i in range(ny)]))
    moments = jnp.concatenate(shares, axis=0)

    weights = lax.dynamic_slice_in_dim(cotangents, mine, 1, axis=1)[:, 0]
    inverse_count = 1.0 / (X * by * ny * Z)
    out = pl.pallas_call(
        functools.partial(second_kernel, grid, inverse_count, ny),
        out_shape=f32(group * bx * by, bz),
        in_specs=[smem(), smem(), vmem()] + [anywhere()] * 7,
        out_specs=anywhere(),
        scratch_shapes=[
            scratch(rows)
            for rows in (by, by, by, by, by + 6, by + 8, by + 6, by + 6, by + 4, by + 2)
        ]
        + [
            columns_of(group * bx * by),
            pltpu.SemaphoreType.DMA((7,)),
            pltpu.SemaphoreType.DMA((bz // 128,)),
        ],
        compiler_params=pltpu.CompilerParams(vmem_limit_bytes=48 * MIB),
        name="last_steps",
    )(bounds, weights, moments, own, d0, c1, d1, c2, d2, diagonal)

    out = lax.all_to_all(out.reshape(group, bx, by, bz), ("gx", "gz"), 0, 0, tiled=True)
    return jnp.sum(out[:count], axis=0)


def solution(mesh):
    return jax.shard_map(
        body,
        mesh=mesh,
        in_specs=(P(None, "gx", "gy", "gz"), P("gx", "gy", "gz"), P()),
        out_specs=P("gx", "gy", "gz"),
        check_vma=False,
    )
```

```python
import functools

import jax
import jax.numpy as jnp
from jax import lax
from jax.experimental import pallas as pl
from jax.experimental.pallas import tpu as pltpu
from jax.sharding import PartitionSpec as P

EPSILON = 1e-06
SHIFT = 64.0
HALO = 5
DIAGONAL_HALO = 4
PAD = 8
MIB = 1024 * 1024


def loss_of_moments(moments, weights):
    m0, m1, m2, m3, m4, m5 = moments
    norm = m0 + EPSILON
    alpha1 = (m1 + SHIFT * m0) / norm
    e1 = SHIFT - alpha1
    rest1 = jnp.maximum(m2 + 2.0 * e1 * m1 + e1 * e1 * m0, 0.0)
    beta1_square = rest1 / norm + EPSILON
    beta1 = jnp.sqrt(beta1_square)
    scale = 1.0 / (norm * beta1_square)
    alpha2 = scale * (m3 + 2.0 * e1 * m2 + e1 * e1 * m1 + SHIFT * rest1) - (m1 + e1 * m0) / norm
    e2 = SHIFT - alpha2
    f1 = e1 + e2
    f0 = e1 * e2 - beta1_square
    g = f1 * f1 + 2.0 * f0
    rest2 = jnp.maximum(m4 + 2.0 * f1 * m3 + g * m2 + 2.0 * f1 * f0 * m1 + f0 * f0 * m0, 0.0)
    beta2_square = scale * rest2 + EPSILON
    beta2 = jnp.sqrt(beta2_square)
    image2 = m5 + 2.0 * f1 * m4 + g * m3 + 2.0 * f1 * f0 * m2 + f0 * f0 * m1
    cross = m3 + f1 * m2 + f0 * m1 + e1 * (m2 + f1 * m1 + f0 * m0)
    alpha3 = scale * ((image2 + SHIFT * rest2) / beta2_square - cross)
    return (
        weights[0] * alpha1
        + weights[1] * alpha2
        + weights[2] * alpha3
        + weights[3] * beta1
        + weights[4] * beta2
    )


class Field:
    def __init__(self, ref, halo):
        self.ref = ref
        self.halo = halo
        self.columns, self.rows, self.pitch, _ = ref.shape
        self.cells = self.pitch - PAD
        self.flat = ref.reshape(self.columns * self.rows * self.pitch, 128)

    def at(self, column, row, x):
        moving, fixed = row
        start = (column * self.rows + fixed + self.halo) * self.pitch + x
        return pl.ds(moving * self.pitch + start, 8)

    def load(self, column, row, x):
        return self.flat[self.at(column, row, x), :]

    def store(self, column, row, x, value):
        self.flat[self.at(column, row, x), :] = value

    def part(self, first, count):
        return self.ref.at[:, pl.ds(first + self.halo, count), pl.ds(0, self.cells), :]

    def clear_pads(self):
        zero = jnp.zeros((8, 128), jnp.float32)

        def body(row, carry):
            for column in range(self.columns):
                self.store(column, (row, -self.halo), self.cells, zero)
            return carry

        lax.fori_loop(0, self.rows, body, 0)

    def clear_row(self, row):
        zero = jnp.zeros((8, 128), jnp.float32)
        for column in range(self.columns):
            for x in range(0, self.cells, 8):
                self.store(column, (0, row), x, zero)


def lane_masks():
    lane = lax.broadcasted_iota(jnp.int32, (8, 128), 1)
    return lane == 0, lane == 127


def stencil_tiles(source, diagonal, row, x, masks):
    columns = range(source.columns)
    moving, fixed = row
    centre = [source.load(c, row, x) for c in columns]
    after = [pltpu.roll(value, 1, 1) for value in centre]
    before = [pltpu.roll(value, 127, 1) for value in centre]
    results = []
    for c in columns:
        low = after[c - 1] if c else 0.0
        high = before[c + 1] if c + 1 < source.columns else 0.0
        total = jnp.where(masks[0], low, after[c]) + jnp.where(masks[1], high, before[c])
        total = total + (source.load(c, row, x - 1) + source.load(c, row, x + 1))
        total = total + (source.load(c, (moving, fixed - 1), x) + source.load(c, (moving, fixed + 1), x))
        results.append(diagonal.load(c, row, x) * centre[c] - total)
    return results


def apply_rows(target, source, diagonal, first, count, minus=None, unroll=2):
    masks = lane_masks()

    def body(step, carry):
        for offset in range(unroll):
            row = (step * unroll, first + offset)
            for x in range(0, source.cells, 8):
                values = stencil_tiles(source, diagonal, row, x, masks)
                for c, value in enumerate(values):
                    if minus is not None:
                        value = value - SHIFT * minus.load(c, row, x)
                    target.store(c, row, x, value)
        return carry

    assert count % unroll == 0
    lax.fori_loop(0, count // unroll, body, 0)


def clear_outside(ends_ref, own, field):
    @pl.when(ends_ref[0] == 1)
    def _():
        field.clear_row(-1)

    @pl.when(ends_ref[1] == 1)
    def _():
        field.clear_row(own)


def apply_steps(ends_ref, own, target, source, diagonal, halo, minus=None):
    apply_rows(target, source, diagonal, -halo, own + 2 * halo, minus)
    if halo:
        clear_outside(ends_ref, own, target)


def column_copies(whole, columns, sem, inward):
    copies = []
    for index in range(columns.shape[0]):
        pair = (whole.at[:, pl.ds(index * 128, 128)], columns.at[index])
        source, target = pair if inward else pair[::-1]
        copies.append(pltpu.make_async_copy(source, target, sem.at[index]))
    return copies


def start_all(pairs, sem):
    copies = []
    for index, (source, target) in enumerate(pairs):
        copy = pltpu.make_async_copy(source, target, sem.at[index])
        copy.start()
        copies.append(copy)
    return copies


def places(grid):
    nx, nz, bx, by, bz = grid
    per = bz // 128
    for s in range(nx * nz):
        for column in range(per):
            yield (s // nz) * bx, (s % nz) * per + column, s, column


def assemble_kernel(
    grid, blocks_ref, kappa_ref,
    own_ref, diagonal_ref, up_ref, down_ref,
    block_columns, kappa_columns, block_sem, kappa_sem,
):
    nx, nz, bx, by, bz = grid
    copies = column_copies(blocks_ref, block_columns, block_sem, True)
    copies += column_copies(kappa_ref, kappa_columns, kappa_sem, True)
    for copy in copies:
        copy.start()
    for copy in copies:
        copy.wait()
    for x, z, s, column in places(grid):
        xs = pl.ds(x, bx)
        for y in range(by):
            rows = pl.ds(s * bx * by + y, bx, stride=by)
            value = block_columns[column, rows, :]
            own_ref[z, y, xs, :] = value
            if y < HALO:
                down_ref[z, y, xs, :] = value
            if y >= by - HALO:
                up_ref[z, y - (by - HALO), xs, :] = value
            value = 6.0 + kappa_columns[column, rows, :]
            diagonal_ref[z, y, xs, :] = value
            if y < DIAGONAL_HALO:
                down_ref[z, HALO + y, xs, :] = value
            if y >= by - DIAGONAL_HALO:
                up_ref[z, HALO + y - (by - DIAGONAL_HALO), xs, :] = value


def halo_pairs(field, own, low_ref, high_ref, start, halo):
    rows = pl.ds(start, halo)
    return [
        (low_ref.at[:, rows], field.part(-halo, halo)),
        (high_ref.at[:, rows], field.part(own, halo)),
    ]


def first_kernel(
    grid,
    ends_ref, own_in, diagonal_in, low_in, high_in,
    d0_out, c1_out, d1_out, c2_out, up_out, down_out,
    c0_ref, d0_ref, c1_ref, d1_ref, c2_ref, diagonal_ref, in_sem, out_sem,
):
    nx, nz, bx, by, bz = grid
    c0 = Field(c0_ref, 5)
    d0 = Field(d0_ref, 4)
    c1 = Field(c1_ref, 3)
    d1 = Field(d1_ref, 2)
    c2 = Field(c2_ref, 1)
    diagonal = Field(diagonal_ref, DIAGONAL_HALO)
    arrivals = start_all(
        [(own_in, c0.part(0, by)), (diagonal_in, diagonal.part(0, by))]
        + halo_pairs(c0, by, low_in, high_in, 0, HALO)
        + halo_pairs(diagonal, by, low_in, high_in, HALO, DIAGONAL_HALO),
        in_sem,
    )
    for field in (c0, d0, c1, d1, c2):
        field.clear_pads()
    departures = []

    def depart(source, out):
        copy = pltpu.make_async_copy(source, out, out_sem.at[len(departures)])
        copy.start()
        departures.append(copy)

    for copy in arrivals:
        copy.wait()
    steps = functools.partial(apply_steps, ends_ref, by)
    steps(d0, c0, diagonal, 4)
    depart(d0.part(0, by), d0_out)
    steps(c1, d0, diagonal, 3, c0)
    depart(c1.part(0, by), c1_out)
    steps(d1, c1, diagonal, 2)
    depart(d1.part(0, by), d1_out)
    steps(c2, d1, diagonal, 1, c1)
    depart(c2.part(by - HALO, HALO), up_out)
    depart(c2.part(0, HALO), down_out)
    depart(c2.part(-1, by + 2), c2_out)
    for copy in departures:
        copy.wait()


def middle_kernel(
    grid,
    c0_in, c1_in, c2_in, diagonal_in,
    d2_out, moments_ref,
    c0_ref, c1_ref, c2_ref, d2_ref, diagonal_ref, in_sem, out_sem,
):
    nx, nz, bx, by, bz = grid
    c0 = Field(c0_ref, 0)
    c1 = Field(c1_ref, 0)
    c2 = Field(c2_ref, 1)
    d2 = Field(d2_ref, 0)
    diagonal = Field(diagonal_ref, 0)
    copies = start_all(
        [
            (c2_in, c2.part(-1, by + 2)), (diagonal_in, diagonal.part(0, by)),
            (c0_in, c0.part(0, by)), (c1_in, c1.part(0, by)),
        ],
        in_sem,
    )
    c2.clear_pads()
    for copy in copies[:2]:
        copy.wait()
    apply_rows(d2, c2, diagonal, 0, by)
    out = pltpu.make_async_copy(d2.part(0, by), d2_out, out_sem.at[0])
    out.start()
    for copy in copies[2:]:
        copy.wait()

    def moment_row(step, sums):
        row = (step, 0)
        for x in range(0, c0.cells, 8):
            for c in range(c0.columns):
                a, b, e, d = (field.load(c, row, x) for field in (c0, c1, c2, d2))
                pairs = ((a, a), (a, b), (b, b), (b, e), (e, e), (d, d))
                sums = tuple(total + u * v for total, (u, v) in zip(sums, pairs))
        return sums

    zero = jnp.zeros((8, 128), jnp.float32)
    sums = lax.fori_loop(0, by, moment_row, (zero,) * 6)
    for index, total in enumerate(sums):
        moments_ref[index] = total
    out.wait()


def moment_slopes(inverse_count, parts, weights_ref, moments_ref):
    raw = []
    for k in range(6):
        total = moments_ref[k]
        for part in range(1, parts):
            total = total + moments_ref[part * 6 + k]
        total = jnp.sum(jnp.sum(total, axis=0, keepdims=True), axis=1, keepdims=True)
        raw.append(jnp.broadcast_to(total * inverse_count, (8, 128)))
    moments = tuple(raw[:5]) + (raw[5] - SHIFT * raw[4],)
    weights = [weights_ref[k] for k in range(5)]
    value, pullback = jax.vjp(lambda m: loss_of_moments(m, weights), moments)
    (slopes,) = pullback(jnp.full((8, 128), 2.0, jnp.float32))
    return [slope[0, 0] for slope in slopes]


def last_kernel(
    grid, inverse_count, parts,
    ends_ref, weights_ref, moments_ref,
    c0_in, d0_in, c1_in, d1_in, c2_in, d2_in, diagonal_in, low1_in, high1_in, low2_in, high2_in,
    out_ref,
    c0_ref, d0_ref, c1_ref, d1_ref, c2_ref, d2_ref, diagonal_ref, c3_ref, d3_ref, c4_ref,
    columns_ref, in_sem, out_sem,
):
    nx, nz, bx, by, bz = grid
    c0, d0, c1, d1 = (Field(ref, 0) for ref in (c0_ref, d0_ref, c1_ref, d1_ref))
    c2 = Field(c2_ref, HALO)
    d2 = Field(d2_ref, 4)
    c3 = Field(c3_ref, 3)
    d3 = Field(d3_ref, 2)
    c4 = Field(c4_ref, 1)
    diagonal = Field(diagonal_ref, DIAGONAL_HALO)
    copies = start_all(
        [(diagonal_in, diagonal.part(0, by)), (c2_in.at[:, pl.ds(1, by)], c2.part(0, by))]
        + halo_pairs(diagonal, by, low1_in, high1_in, HALO, DIAGONAL_HALO)
        + halo_pairs(c2, by, low2_in, high2_in, 0, HALO)
        + [
            (d2_in, d2.part(0, by)), (c0_in, c0.part(0, by)), (d0_in, d0.part(0, by)),
            (c1_in, c1.part(0, by)), (d1_in, d1.part(0, by)),
        ],
        in_sem,
    )
    for field in (c2, d2, c3, d3, c4):
        field.clear_pads()
    slopes = moment_slopes(inverse_count, parts, weights_ref, moments_ref)
    for copy in copies[:6]:
        copy.wait()
    apply_rows(d2, c2, diagonal, -4, 4)
    apply_rows(d2, c2, diagonal, by, 4)
    clear_outside(ends_ref, by, d2)
    copies[6].wait()
    steps = functools.partial(apply_steps, ends_ref, by)
    steps(c3, d2, diagonal, 3, c2)
    steps(d3, c3, diagonal, 2)
    steps(c4, d3, diagonal, 1, c3)
    for copy in copies[7:]:
        copy.wait()
    masks = lane_masks()
    place = {(x, z): (s, column) for x, z, s, column in places(grid)}

    def out_row(step, carry):
        row = (step, 0)
        for x in range(0, c4.cells, 8):
            last = stencil_tiles(c4, diagonal, row, x, masks)
            for z in range(c4.columns):
                cs = [field.load(z, row, x) for field in (c0, c1, c2, c3, c4)]
                ds = [field.load(z, row, x) for field in (d0, d1, d2, d3)] + [last[z]]
                total = None
                for i in range(5):
                    inner = None
                    for j in range(5 - i):
                        term = slopes[i + j + 1] * ds[j]
                        inner = term if inner is None else inner + term
                    term = cs[i] * inner
                    total = term if total is None else total + term
                s, column = place[x, z]
                columns_ref[column, pl.ds(s * bx * by + step, bx, stride=by), :] = total
        return carry

    lax.fori_loop(0, by, out_row, 0)
    copies = column_copies(out_ref, columns_ref, out_sem, False)
    for copy in copies:
        copy.start()
    for copy in copies:
        copy.wait()


def vmem():
    return pl.BlockSpec(memory_space=pltpu.VMEM)


def smem():
    return pl.BlockSpec(memory_space=pltpu.SMEM)


def anywhere():
    return pl.BlockSpec(memory_space=pl.ANY)


def f32(*shape):
    return jax.ShapeDtypeStruct(shape, jnp.float32)


def params():
    return pltpu.CompilerParams(vmem_limit_bytes=60 * MIB)


def body(probes, kappa2, cotangents):
    nx, ny, nz = (lax.axis_size(axis) for axis in ("gx", "gy", "gz"))
    count, bx, by, bz = probes.shape
    group = nx * nz
    assert group % count == 0 and bx == 8 and by % 2 == 0 and by >= HALO and bz % 128 == 0
    copies = group // count
    X = nx * bx
    columns = nz * bz // 128
    per = bz // 128
    grid = (nx, nz, bx, by, bz)
    gy = lax.axis_index("gy")
    mine = (lax.axis_index("gx") * nz + lax.axis_index("gz")) % count
    up = [(i, i + 1) for i in range(ny - 1)]
    down = [(target, source) for source, target in up]

    def rows_of(rows):
        return f32(columns, rows, X, 128)

    def scratch(rows):
        return pltpu.VMEM((columns, rows, X + PAD, 128), jnp.float32)

    def block_scratch():
        return pltpu.VMEM((per, group * bx * by, 128), jnp.float32)

    dma = pltpu.SemaphoreType.DMA

    kappa = lax.all_gather(kappa2, ("gx", "gz"), axis=0, tiled=False)
    blocks = jnp.concatenate([probes] * copies, axis=0) if copies > 1 else probes
    blocks = lax.all_to_all(blocks, ("gx", "gz"), 0, 0, tiled=True)
    c0, diagonal, up_edge, down_edge = pl.pallas_call(
        functools.partial(assemble_kernel, grid),
        out_shape=(
            rows_of(by), rows_of(by), rows_of(HALO + DIAGONAL_HALO), rows_of(HALO + DIAGONAL_HALO)
        ),
        in_specs=[anywhere(), anywhere()],
        out_specs=(vmem(),) * 4,
        scratch_shapes=[block_scratch(), block_scratch(), dma((per,)), dma((per,))],
        compiler_params=params(),
        name="assemble",
    )(blocks.reshape(group * bx * by, bz), kappa.reshape(group * bx * by, bz))
    low1 = lax.ppermute(up_edge, "gy", up)
    high1 = lax.ppermute(down_edge, "gy", down)

    ends = jnp.stack([gy == 0, gy == ny - 1]).astype(jnp.int32)
    d0, c1, d1, c2, up_edge, down_edge = pl.pallas_call(
        functools.partial(first_kernel, grid),
        out_shape=(rows_of(by),) * 3 + (rows_of(by + 2), rows_of(HALO), rows_of(HALO)),
        in_specs=[smem()] + [anywhere()] * 4,
        out_specs=(anywhere(),) * 6,
        scratch_shapes=[scratch(by + 2 * halo) for halo in (5, 4, 3, 2, 1, DIAGONAL_HALO)]
        + [dma((6,)), dma((6,))],
        compiler_params=params(),
        name="first_steps",
    )(ends, c0, diagonal, low1, high1)
    low2 = lax.ppermute(up_edge, "gy", up)
    high2 = lax.ppermute(down_edge, "gy", down)

    d2, moments = pl.pallas_call(
        functools.partial(middle_kernel, grid),
        out_shape=(rows_of(by), f32(6, 8, 128)),
        in_specs=[anywhere()] * 4,
        out_specs=(anywhere(), vmem()),
        scratch_shapes=[scratch(rows) for rows in (by, by, by + 2, by, by)] + [dma((4,)), dma((1,))],
        compiler_params=params(),
        cost_estimate=pl.CostEstimate(
            flops=40 * by * X * columns * 128, bytes_accessed=24 * by * X * columns * 128,
            transcendentals=0,
        ),
        name="middle_step",
    )(c0, c1, c2, diagonal)
    shares = [moments]
    for step in range(1, ny):
        shares.append(lax.ppermute(moments, "gy", [(i, (i + step) % ny) for i in range(ny)]))
    moments = jnp.concatenate(shares, axis=0)

    weights = lax.dynamic_slice_in_dim(cotangents, mine, 1, axis=1)[:, 0]
    inverse_count = 1.0 / (X * by * ny * columns * 128)
    out = pl.pallas_call(
        functools.partial(last_kernel, grid, inverse_count, ny),
        out_shape=f32(group * bx * by, bz),
        in_specs=[smem(), smem(), vmem()] + [anywhere()] * 11,
        out_specs=anywhere(),
        scratch_shapes=[
            scratch(by + rows) for rows in (0, 0, 0, 0, 2 * HALO, 8, 2 * DIAGONAL_HALO, 6, 4, 2)
        ]
        + [block_scratch(), dma((11,)), dma((per,))],
        compiler_params=params(),
        name="last_steps",
    )(ends, weights, moments, c0, d0, c1, d1, c2, d2, diagonal, low1, high1, low2, high2)

    out = lax.all_to_all(out.reshape(group, bx, by, bz), ("gx", "gz"), 0, 0, tiled=True)
    return jnp.sum(out[:count], axis=0)


def solution(mesh):
    return jax.shard_map(
        body,
        mesh=mesh,
        in_specs=(P(None, "gx", "gy", "gz"), P("gx", "gy", "gz"), P()),
        out_specs=P("gx", "gy", "gz"),
        check_vma=False,
    )
```

```python
import functools

import jax
import jax.numpy as jnp
from jax import lax
from jax.experimental import pallas as pl
from jax.experimental.pallas import tpu as pltpu
from jax.sharding import PartitionSpec as P

EPSILON = 1e-06
SHIFT = 64.0
HALO = 5
DIAGONAL_HALO = 4
PAD = 8
MIB = 1024 * 1024


def loss_of_moments(moments, weights):
    m0, m1, m2, m3, m4, m5 = moments
    norm = m0 + EPSILON
    alpha1 = (m1 + SHIFT * m0) / norm
    e1 = SHIFT - alpha1
    rest1 = jnp.maximum(m2 + 2.0 * e1 * m1 + e1 * e1 * m0, 0.0)
    beta1_square = rest1 / norm + EPSILON
    beta1 = jnp.sqrt(beta1_square)
    scale = 1.0 / (norm * beta1_square)
    alpha2 = scale * (m3 + 2.0 * e1 * m2 + e1 * e1 * m1 + SHIFT * rest1) - (m1 + e1 * m0) / norm
    e2 = SHIFT - alpha2
    f1 = e1 + e2
    f0 = e1 * e2 - beta1_square
    g = f1 * f1 + 2.0 * f0
    rest2 = jnp.maximum(m4 + 2.0 * f1 * m3 + g * m2 + 2.0 * f1 * f0 * m1 + f0 * f0 * m0, 0.0)
    beta2_square = scale * rest2 + EPSILON
    beta2 = jnp.sqrt(beta2_square)
    image2 = m5 + 2.0 * f1 * m4 + g * m3 + 2.0 * f1 * f0 * m2 + f0 * f0 * m1
    cross = m3 + f1 * m2 + f0 * m1 + e1 * (m2 + f1 * m1 + f0 * m0)
    alpha3 = scale * ((image2 + SHIFT * rest2) / beta2_square - cross)
    return (
        weights[0] * alpha1
        + weights[1] * alpha2
        + weights[2] * alpha3
        + weights[3] * beta1
        + weights[4] * beta2
    )


class Field:
    def __init__(self, ref, halo):
        self.ref = ref
        self.halo = halo
        self.columns, self.rows, self.pitch, _ = ref.shape
        self.cells = self.pitch - PAD
        self.flat = ref.reshape(self.columns * self.rows * self.pitch, 128)

    def at(self, column, row, x):
        moving, fixed = row
        start = (column * self.rows + fixed + self.halo) * self.pitch + x
        return pl.ds(moving * self.pitch + start, 8)

    def load(self, column, row, x):
        return self.flat[self.at(column, row, x), :]

    def store(self, column, row, x, value):
        self.flat[self.at(column, row, x), :] = value

    def part(self, first, count):
        return self.ref.at[:, pl.ds(first + self.halo, count), pl.ds(0, self.cells), :]

    def clear_pads(self):
        zero = jnp.zeros((8, 128), jnp.float32)

        def body(row, carry):
            for column in range(self.columns):
                self.store(column, (row, -self.halo), self.cells, zero)
            return carry

        lax.fori_loop(0, self.rows, body, 0)

    def clear_row(self, row):
        zero = jnp.zeros((8, 128), jnp.float32)
        for column in range(self.columns):
            for x in range(0, self.cells, 8):
                self.store(column, (0, row), x, zero)


def lane_masks():
    lane = lax.broadcasted_iota(jnp.int32, (8, 128), 1)
    return lane == 0, lane == 127


def stencil_tiles(source, diagonal, row, x, masks):
    columns = range(source.columns)
    moving, fixed = row
    centre = [source.load(c, row, x) for c in columns]
    after = [pltpu.roll(value, 1, 1) for value in centre]
    before = [pltpu.roll(value, 127, 1) for value in centre]
    results = []
    for c in columns:
        low = after[c - 1] if c else 0.0
        high = before[c + 1] if c + 1 < source.columns else 0.0
        total = jnp.where(masks[0], low, after[c]) + jnp.where(masks[1], high, before[c])
        total = total + (source.load(c, row, x - 1) + source.load(c, row, x + 1))
        total = total + (source.load(c, (moving, fixed - 1), x) + source.load(c, (moving, fixed + 1), x))
        results.append(diagonal.load(c, row, x) * centre[c] - total)
    return results


def apply_rows(target, source, diagonal, first, count, minus=None, unroll=2):
    masks = lane_masks()

    def body(step, carry):
        results = []
        for offset in range(unroll):
            row = (step * unroll, first + offset)
            for x in range(0, source.cells, 8):
                values = stencil_tiles(source, diagonal, row, x, masks)
                for c, value in enumerate(values):
                    if minus is not None:
                        value = value - SHIFT * minus.load(c, row, x)
                    results.append((c, row, x, value))
        for result in results:
            target.store(*result)
        return carry

    assert count % unroll == 0
    lax.fori_loop(0, count // unroll, body, 0)


def clear_outside(ends_ref, own, field):
    @pl.when(ends_ref[0] == 1)
    def _():
        field.clear_row(-1)

    @pl.when(ends_ref[1] == 1)
    def _():
        field.clear_row(own)


def apply_steps(ends_ref, own, target, source, diagonal, halo, minus=None):
    apply_rows(target, source, diagonal, -halo, own + 2 * halo, minus)
    if halo:
        clear_outside(ends_ref, own, target)


def column_copies(whole, columns, sem, inward):
    copies = []
    for index in range(columns.shape[0]):
        pair = (whole.at[:, pl.ds(index * 128, 128)], columns.at[index])
        source, target = pair if inward else pair[::-1]
        copies.append(pltpu.make_async_copy(source, target, sem.at[index]))
    return copies


def start_all(pairs, sem):
    copies = []
    for index, (source, target) in enumerate(pairs):
        copy = pltpu.make_async_copy(source, target, sem.at[index])
        copy.start()
        copies.append(copy)
    return copies


def places(grid):
    nx, nz, bx, by, bz = grid
    per = bz // 128
    for s in range(nx * nz):
        for column in range(per):
            yield (s // nz) * bx, (s % nz) * per + column, s, column


def assemble_kernel(
    grid, blocks_ref, own_ref, diagonal_ref, up_ref, down_ref, block_columns, block_sem,
):
    nx, nz, bx, by, bz = grid
    copies = column_copies(blocks_ref, block_columns, block_sem, True)
    for copy in copies:
        copy.start()
    for copy in copies:
        copy.wait()
    for x, z, s, column in places(grid):
        xs = pl.ds(x, bx)
        start = 2 * s * bx * by
        rows = [pl.ds(start + y, bx, stride=by) for y in range(by)]
        probe = [block_columns[column, at, :] for at in rows]
        rows = [pl.ds(start + bx * by + y, bx, stride=by) for y in range(by)]
        kappa = [6.0 + block_columns[column, at, :] for at in rows]
        for y in range(by):
            own_ref[z, y, xs, :] = probe[y]
            diagonal_ref[z, y, xs, :] = kappa[y]
        for y in range(HALO):
            down_ref[z, y, xs, :] = probe[y]
            up_ref[z, y, xs, :] = probe[by - HALO + y]
        for y in range(DIAGONAL_HALO):
            down_ref[z, HALO + y, xs, :] = kappa[y]
            up_ref[z, HALO + y, xs, :] = kappa[by - DIAGONAL_HALO + y]


def halo_pairs(field, own, low_ref, high_ref, start, halo):
    rows = pl.ds(start, halo)
    return [
        (low_ref.at[:, rows], field.part(-halo, halo)),
        (high_ref.at[:, rows], field.part(own, halo)),
    ]


def first_kernel(
    grid,
    ends_ref, own_in, diagonal_in, low_in, high_in,
    d0_out, c1_out, d1_out, c2_out, up_out, down_out,
    c0_ref, d0_ref, c1_ref, d1_ref, c2_ref, diagonal_ref, in_sem, out_sem,
):
    nx, nz, bx, by, bz = grid
    c0 = Field(c0_ref, 5)
    d0 = Field(d0_ref, 4)
    c1 = Field(c1_ref, 3)
    d1 = Field(d1_ref, 2)
    c2 = Field(c2_ref, 1)
    diagonal = Field(diagonal_ref, DIAGONAL_HALO)
    arrivals = start_all(
        [(own_in, c0.part(0, by)), (diagonal_in, diagonal.part(0, by))]
        + halo_pairs(c0, by, low_in, high_in, 0, HALO)
        + halo_pairs(diagonal, by, low_in, high_in, HALO, DIAGONAL_HALO),
        in_sem,
    )
    for field in (c0, d0, c1, d1, c2):
        field.clear_pads()
    departures = []

    def depart(source, out):
        copy = pltpu.make_async_copy(source, out, out_sem.at[len(departures)])
        copy.start()
        departures.append(copy)

    for copy in arrivals:
        copy.wait()
    steps = functools.partial(apply_steps, ends_ref, by)
    steps(d0, c0, diagonal, 4)
    depart(d0.part(0, by), d0_out)
    steps(c1, d0, diagonal, 3, c0)
    depart(c1.part(0, by), c1_out)
    steps(d1, c1, diagonal, 2)
    depart(d1.part(0, by), d1_out)
    steps(c2, d1, diagonal, 1, c1)
    depart(c2.part(by - HALO, HALO), up_out)
    depart(c2.part(0, HALO), down_out)
    depart(c2.part(-1, by + 2), c2_out)
    for copy in departures:
        copy.wait()


def middle_kernel(
    grid,
    c0_in, c1_in, c2_in, diagonal_in,
    d2_out, moments_ref,
    c0_ref, c1_ref, c2_ref, d2_ref, diagonal_ref, in_sem, out_sem,
):
    nx, nz, bx, by, bz = grid
    c0 = Field(c0_ref, 0)
    c1 = Field(c1_ref, 0)
    c2 = Field(c2_ref, 1)
    d2 = Field(d2_ref, 0)
    diagonal = Field(diagonal_ref, 0)
    copies = start_all(
        [
            (c2_in, c2.part(-1, by + 2)), (diagonal_in, diagonal.part(0, by)),
            (c0_in, c0.part(0, by)), (c1_in, c1.part(0, by)),
        ],
        in_sem,
    )
    c2.clear_pads()
    for copy in copies[:2]:
        copy.wait()
    apply_rows(d2, c2, diagonal, 0, by)
    out = pltpu.make_async_copy(d2.part(0, by), d2_out, out_sem.at[0])
    out.start()
    for copy in copies[2:]:
        copy.wait()

    def moment_row(step, sums):
        row = (step, 0)
        for x in range(0, c0.cells, 8):
            for c in range(c0.columns):
                a, b, e, d = (field.load(c, row, x) for field in (c0, c1, c2, d2))
                pairs = ((a, a), (a, b), (b, b), (b, e), (e, e), (d, d))
                sums = tuple(total + u * v for total, (u, v) in zip(sums, pairs))
        return sums

    zero = jnp.zeros((8, 128), jnp.float32)
    sums = lax.fori_loop(0, by, moment_row, (zero,) * 6)
    for index, total in enumerate(sums):
        moments_ref[index] = total
    out.wait()


def moment_slopes(inverse_count, parts, weights_ref, moments_ref):
    raw = []
    for k in range(6):
        total = moments_ref[k]
        for part in range(1, parts):
            total = total + moments_ref[part * 6 + k]
        total = jnp.sum(jnp.sum(total, axis=0, keepdims=True), axis=1, keepdims=True)
        raw.append(jnp.broadcast_to(total * inverse_count, (8, 128)))
    moments = tuple(raw[:5]) + (raw[5] - SHIFT * raw[4],)
    weights = [weights_ref[k] for k in range(5)]
    value, pullback = jax.vjp(lambda m: loss_of_moments(m, weights), moments)
    (slopes,) = pullback(jnp.full((8, 128), 2.0, jnp.float32))
    return [slope[0, 0] for slope in slopes]


def last_kernel(
    grid, inverse_count, parts,
    ends_ref, weights_ref, moments_ref,
    c0_in, d0_in, c1_in, d1_in, c2_in, d2_in, diagonal_in, low1_in, high1_in, low2_in, high2_in,
    out_ref,
    c0_ref, d0_ref, c1_ref, d1_ref, c2_ref, d2_ref, diagonal_ref, c3_ref, d3_ref, c4_ref,
    columns_ref, in_sem, out_sem,
):
    nx, nz, bx, by, bz = grid
    c0, d0, c1, d1 = (Field(ref, 0) for ref in (c0_ref, d0_ref, c1_ref, d1_ref))
    c2 = Field(c2_ref, HALO)
    d2 = Field(d2_ref, 4)
    c3 = Field(c3_ref, 3)
    d3 = Field(d3_ref, 2)
    c4 = Field(c4_ref, 1)
    diagonal = Field(diagonal_ref, DIAGONAL_HALO)
    copies = start_all(
        [(diagonal_in, diagonal.part(0, by)), (c2_in.at[:, pl.ds(1, by)], c2.part(0, by))]
        + halo_pairs(diagonal, by, low1_in, high1_in, HALO, DIAGONAL_HALO)
        + halo_pairs(c2, by, low2_in, high2_in, 0, HALO)
        + [
            (d2_in, d2.part(0, by)), (c0_in, c0.part(0, by)), (d0_in, d0.part(0, by)),
            (c1_in, c1.part(0, by)), (d1_in, d1.part(0, by)),
        ],
        in_sem,
    )
    for field in (c2, d2, c3, d3, c4):
        field.clear_pads()
    slopes = moment_slopes(inverse_count, parts, weights_ref, moments_ref)
    for copy in copies[:6]:
        copy.wait()
    apply_rows(d2, c2, diagonal, -4, 4)
    apply_rows(d2, c2, diagonal, by, 4)
    clear_outside(ends_ref, by, d2)
    copies[6].wait()
    steps = functools.partial(apply_steps, ends_ref, by)
    steps(c3, d2, diagonal, 3, c2)
    steps(d3, c3, diagonal, 2)
    steps(c4, d3, diagonal, 1, c3)
    for copy in copies[7:]:
        copy.wait()
    masks = lane_masks()
    place = {(x, z): (s, column) for x, z, s, column in places(grid)}

    def out_row(step, carry):
        row = (step, 0)
        results = []
        for x in range(0, c4.cells, 8):
            last = stencil_tiles(c4, diagonal, row, x, masks)
            for z in range(c4.columns):
                cs = [field.load(z, row, x) for field in (c0, c1, c2, c3, c4)]
                ds = [field.load(z, row, x) for field in (d0, d1, d2, d3)] + [last[z]]
                total = None
                for i in range(5):
                    inner = None
                    for j in range(5 - i):
                        term = slopes[i + j + 1] * ds[j]
                        inner = term if inner is None else inner + term
                    term = cs[i] * inner
                    total = term if total is None else total + term
                s, column = place[x, z]
                results.append((column, s, total))
        for column, s, total in results:
            columns_ref[column, pl.ds(s * bx * by + step, bx, stride=by), :] = total
        return carry

    lax.fori_loop(0, by, out_row, 0)
    copies = column_copies(out_ref, columns_ref, out_sem, False)
    for copy in copies:
        copy.start()
    for copy in copies:
        copy.wait()


def vmem():
    return pl.BlockSpec(memory_space=pltpu.VMEM)


def smem():
    return pl.BlockSpec(memory_space=pltpu.SMEM)


def anywhere():
    return pl.BlockSpec(memory_space=pl.ANY)


def f32(*shape):
    return jax.ShapeDtypeStruct(shape, jnp.float32)


def params():
    return pltpu.CompilerParams(vmem_limit_bytes=60 * MIB)


def body(probes, kappa2, cotangents):
    nx, ny, nz = (lax.axis_size(axis) for axis in ("gx", "gy", "gz"))
    count, bx, by, bz = probes.shape
    group = nx * nz
    assert group % count == 0 and bx == 8 and by % 2 == 0 and by >= HALO and bz % 128 == 0
    copies = group // count
    X = nx * bx
    columns = nz * bz // 128
    per = bz // 128
    grid = (nx, nz, bx, by, bz)
    gy = lax.axis_index("gy")
    mine = (lax.axis_index("gx") * nz + lax.axis_index("gz")) % count
    up = [(i, i + 1) for i in range(ny - 1)]
    down = [(target, source) for source, target in up]

    def rows_of(rows):
        return f32(columns, rows, X, 128)

    def scratch(rows):
        return pltpu.VMEM((columns, rows, X + PAD, 128), jnp.float32)

    def block_scratch():
        return pltpu.VMEM((per, group * bx * by, 128), jnp.float32)

    dma = pltpu.SemaphoreType.DMA

    blocks = jnp.concatenate([probes] * copies, axis=0) if copies > 1 else probes
    kappa = jnp.broadcast_to(kappa2[None], blocks.shape)
    blocks = jnp.concatenate([blocks, kappa], axis=1)
    blocks = lax.all_to_all(blocks, ("gx", "gz"), 0, 0, tiled=True)
    c0, diagonal, up_edge, down_edge = pl.pallas_call(
        functools.partial(assemble_kernel, grid),
        out_shape=(
            rows_of(by), rows_of(by), rows_of(HALO + DIAGONAL_HALO), rows_of(HALO + DIAGONAL_HALO)
        ),
        in_specs=[anywhere()],
        out_specs=(vmem(),) * 4,
        scratch_shapes=[pltpu.VMEM((per, 2 * group * bx * by, 128), jnp.float32), dma((per,))],
        compiler_params=params(),
        name="assemble",
    )(blocks.reshape(2 * group * bx * by, bz))
    low1 = lax.ppermute(up_edge, "gy", up)
    high1 = lax.ppermute(down_edge, "gy", down)

    ends = jnp.stack([gy == 0, gy == ny - 1]).astype(jnp.int32)
    d0, c1, d1, c2, up_edge, down_edge = pl.pallas_call(
        functools.partial(first_kernel, grid),
        out_shape=(rows_of(by),) * 3 + (rows_of(by + 2), rows_of(HALO), rows_of(HALO)),
        in_specs=[smem()] + [anywhere()] * 4,
        out_specs=(anywhere(),) * 6,
        scratch_shapes=[scratch(by + 2 * halo) for halo in (5, 4, 3, 2, 1, DIAGONAL_HALO)]
        + [dma((6,)), dma((6,))],
        compiler_params=params(),
        name="first_steps",
    )(ends, c0, diagonal, low1, high1)
    low2 = lax.ppermute(up_edge, "gy", up)
    high2 = lax.ppermute(down_edge, "gy", down)

    d2, moments = pl.pallas_call(
        functools.partial(middle_kernel, grid),
        out_shape=(rows_of(by), f32(6, 8, 128)),
        in_specs=[anywhere()] * 4,
        out_specs=(anywhere(), vmem()),
        scratch_shapes=[scratch(rows) for rows in (by, by, by + 2, by, by)] + [dma((4,)), dma((1,))],
        compiler_params=params(),
        cost_estimate=pl.CostEstimate(
            flops=40 * by * X * columns * 128, bytes_accessed=24 * by * X * columns * 128,
            transcendentals=0,
        ),
        name="middle_step",
    )(c0, c1, c2, diagonal)
    shares = [moments]
    for step in range(1, ny):
        shares.append(lax.ppermute(moments, "gy", [(i, (i + step) % ny) for i in range(ny)]))
    moments = jnp.concatenate(shares, axis=0)

    weights = lax.dynamic_slice_in_dim(cotangents, mine, 1, axis=1)[:, 0]
    inverse_count = 1.0 / (X * by * ny * columns * 128)
    out = pl.pallas_call(
        functools.partial(last_kernel, grid, inverse_count, ny),
        out_shape=f32(group * bx * by, bz),
        in_specs=[smem(), smem(), vmem()] + [anywhere()] * 11,
        out_specs=anywhere(),
        scratch_shapes=[
            scratch(by + rows) for rows in (0, 0, 0, 0, 2 * HALO, 8, 2 * DIAGONAL_HALO, 6, 4, 2)
        ]
        + [block_scratch(), dma((11,)), dma((per,))],
        compiler_params=params(),
        name="last_steps",
    )(ends, weights, moments, c0, d0, c1, d1, c2, d2, diagonal, low1, high1, low2, high2)

    out = lax.all_to_all(out.reshape(group, bx, by, bz), ("gx", "gz"), 0, 0, tiled=True)
    return jnp.sum(out[:count], axis=0)


def solution(mesh):
    return jax.shard_map(
        body,
        mesh=mesh,
        in_specs=(P(None, "gx", "gy", "gz"), P("gx", "gy", "gz"), P()),
        out_specs=P("gx", "gy", "gz"),
        check_vma=False,
    )
```

```python
import functools

import jax
import jax.numpy as jnp
from jax import lax
from jax.experimental import pallas as pl
from jax.experimental.pallas import tpu as pltpu
from jax.sharding import PartitionSpec as P

EPSILON = 1e-06
SHIFT = 64.0
HALO = 5
DIAGONAL_HALO = 4
PAD = 8
MIB = 1024 * 1024


def loss_of_moments(moments, weights):
    m0, m1, m2, m3, m4, m5 = moments
    norm = m0 + EPSILON
    alpha1 = (m1 + SHIFT * m0) / norm
    e1 = SHIFT - alpha1
    rest1 = jnp.maximum(m2 + 2.0 * e1 * m1 + e1 * e1 * m0, 0.0)
    beta1_square = rest1 / norm + EPSILON
    beta1 = jnp.sqrt(beta1_square)
    scale = 1.0 / (norm * beta1_square)
    alpha2 = scale * (m3 + 2.0 * e1 * m2 + e1 * e1 * m1 + SHIFT * rest1) - (m1 + e1 * m0) / norm
    e2 = SHIFT - alpha2
    f1 = e1 + e2
    f0 = e1 * e2 - beta1_square
    g = f1 * f1 + 2.0 * f0
    rest2 = jnp.maximum(m4 + 2.0 * f1 * m3 + g * m2 + 2.0 * f1 * f0 * m1 + f0 * f0 * m0, 0.0)
    beta2_square = scale * rest2 + EPSILON
    beta2 = jnp.sqrt(beta2_square)
    image2 = m5 + 2.0 * f1 * m4 + g * m3 + 2.0 * f1 * f0 * m2 + f0 * f0 * m1
    cross = m3 + f1 * m2 + f0 * m1 + e1 * (m2 + f1 * m1 + f0 * m0)
    alpha3 = scale * ((image2 + SHIFT * rest2) / beta2_square - cross)
    return (
        weights[0] * alpha1
        + weights[1] * alpha2
        + weights[2] * alpha3
        + weights[3] * beta1
        + weights[4] * beta2
    )


class Field:
    def __init__(self, ref, halo):
        self.ref = ref
        self.halo = halo
        self.columns, self.rows, self.pitch, _ = ref.shape
        self.cells = self.pitch - PAD
        self.flat = ref.reshape(self.columns * self.rows * self.pitch, 128)

    def at(self, column, row, x):
        moving, fixed = row
        start = (column * self.rows + fixed + self.halo) * self.pitch + x
        return pl.ds(moving * self.pitch + start, 8)

    def load(self, column, row, x):
        return self.flat[self.at(column, row, x), :]

    def store(self, column, row, x, value):
        self.flat[self.at(column, row, x), :] = value

    def part(self, first, count):
        return self.ref.at[:, pl.ds(first + self.halo, count), pl.ds(0, self.cells), :]

    def clear_pads(self):
        zero = jnp.zeros((8, 128), jnp.float32)

        def body(row, carry):
            for column in range(self.columns):
                self.store(column, (row, -self.halo), self.cells, zero)
            return carry

        lax.fori_loop(0, self.rows, body, 0)

    def clear_row(self, row):
        zero = jnp.zeros((8, 128), jnp.float32)
        for column in range(self.columns):
            for x in range(0, self.cells, 8):
                self.store(column, (0, row), x, zero)


def lane_masks():
    lane = lax.broadcasted_iota(jnp.int32, (8, 128), 1)
    return lane == 0, lane == 127


def stencil_tiles(source, diagonal, row, x, masks):
    columns = range(source.columns)
    moving, fixed = row
    centre = [source.load(c, row, x) for c in columns]
    after = [pltpu.roll(value, 1, 1) for value in centre]
    before = [pltpu.roll(value, 127, 1) for value in centre]
    results = []
    for c in columns:
        low = after[c - 1] if c else 0.0
        high = before[c + 1] if c + 1 < source.columns else 0.0
        total = jnp.where(masks[0], low, after[c]) + jnp.where(masks[1], high, before[c])
        total = total + (source.load(c, row, x - 1) + source.load(c, row, x + 1))
        total = total + (source.load(c, (moving, fixed - 1), x) + source.load(c, (moving, fixed + 1), x))
        results.append(diagonal.load(c, row, x) * centre[c] - total)
    return results


def apply_rows(target, source, diagonal, first, count, minus=None, unroll=2):
    masks = lane_masks()

    def body(step, carry):
        results = []
        for offset in range(unroll):
            row = (step * unroll, first + offset)
            for x in range(0, source.cells, 8):
                values = stencil_tiles(source, diagonal, row, x, masks)
                for c, value in enumerate(values):
                    if minus is not None:
                        value = value - SHIFT * minus.load(c, row, x)
                    results.append((c, row, x, value))
        for result in results:
            target.store(*result)
        return carry

    assert count % unroll == 0
    lax.fori_loop(0, count // unroll, body, 0)


def clear_outside(ends_ref, own, field):
    @pl.when(ends_ref[0] == 1)
    def _():
        field.clear_row(-1)

    @pl.when(ends_ref[1] == 1)
    def _():
        field.clear_row(own)


def apply_steps(ends_ref, own, target, source, diagonal, halo, minus=None):
    apply_rows(target, source, diagonal, -halo, own + 2 * halo, minus)
    if halo:
        clear_outside(ends_ref, own, target)


def places(grid):
    nx, nz, bx, by, bz = grid
    per = bz // 128
    for s in range(nx * nz):
        for column in range(per):
            yield s, column, (s // nz) * bx, (s % nz) * per + column


def pack_kernel(grid, count, probes_ref, kappa_ref, out_ref, sem):
    nx, nz, bx, by, bz = grid
    per = bz // 128
    rows = bx * by
    copies = []
    for s in range(nx * nz):
        parts = [
            probes_ref.at[pl.ds((s % count) * rows, rows), pl.ds(column * 128, 128)]
            for column in range(per)
        ]
        parts.append(kappa_ref.at[:, pl.ds((s // nz) % 2 * 128, 128)])
        for index, part in enumerate(parts):
            copies.append(pltpu.make_async_copy(part, out_ref.at[s, index], sem.at[s, index]))
    for copy in copies:
        copy.start()
    for copy in copies:
        copy.wait()


def probe_kernel(grid, blocks_ref, own_ref, up_ref, down_ref, half_ref):
    nx, nz, bx, by, bz = grid
    per = bz // 128
    own = Field(own_ref, HALO)
    own.clear_pads()
    for s, column, x, z in places(grid):
        values = [blocks_ref[s, column, pl.ds(y, bx, stride=by), :] for y in range(by)]
        for y in range(by):
            own.store(z, (0, y), x, values[y])
        for y in range(HALO):
            down_ref[z, y, pl.ds(x, bx), :] = values[y]
            up_ref[z, y, pl.ds(x, bx), :] = values[by - HALO + y]
    for s in range(nx * nz):
        half_ref[s] = blocks_ref[s, per]


def diagonal_kernel(grid, core_ref, half_ref, other_ref, own_ref, up_ref, down_ref):
    nx, nz, bx, by, bz = grid
    own = Field(own_ref, DIAGONAL_HALO)
    first = core_ref[0] == 0
    for s, column, x, z in places(grid):
        values = []
        for y in range(by):
            rows = pl.ds(y, bx, stride=by)
            mine, other = half_ref[s, rows, :], other_ref[s, rows, :]
            pair = (mine, other) if column == 0 else (other, mine)
            values.append(6.0 + jnp.where(first, *pair))
        for y in range(by):
            own.store(z, (0, y), x, values[y])
        for y in range(DIAGONAL_HALO):
            down_ref[z, y, pl.ds(x, bx), :] = values[y]
            up_ref[z, y, pl.ds(x, bx), :] = values[by - DIAGONAL_HALO + y]


def fill_halo(field, own, low_ref, high_ref):
    for c in range(field.columns):
        for y in range(field.halo):
            for x in range(0, field.cells, 8):
                field.store(c, (0, y - field.halo), x, low_ref[c, y, pl.ds(x, 8), :])
                field.store(c, (0, own + y), x, high_ref[c, y, pl.ds(x, 8), :])


def first_kernel(
    own,
    ends_ref, c0_in, diagonal_in, low_ref, high_ref, low_diagonal_ref, high_diagonal_ref,
    c0_ref, diagonal_ref, d0_ref, c1_ref, d1_ref, c2_ref, d2_ref, up_ref, down_ref, moments_ref,
):
    c0 = Field(c0_ref, HALO)
    diagonal = Field(diagonal_ref, DIAGONAL_HALO)
    d0 = Field(d0_ref, 4)
    c1 = Field(c1_ref, 3)
    d1 = Field(d1_ref, 2)
    c2 = Field(c2_ref, HALO)
    d2 = Field(d2_ref, 4)
    for field in (d0, c1, d1, c2, d2):
        field.clear_pads()
    fill_halo(c0, own, low_ref, high_ref)
    fill_halo(diagonal, own, low_diagonal_ref, high_diagonal_ref)
    steps = functools.partial(apply_steps, ends_ref, own)
    steps(d0, c0, diagonal, 4)
    steps(c1, d0, diagonal, 3, c0)
    steps(d1, c1, diagonal, 2)
    steps(c2, d1, diagonal, 1, c1)
    for c in range(c2.columns):
        for y in range(HALO):
            for x in range(0, c2.cells, 8):
                down_ref[c, y, pl.ds(x, 8), :] = c2.load(c, (0, y), x)
                up_ref[c, y, pl.ds(x, 8), :] = c2.load(c, (0, own - HALO + y), x)
    steps(d2, c2, diagonal, 0)

    def moment_row(step, sums):
        row = (step, 0)
        for x in range(0, c0.cells, 8):
            for c in range(c0.columns):
                a, b, e, d = (field.load(c, row, x) for field in (c0, c1, c2, d2))
                pairs = ((a, a), (a, b), (b, b), (b, e), (e, e), (d, d))
                sums = tuple(total + u * v for total, (u, v) in zip(sums, pairs))
        return sums

    zero = jnp.zeros((8, 128), jnp.float32)
    sums = lax.fori_loop(0, own, moment_row, (zero,) * 6)
    for index, total in enumerate(sums):
        for part in range(moments_ref.shape[0]):
            moments_ref[part, index] = total


def moment_slopes(inverse_count, probe, weights_ref, moments_ref):
    raw = []
    for k in range(6):
        total = moments_ref[0, k]
        for part in range(1, moments_ref.shape[0]):
            total = total + moments_ref[part, k]
        total = jnp.sum(jnp.sum(total, axis=0, keepdims=True), axis=1, keepdims=True)
        raw.append(jnp.broadcast_to(total * inverse_count, (8, 128)))
    moments = tuple(raw[:5]) + (raw[5] - SHIFT * raw[4],)
    weights = [weights_ref[k, probe] for k in range(5)]
    value, pullback = jax.vjp(lambda m: loss_of_moments(m, weights), moments)
    (slopes,) = pullback(jnp.full((8, 128), 2.0, jnp.float32))
    return [slope[0, 0] for slope in slopes]


def last_kernel(
    grid, inverse_count,
    ends_ref, weights_ref, moments_ref, c0_ref, diagonal_ref, d0_ref, c1_ref, d1_ref,
    c2_in, d2_in, low_ref, high_ref,
    c2_ref, d2_ref, out_ref, c3_ref, d3_ref, c4_ref,
):
    nx, nz, bx, by, bz = grid
    c0 = Field(c0_ref, HALO)
    diagonal = Field(diagonal_ref, DIAGONAL_HALO)
    d0 = Field(d0_ref, 4)
    c1 = Field(c1_ref, 3)
    d1 = Field(d1_ref, 2)
    c2 = Field(c2_ref, HALO)
    d2 = Field(d2_ref, 4)
    c3 = Field(c3_ref, 3)
    d3 = Field(d3_ref, 2)
    c4 = Field(c4_ref, 1)
    for field in (c3, d3, c4):
        field.clear_pads()
    slopes = moment_slopes(inverse_count, ends_ref[2], weights_ref, moments_ref)
    fill_halo(c2, by, low_ref, high_ref)
    apply_rows(d2, c2, diagonal, -4, 4)
    apply_rows(d2, c2, diagonal, by, 4)
    clear_outside(ends_ref, by, d2)
    steps = functools.partial(apply_steps, ends_ref, by)
    steps(c3, d2, diagonal, 3, c2)
    steps(d3, c3, diagonal, 2)
    steps(c4, d3, diagonal, 1, c3)
    masks = lane_masks()
    place = {(x, z): (s, column) for s, column, x, z in places(grid)}

    def out_row(step, carry):
        row = (step, 0)
        results = []
        for x in range(0, c4.cells, 8):
            last = stencil_tiles(c4, diagonal, row, x, masks)
            for z in range(c4.columns):
                cs = [field.load(z, row, x) for field in (c0, c1, c2, c3, c4)]
                ds = [field.load(z, row, x) for field in (d0, d1, d2, d3)] + [last[z]]
                total = None
                for i in range(5):
                    inner = None
                    for j in range(5 - i):
                        term = slopes[i + j + 1] * ds[j]
                        inner = term if inner is None else inner + term
                    term = cs[i] * inner
                    total = term if total is None else total + term
                results.append(place[x, z] + (total,))
        for s, column, total in results:
            out_ref[s, column, pl.ds(step, bx, stride=by), :] = total
        return carry

    lax.fori_loop(0, by, out_row, 0)


def sum_kernel(grid, count, parts_ref, out_ref):
    nx, nz, bx, by, bz = grid
    for column in range(bz // 128):
        for x in range(bx):
            total = None
            for p in range(count):
                part = parts_ref[p, column, pl.ds(x * by, by), :]
                total = part if total is None else total + part
            out_ref[x, :, pl.ds(column * 128, 128)] = total


def vmem():
    return pl.BlockSpec(memory_space=pltpu.VMEM)


def smem():
    return pl.BlockSpec(memory_space=pltpu.SMEM)


def anywhere():
    return pl.BlockSpec(memory_space=pl.ANY)


def f32(*shape):
    return jax.ShapeDtypeStruct(shape, jnp.float32)


def params():
    return pltpu.CompilerParams(vmem_limit_bytes=32 * MIB)


def body(probes, kappa2, cotangents):
    nx, ny, nz = (lax.axis_size(axis) for axis in ("gx", "gy", "gz"))
    count, bx, by, bz = probes.shape
    group = nx * nz
    assert group % count == 0 and nx % 2 == 0 and bx == 8 and bz == 256
    assert by % 8 == 0 and by >= HALO
    X = nx * bx
    columns = nz * bz // 128
    per = bz // 128
    rows = bx * by
    grid = (nx, nz, bx, by, bz)
    gx, gy = lax.axis_index("gx"), lax.axis_index("gy")
    mine = (gx * nz + lax.axis_index("gz")) % count
    up = [(i, i + 1) for i in range(ny - 1)]
    down = [(target, source) for source, target in up]
    sibling = [(i, i ^ 1) for i in range(nx)]

    def edge(halo):
        return f32(columns, halo, X, 128)

    def padded(halo):
        return (columns, by + 2 * halo, X + PAD, 128)

    blocks = pl.pallas_call(
        functools.partial(pack_kernel, grid, count),
        out_shape=f32(group, per + 1, rows, 128),
        in_specs=[anywhere(), anywhere()],
        out_specs=vmem(),
        scratch_shapes=[pltpu.SemaphoreType.DMA((group, per + 1))],
        compiler_params=params(),
        name="pack",
    )(probes.reshape(count * rows, bz), kappa2.reshape(rows, bz))
    blocks = lax.all_to_all(blocks, ("gx", "gz"), 0, 0, tiled=True)
    c0, up_edge, down_edge, half = pl.pallas_call(
        functools.partial(probe_kernel, grid),
        out_shape=(f32(*padded(HALO)), edge(HALO), edge(HALO), f32(group, rows, 128)),
        in_specs=[vmem()],
        out_specs=(vmem(),) * 4,
        compiler_params=params(),
        name="probe_rows",
    )(blocks)
    low1 = lax.ppermute(up_edge, "gy", up)
    high1 = lax.ppermute(down_edge, "gy", down)
    other = lax.ppermute(half, "gx", sibling)
    diagonal, up_edge, down_edge = pl.pallas_call(
        functools.partial(diagonal_kernel, grid),
        out_shape=(f32(*padded(DIAGONAL_HALO)), edge(DIAGONAL_HALO), edge(DIAGONAL_HALO)),
        in_specs=[smem(), vmem(), vmem()],
        out_specs=(vmem(),) * 3,
        compiler_params=params(),
        name="diagonal_rows",
    )((gx % 2).astype(jnp.int32).reshape(1), half, other)
    low_diagonal = lax.ppermute(up_edge, "gy", up)
    high_diagonal = lax.ppermute(down_edge, "gy", down)

    ends = jnp.stack([gy == 0, gy == ny - 1, mine]).astype(jnp.int32)
    c0, diagonal, d0, c1, d1, c2, d2, up_edge, down_edge, moments = pl.pallas_call(
        functools.partial(first_kernel, by),
        out_shape=tuple(f32(*padded(h)) for h in (HALO, DIAGONAL_HALO, 4, 3, 2, HALO, 4))
        + (edge(HALO), edge(HALO), f32(ny, 6, 8, 128)),
        in_specs=[smem()] + [vmem()] * 6,
        out_specs=(vmem(),) * 10,
        input_output_aliases={1: 0, 2: 1},
        compiler_params=params(),
        name="first_steps",
    )(ends, c0, diagonal, low1, high1, low_diagonal, high_diagonal)
    low2 = lax.ppermute(up_edge, "gy", up)
    high2 = lax.ppermute(down_edge, "gy", down)
    moments = lax.all_to_all(moments, "gy", 0, 0, tiled=True)

    inverse_count = 1.0 / (X * by * ny * columns * 128)
    _, _, out = pl.pallas_call(
        functools.partial(last_kernel, grid, inverse_count),
        out_shape=(f32(*padded(HALO)), f32(*padded(4)), f32(group, per, rows, 128)),
        in_specs=[smem(), smem()] + [vmem()] * 10,
        out_specs=(vmem(),) * 3,
        scratch_shapes=[pltpu.VMEM(padded(h), jnp.float32) for h in (3, 2, 1)],
        input_output_aliases={8: 0, 9: 1},
        compiler_params=params(),
        name="last_steps",
    )(ends, cotangents, moments, c0, diagonal, d0, c1, d1, c2, d2, low2, high2)

    out = lax.all_to_all(out, ("gx", "gz"), 0, 0, tiled=True)
    return pl.pallas_call(
        functools.partial(sum_kernel, grid, count),
        out_shape=f32(bx, by, bz),
        in_specs=[vmem()],
        out_specs=vmem(),
        compiler_params=params(),
        name="sum_probes",
    )(out)


def solution(mesh):
    return jax.shard_map(
        body,
        mesh=mesh,
        in_specs=(P(None, "gx", "gy", "gz"), P("gx", "gy", "gz"), P()),
        out_specs=P("gx", "gy", "gz"),
        check_vma=False,
    )
```

```python
import functools

import jax
import jax.numpy as jnp
from jax import lax
from jax.experimental import pallas as pl
from jax.experimental.pallas import tpu as pltpu
from jax.sharding import PartitionSpec as P

EPSILON = 1e-06
SHIFT = 64.0
HALO = 5
DIAGONAL_HALO = 4
PAD = 8
MIB = 1024 * 1024


def loss_of_moments(moments, weights):
    m0, m1, m2, m3, m4, m5 = moments
    norm = m0 + EPSILON
    alpha1 = (m1 + SHIFT * m0) / norm
    e1 = SHIFT - alpha1
    rest1 = jnp.maximum(m2 + 2.0 * e1 * m1 + e1 * e1 * m0, 0.0)
    beta1_square = rest1 / norm + EPSILON
    beta1 = jnp.sqrt(beta1_square)
    scale = 1.0 / (norm * beta1_square)
    alpha2 = scale * (m3 + 2.0 * e1 * m2 + e1 * e1 * m1 + SHIFT * rest1) - (m1 + e1 * m0) / norm
    e2 = SHIFT - alpha2
    f1 = e1 + e2
    f0 = e1 * e2 - beta1_square
    g = f1 * f1 + 2.0 * f0
    rest2 = jnp.maximum(m4 + 2.0 * f1 * m3 + g * m2 + 2.0 * f1 * f0 * m1 + f0 * f0 * m0, 0.0)
    beta2_square = scale * rest2 + EPSILON
    beta2 = jnp.sqrt(beta2_square)
    image2 = m5 + 2.0 * f1 * m4 + g * m3 + 2.0 * f1 * f0 * m2 + f0 * f0 * m1
    cross = m3 + f1 * m2 + f0 * m1 + e1 * (m2 + f1 * m1 + f0 * m0)
    alpha3 = scale * ((image2 + SHIFT * rest2) / beta2_square - cross)
    return (
        weights[0] * alpha1
        + weights[1] * alpha2
        + weights[2] * alpha3
        + weights[3] * beta1
        + weights[4] * beta2
    )


class Field:
    def __init__(self, ref, halo):
        self.ref = ref
        self.halo = halo
        self.columns, self.rows, self.pitch, _ = ref.shape
        self.cells = self.pitch - 2 * PAD

    def load(self, column, row, x):
        return self.ref[column, row + self.halo, pl.ds(PAD + x, 8), :]

    def store(self, column, row, x, value):
        self.ref[column, row + self.halo, pl.ds(PAD + x, 8), :] = value

    def clear_pads(self):
        zero = jnp.zeros((8, 128), jnp.float32)

        def body(at, carry):
            for column in range(self.columns):
                self.ref[column, at, pl.ds(0, PAD), :] = zero
                self.ref[column, at, pl.ds(PAD + self.cells, PAD), :] = zero
            return carry

        lax.fori_loop(0, self.rows, body, 0)

    def clear_row(self, row):
        zero = jnp.zeros((8, 128), jnp.float32)
        for column in range(self.columns):
            for x in range(0, self.cells, 8):
                self.store(column, row, x, zero)


def lane_masks():
    lane = lax.broadcasted_iota(jnp.int32, (8, 128), 1)
    return lane == 0, lane == 127


def stencil_tiles(source, diagonal, row, x, masks):
    columns = range(source.columns)
    centre = [source.load(c, row, x) for c in columns]
    after = [pltpu.roll(value, 1, 1) for value in centre]
    before = [pltpu.roll(value, 127, 1) for value in centre]
    results = []
    for c in columns:
        low = after[c - 1] if c else 0.0
        high = before[c + 1] if c + 1 < source.columns else 0.0
        total = jnp.where(masks[0], low, after[c]) + jnp.where(masks[1], high, before[c])
        total = total + (source.load(c, row, x - 1) + source.load(c, row, x + 1))
        total = total + (source.load(c, row - 1, x) + source.load(c, row + 1, x))
        results.append(diagonal.load(c, row, x) * centre[c] - total)
    return results


def apply_rows(target, source, diagonal, first, count, minus=None, unroll=2):
    masks = lane_masks()

    def body(step, carry):
        results = []
        for offset in range(unroll):
            row = step * unroll + (first + offset)
            for x in range(0, source.cells, 8):
                values = stencil_tiles(source, diagonal, row, x, masks)
                for c, value in enumerate(values):
                    if minus is not None:
                        value = value - SHIFT * minus.load(c, row, x)
                    results.append((c, row, x, value))
        for result in results:
            target.store(*result)
        return carry

    assert count % unroll == 0
    lax.fori_loop(0, count // unroll, body, 0)


def clear_outside(ends_ref, own, field):
    @pl.when(ends_ref[0] == 1)
    def _():
        field.clear_row(-1)

    @pl.when(ends_ref[1] == 1)
    def _():
        field.clear_row(own)


def apply_steps(ends_ref, own, target, source, diagonal, halo, minus=None):
    apply_rows(target, source, diagonal, -halo, own + 2 * halo, minus)
    if halo:
        clear_outside(ends_ref, own, target)


def places(grid):
    nx, nz, bx, by, bz = grid
    per = bz // 128
    for s in range(nx * nz):
        for column in range(per):
            yield s, column, (s // nz) * bx, (s % nz) * per + column


def pack_kernel(grid, count, probes_ref, kappa_ref, out_ref, sem):
    nx, nz, bx, by, bz = grid
    per = bz // 128
    rows = bx * by
    copies = []
    for s in range(nx * nz):
        parts = [
            probes_ref.at[pl.ds((s % count) * rows, rows), pl.ds(column * 128, 128)]
            for column in range(per)
        ]
        parts.append(kappa_ref.at[:, pl.ds((s // nz) % 2 * 128, 128)])
        for index, part in enumerate(parts):
            copies.append(pltpu.make_async_copy(part, out_ref.at[s, index], sem.at[s, index]))
    for copy in copies:
        copy.start()
    for copy in copies:
        copy.wait()


def probe_kernel(grid, blocks_ref, own_ref, up_ref, down_ref, half_ref):
    nx, nz, bx, by, bz = grid
    per = bz // 128
    own = Field(own_ref, HALO)
    own.clear_pads()
    for s, column, x, z in places(grid):
        values = [blocks_ref[s, column, pl.ds(y, bx, stride=by), :] for y in range(by)]
        for y in range(by):
            own.store(z, y, x, values[y])
        for y in range(HALO):
            down_ref[z, y, pl.ds(x, bx), :] = values[y]
            up_ref[z, y, pl.ds(x, bx), :] = values[by - HALO + y]
    for s in range(nx * nz):
        half_ref[s] = blocks_ref[s, per]


def diagonal_kernel(grid, core_ref, half_ref, other_ref, own_ref, up_ref, down_ref):
    nx, nz, bx, by, bz = grid
    own = Field(own_ref, DIAGONAL_HALO)
    first = core_ref[0] == 0
    for s, column, x, z in places(grid):
        values = []
        for y in range(by):
            rows = pl.ds(y, bx, stride=by)
            mine, other = half_ref[s, rows, :], other_ref[s, rows, :]
            pair = (mine, other) if column == 0 else (other, mine)
            values.append(6.0 + jnp.where(first, *pair))
        for y in range(by):
            own.store(z, y, x, values[y])
        for y in range(DIAGONAL_HALO):
            down_ref[z, y, pl.ds(x, bx), :] = values[y]
            up_ref[z, y, pl.ds(x, bx), :] = values[by - DIAGONAL_HALO + y]


def fill_halo(field, own, low_ref, high_ref):
    for c in range(field.columns):
        for y in range(field.halo):
            for x in range(0, field.cells, 8):
                field.store(c, y - field.halo, x, low_ref[c, y, pl.ds(x, 8), :])
                field.store(c, own + y, x, high_ref[c, y, pl.ds(x, 8), :])


def first_kernel(
    own,
    ends_ref, c0_in, diagonal_in, low_ref, high_ref, low_diagonal_ref, high_diagonal_ref,
    c0_ref, diagonal_ref, d0_ref, c1_ref, d1_ref, c2_ref, up_ref, down_ref,
):
    c0 = Field(c0_ref, HALO)
    diagonal = Field(diagonal_ref, DIAGONAL_HALO)
    d0 = Field(d0_ref, 4)
    c1 = Field(c1_ref, 3)
    d1 = Field(d1_ref, 2)
    c2 = Field(c2_ref, HALO)
    for field in (d0, c1, d1, c2):
        field.clear_pads()
    fill_halo(c0, own, low_ref, high_ref)
    fill_halo(diagonal, own, low_diagonal_ref, high_diagonal_ref)
    steps = functools.partial(apply_steps, ends_ref, own)
    steps(d0, c0, diagonal, 4)
    steps(c1, d0, diagonal, 3, c0)
    steps(d1, c1, diagonal, 2)
    steps(c2, d1, diagonal, 1, c1)
    for c in range(c2.columns):
        for y in range(HALO):
            for x in range(0, c2.cells, 8):
                down_ref[c, y, pl.ds(x, 8), :] = c2.load(c, y, x)
                up_ref[c, y, pl.ds(x, 8), :] = c2.load(c, own - HALO + y, x)


def middle_kernel(own, c0_ref, c1_ref, c2_ref, diagonal_ref, d2_ref, moments_ref):
    c0 = Field(c0_ref, HALO)
    diagonal = Field(diagonal_ref, DIAGONAL_HALO)
    c1 = Field(c1_ref, 3)
    c2 = Field(c2_ref, HALO)
    d2 = Field(d2_ref, 4)
    d2.clear_pads()
    apply_rows(d2, c2, diagonal, 0, own)

    def moment_row(row, sums):
        for x in range(0, c0.cells, 8):
            for c in range(c0.columns):
                a, b, e, d = (field.load(c, row, x) for field in (c0, c1, c2, d2))
                pairs = ((a, a), (a, b), (b, b), (b, e), (e, e), (d, d))
                sums = tuple(total + u * v for total, (u, v) in zip(sums, pairs))
        return sums

    zero = jnp.zeros((8, 128), jnp.float32)
    sums = lax.fori_loop(0, own, moment_row, (zero,) * 6)
    sums = [jnp.sum(total, axis=0, keepdims=True) for total in sums]
    sums = jnp.concatenate(sums + [zero[:2]], axis=0)
    for part in range(moments_ref.shape[0]):
        moments_ref[part] = sums


def moment_slopes(inverse_count, probe, weights_ref, moments_ref):
    total = moments_ref[0]
    for part in range(1, moments_ref.shape[0]):
        total = total + moments_ref[part]
    total = jnp.sum(total, axis=1, keepdims=True) * inverse_count
    raw = [jnp.broadcast_to(total[k : k + 1], (8, 128)) for k in range(6)]
    moments = tuple(raw[:5]) + (raw[5] - SHIFT * raw[4],)
    weights = [weights_ref[k, probe] for k in range(5)]
    value, pullback = jax.vjp(lambda m: loss_of_moments(m, weights), moments)
    (slopes,) = pullback(jnp.full((8, 128), 2.0, jnp.float32))
    return [slope[0, 0] for slope in slopes]


def last_kernel(
    grid, inverse_count,
    ends_ref, weights_ref, moments_ref, c0_ref, diagonal_ref, d0_ref, c1_ref, d1_ref,
    c2_in, d2_in, low_ref, high_ref,
    c2_ref, d2_ref, out_ref, c3_ref, d3_ref, c4_ref,
):
    nx, nz, bx, by, bz = grid
    c0 = Field(c0_ref, HALO)
    diagonal = Field(diagonal_ref, DIAGONAL_HALO)
    d0 = Field(d0_ref, 4)
    c1 = Field(c1_ref, 3)
    d1 = Field(d1_ref, 2)
    c2 = Field(c2_ref, HALO)
    d2 = Field(d2_ref, 4)
    c3 = Field(c3_ref, 3)
    d3 = Field(d3_ref, 2)
    c4 = Field(c4_ref, 1)
    for field in (c3, d3, c4):
        field.clear_pads()
    slopes = moment_slopes(inverse_count, ends_ref[2], weights_ref, moments_ref)
    fill_halo(c2, by, low_ref, high_ref)
    apply_rows(d2, c2, diagonal, -4, 4)
    apply_rows(d2, c2, diagonal, by, 4)
    clear_outside(ends_ref, by, d2)
    steps = functools.partial(apply_steps, ends_ref, by)
    steps(c3, d2, diagonal, 3, c2)
    steps(d3, c3, diagonal, 2)
    steps(c4, d3, diagonal, 1, c3)
    masks = lane_masks()
    place = {(x, z): (s, column) for s, column, x, z in places(grid)}

    def out_row(step, carry):
        row = step
        results = []
        for x in range(0, c4.cells, 8):
            last = stencil_tiles(c4, diagonal, row, x, masks)
            for z in range(c4.columns):
                cs = [field.load(z, row, x) for field in (c0, c1, c2, c3, c4)]
                ds = [field.load(z, row, x) for field in (d0, d1, d2, d3)] + [last[z]]
                total = None
                for i in range(5):
                    inner = None
                    for j in range(5 - i):
                        term = slopes[i + j + 1] * ds[j]
                        inner = term if inner is None else inner + term
                    term = cs[i] * inner
                    total = term if total is None else total + term
                results.append(place[x, z] + (total,))
        for s, column, total in results:
            out_ref[s, column, pl.ds(step, bx, stride=by), :] = total
        return carry

    lax.fori_loop(0, by, out_row, 0)


def sum_kernel(grid, count, parts_ref, out_ref):
    nx, nz, bx, by, bz = grid
    for column in range(bz // 128):
        for x in range(bx):
            total = None
            for p in range(count):
                part = parts_ref[p, column, pl.ds(x * by, by), :]
                total = part if total is None else total + part
            out_ref[x, :, pl.ds(column * 128, 128)] = total


def vmem():
    return pl.BlockSpec(memory_space=pltpu.VMEM)


def smem():
    return pl.BlockSpec(memory_space=pltpu.SMEM)


def hbm():
    return pl.BlockSpec(memory_space=pltpu.HBM)


def here(value):
    return pltpu.with_memory_space_constraint(value, pltpu.VMEM)


def there(value):
    return pltpu.with_memory_space_constraint(value, pltpu.HBM)


def f32(*shape):
    return jax.ShapeDtypeStruct(shape, jnp.float32)


def params():
    return pltpu.CompilerParams(vmem_limit_bytes=24 * MIB)


def body(probes, kappa2, cotangents):
    nx, ny, nz = (lax.axis_size(axis) for axis in ("gx", "gy", "gz"))
    count, bx, by, bz = probes.shape
    group = nx * nz
    assert group % count == 0 and nx % 2 == 0 and bx == 8 and bz == 256
    assert by % 8 == 0 and by >= HALO
    X = nx * bx
    columns = nz * bz // 128
    per = bz // 128
    rows = bx * by
    grid = (nx, nz, bx, by, bz)
    gx, gy = lax.axis_index("gx"), lax.axis_index("gy")
    mine = (gx * nz + lax.axis_index("gz")) % count
    up = [(i, i + 1) for i in range(ny - 1)]
    down = [(target, source) for source, target in up]
    sibling = [(i, i ^ 1) for i in range(nx)]

    def edge(halo):
        return f32(columns, halo, X, 128)

    def padded(halo):
        return (columns, by + 2 * halo, X + 2 * PAD, 128)

    def vector(halo):
        return pltpu.VMEM(padded(halo), jnp.float32)

    blocks = pl.pallas_call(
        functools.partial(pack_kernel, grid, count),
        out_shape=f32(group, per + 1, rows, 128),
        in_specs=[hbm(), hbm()],
        out_specs=vmem(),
        scratch_shapes=[pltpu.SemaphoreType.DMA((group, per + 1))],
        compiler_params=params(),
        name="pack",
    )(there(probes.reshape(count * rows, bz)), there(kappa2.reshape(rows, bz)))
    blocks = lax.all_to_all(blocks, ("gx", "gz"), 0, 0, tiled=True)
    c0, up_edge, down_edge, half = pl.pallas_call(
        functools.partial(probe_kernel, grid),
        out_shape=(vector(HALO), edge(HALO), edge(HALO), f32(group, rows, 128)),
        in_specs=[vmem()],
        out_specs=(vmem(),) * 4,
        compiler_params=params(),
        name="probe_rows",
    )(blocks)
    low1 = lax.ppermute(up_edge, "gy", up)
    high1 = lax.ppermute(down_edge, "gy", down)
    other = lax.ppermute(half, "gx", sibling)
    diagonal, up_edge, down_edge = pl.pallas_call(
        functools.partial(diagonal_kernel, grid),
        out_shape=(vector(DIAGONAL_HALO), edge(DIAGONAL_HALO), edge(DIAGONAL_HALO)),
        in_specs=[smem(), vmem(), vmem()],
        out_specs=(vmem(),) * 3,
        compiler_params=params(),
        name="diagonal_rows",
    )((gx % 2).astype(jnp.int32).reshape(1), half, other)
    low_diagonal = lax.ppermute(up_edge, "gy", up)
    high_diagonal = lax.ppermute(down_edge, "gy", down)

    ends = jnp.stack([gy == 0, gy == ny - 1, mine]).astype(jnp.int32)
    c0, diagonal, d0, c1, d1, c2, up_edge, down_edge = pl.pallas_call(
        functools.partial(first_kernel, by),
        out_shape=tuple(vector(h) for h in (HALO, DIAGONAL_HALO, 4, 3, 2, HALO))
        + (edge(HALO), edge(HALO)),
        in_specs=[smem()] + [vmem()] * 6,
        out_specs=(vmem(),) * 8,
        input_output_aliases={1: 0, 2: 1},
        compiler_params=params(),
        name="first_steps",
    )(ends, here(c0), here(diagonal), low1, high1, low_diagonal, high_diagonal)
    low2 = lax.ppermute(up_edge, "gy", up)
    high2 = lax.ppermute(down_edge, "gy", down)
    cells = by * X * columns * 128
    d2, moments = pl.pallas_call(
        functools.partial(middle_kernel, by),
        out_shape=(vector(4), f32(ny, 8, 128)),
        in_specs=[vmem()] * 4,
        out_specs=(vmem(),) * 2,
        compiler_params=params(),
        cost_estimate=pl.CostEstimate(
            flops=40 * cells, bytes_accessed=24 * cells, transcendentals=0
        ),
        name="middle_step",
    )(here(c0), here(c1), here(c2), here(diagonal))
    moments = lax.all_to_all(moments, "gy", 0, 0, tiled=True)

    inverse_count = 1.0 / (X * by * ny * columns * 128)
    _, _, out = pl.pallas_call(
        functools.partial(last_kernel, grid, inverse_count),
        out_shape=(vector(HALO), vector(4), f32(group, per, rows, 128)),
        in_specs=[smem(), smem()] + [vmem()] * 10,
        out_specs=(vmem(),) * 3,
        scratch_shapes=[vector(h) for h in (3, 2, 1)],
        input_output_aliases={8: 0, 9: 1},
        compiler_params=params(),
        name="last_steps",
    )(
        ends, cotangents, moments, *(here(x) for x in (c0, diagonal, d0, c1, d1, c2, d2)), low2, high2
    )

    out = lax.all_to_all(out, ("gx", "gz"), 0, 0, tiled=True)
    return pl.pallas_call(
        functools.partial(sum_kernel, grid, count),
        out_shape=f32(bx, by, bz),
        in_specs=[vmem()],
        out_specs=vmem(),
        compiler_params=params(),
        name="sum_probes",
    )(out)


def solution(mesh):
    return jax.shard_map(
        body,
        mesh=mesh,
        in_specs=(P(None, "gx", "gy", "gz"), P("gx", "gy", "gz"), P()),
        out_specs=P("gx", "gy", "gz"),
        check_vma=False,
    )
```

```python
import functools

import jax
import jax.numpy as jnp
from jax import lax
from jax.experimental import pallas as pl
from jax.experimental.pallas import tpu as pltpu
from jax.sharding import PartitionSpec as P

EPSILON = 1e-06
SHIFT = 64.0
HALO = 5
DIAGONAL_HALO = 4
PAD = 8
MIB = 1024 * 1024


def loss_of_moments(moments, weights):
    m0, m1, m2, m3, m4, m5 = moments
    norm = m0 + EPSILON
    alpha1 = (m1 + SHIFT * m0) / norm
    e1 = SHIFT - alpha1
    rest1 = jnp.maximum(m2 + 2.0 * e1 * m1 + e1 * e1 * m0, 0.0)
    beta1_square = rest1 / norm + EPSILON
    beta1 = jnp.sqrt(beta1_square)
    scale = 1.0 / (norm * beta1_square)
    alpha2 = scale * (m3 + 2.0 * e1 * m2 + e1 * e1 * m1 + SHIFT * rest1) - (m1 + e1 * m0) / norm
    e2 = SHIFT - alpha2
    f1 = e1 + e2
    f0 = e1 * e2 - beta1_square
    g = f1 * f1 + 2.0 * f0
    rest2 = jnp.maximum(m4 + 2.0 * f1 * m3 + g * m2 + 2.0 * f1 * f0 * m1 + f0 * f0 * m0, 0.0)
    beta2_square = scale * rest2 + EPSILON
    beta2 = jnp.sqrt(beta2_square)
    image2 = m5 + 2.0 * f1 * m4 + g * m3 + 2.0 * f1 * f0 * m2 + f0 * f0 * m1
    cross = m3 + f1 * m2 + f0 * m1 + e1 * (m2 + f1 * m1 + f0 * m0)
    alpha3 = scale * ((image2 + SHIFT * rest2) / beta2_square - cross)
    return (
        weights[0] * alpha1
        + weights[1] * alpha2
        + weights[2] * alpha3
        + weights[3] * beta1
        + weights[4] * beta2
    )


class Field:
    def __init__(self, ref, halo):
        self.ref = ref
        self.halo = halo
        self.columns, self.rows, self.pitch, _ = ref.shape
        self.cells = self.pitch - 2 * PAD

    def load(self, column, row, x):
        return self.ref[column, row + self.halo, pl.ds(PAD + x, 8), :]

    def store(self, column, row, x, value):
        self.ref[column, row + self.halo, pl.ds(PAD + x, 8), :] = value

    def clear_pads(self):
        zero = jnp.zeros((8, 128), jnp.float32)

        def body(at, carry):
            for column in range(self.columns):
                self.ref[column, at, pl.ds(0, PAD), :] = zero
                self.ref[column, at, pl.ds(PAD + self.cells, PAD), :] = zero
            return carry

        lax.fori_loop(0, self.rows, body, 0)

    def clear_row(self, row):
        zero = jnp.zeros((8, 128), jnp.float32)
        for column in range(self.columns):
            for x in range(0, self.cells, 8):
                self.store(column, row, x, zero)


def lane_masks():
    lane = lax.broadcasted_iota(jnp.int32, (8, 128), 1)
    return lane == 0, lane == 127


def stencil_block(source, diagonal, row, rows, x, masks):
    columns = range(source.columns)
    centre = {(r, c): source.load(c, row + r, x) for r in range(-1, rows + 1) for c in columns}
    results = []
    for r in range(rows):
        after = [pltpu.roll(centre[r, c], 1, 1) for c in columns]
        before = [pltpu.roll(centre[r, c], 127, 1) for c in columns]
        for c in columns:
            low = after[c - 1] if c else 0.0
            high = before[c + 1] if c + 1 < source.columns else 0.0
            total = jnp.where(masks[0], low, after[c]) + jnp.where(masks[1], high, before[c])
            total = total + (source.load(c, row + r, x - 1) + source.load(c, row + r, x + 1))
            total = total + (centre[r - 1, c] + centre[r + 1, c])
            value = diagonal.load(c, row + r, x) * centre[r, c] - total
            results.append((c, row + r, value))
    return results


def apply_block(target, source, diagonal, row, rows, minus, masks):
    for x in range(0, source.cells, 8):
        results = stencil_block(source, diagonal, row, rows, x, masks)
        if minus is not None:
            results = [(c, r, value - SHIFT * minus.load(c, r, x)) for c, r, value in results]
        for c, r, value in results:
            target.store(c, r, x, value)


def apply_rows(target, source, diagonal, first, count, minus=None, block=4):
    masks = lane_masks()

    def body(step, carry):
        apply_block(target, source, diagonal, step * block + first, block, minus, masks)
        return carry

    lax.fori_loop(0, count // block, body, 0)
    if count % block:
        start = first + count - count % block
        apply_block(target, source, diagonal, start, count % block, minus, masks)


def apply_strips(target, source, diagonal, own, halo, minus=None):
    masks = lane_masks()

    def body(step, carry):
        row = step * (own - HALO + 2 * halo) - halo
        apply_block(target, source, diagonal, row, HALO, minus, masks)
        return carry

    lax.fori_loop(0, 2, body, 0)


def clear_outside(ends_ref, own, field):
    @pl.when(ends_ref[0] == 1)
    def _():
        field.clear_row(-1)

    @pl.when(ends_ref[1] == 1)
    def _():
        field.clear_row(own)


def apply_steps(ends_ref, own, target, source, diagonal, halo, minus=None):
    apply_rows(target, source, diagonal, -halo, own + 2 * halo, minus)
    if halo:
        clear_outside(ends_ref, own, target)


def places(grid):
    nx, nz, bx, by, bz = grid
    per = bz // 128
    for s in range(nx * nz):
        for column in range(per):
            yield s, column, (s // nz) * bx, (s % nz) * per + column


def pack_kernel(grid, count, probes_ref, kappa_ref, out_ref, sem):
    nx, nz, bx, by, bz = grid
    per = bz // 128
    rows = bx * by
    copies = []
    for s in range(nx * nz):
        parts = [
            probes_ref.at[pl.ds((s % count) * rows, rows), pl.ds(column * 128, 128)]
            for column in range(per)
        ]
        parts.append(kappa_ref.at[:, pl.ds((s // nz) % 2 * 128, 128)])
        for index, part in enumerate(parts):
            copies.append(pltpu.make_async_copy(part, out_ref.at[s, index], sem.at[s, index]))
    for copy in copies:
        copy.start()
    for copy in copies:
        copy.wait()


def probe_kernel(grid, blocks_ref, own_ref, up_ref, down_ref, half_ref):
    nx, nz, bx, by, bz = grid
    per = bz // 128
    own = Field(own_ref, HALO)
    own.clear_pads()
    for s, column, x, z in places(grid):
        values = [blocks_ref[s, column, pl.ds(y, bx, stride=by), :] for y in range(by)]
        for y in range(by):
            own.store(z, y, x, values[y])
        for y in range(HALO):
            down_ref[z, y, pl.ds(x, bx), :] = values[y]
            up_ref[z, y, pl.ds(x, bx), :] = values[by - HALO + y]
    for s in range(nx * nz):
        half_ref[s] = blocks_ref[s, per]


def diagonal_kernel(grid, core_ref, half_ref, other_ref, own_ref, up_ref, down_ref):
    nx, nz, bx, by, bz = grid
    own = Field(own_ref, DIAGONAL_HALO)
    first = core_ref[0] == 0
    for s, column, x, z in places(grid):
        values = []
        for y in range(by):
            rows = pl.ds(y, bx, stride=by)
            mine, other = half_ref[s, rows, :], other_ref[s, rows, :]
            pair = (mine, other) if column == 0 else (other, mine)
            values.append(6.0 + jnp.where(first, *pair))
        for y in range(by):
            own.store(z, y, x, values[y])
        for y in range(DIAGONAL_HALO):
            down_ref[z, y, pl.ds(x, bx), :] = values[y]
            up_ref[z, y, pl.ds(x, bx), :] = values[by - DIAGONAL_HALO + y]


def fill_halo(field, own, low_ref, high_ref):
    for c in range(field.columns):
        for y in range(field.halo):
            for x in range(0, field.cells, 8):
                field.store(c, y - field.halo, x, low_ref[c, y, pl.ds(x, 8), :])
                field.store(c, own + y, x, high_ref[c, y, pl.ds(x, 8), :])


def inner_kernel(own, c0_ref, diagonal_ref, d0_ref, c1_ref, d1_ref, c2_ref):
    c0 = Field(c0_ref, HALO)
    diagonal = Field(diagonal_ref, DIAGONAL_HALO)
    d0 = Field(d0_ref, 4)
    c1 = Field(c1_ref, 3)
    d1 = Field(d1_ref, 2)
    c2 = Field(c2_ref, HALO)
    for field in (d0, c1, d1, c2):
        field.clear_pads()
    apply_rows(d0, c0, diagonal, 1, own - 2)
    apply_rows(c1, d0, diagonal, 2, own - 4, c0)
    apply_rows(d1, c1, diagonal, 3, own - 6)
    apply_rows(c2, d1, diagonal, 4, own - 8, c1)


def first_kernel(
    own,
    ends_ref, c0_in, diagonal_in, d0_in, c1_in, d1_in, c2_in,
    low_ref, high_ref, low_diagonal_ref, high_diagonal_ref,
    c0_ref, diagonal_ref, d0_ref, c1_ref, d1_ref, c2_ref, up_ref, down_ref,
):
    c0 = Field(c0_ref, HALO)
    diagonal = Field(diagonal_ref, DIAGONAL_HALO)
    d0 = Field(d0_ref, 4)
    c1 = Field(c1_ref, 3)
    d1 = Field(d1_ref, 2)
    c2 = Field(c2_ref, HALO)
    fill_halo(c0, own, low_ref, high_ref)
    fill_halo(diagonal, own, low_diagonal_ref, high_diagonal_ref)
    apply_strips(d0, c0, diagonal, own, 4)
    clear_outside(ends_ref, own, d0)
    apply_strips(c1, d0, diagonal, own, 3, c0)
    clear_outside(ends_ref, own, c1)
    apply_strips(d1, c1, diagonal, own, 2)
    clear_outside(ends_ref, own, d1)
    apply_strips(c2, d1, diagonal, own, 1, c1)
    clear_outside(ends_ref, own, c2)
    for c in range(c2.columns):
        for y in range(HALO):
            for x in range(0, c2.cells, 8):
                down_ref[c, y, pl.ds(x, 8), :] = c2.load(c, y, x)
                up_ref[c, y, pl.ds(x, 8), :] = c2.load(c, own - HALO + y, x)


def middle_kernel(own, c0_ref, c1_ref, c2_ref, diagonal_ref, d2_ref, moments_ref):
    c0 = Field(c0_ref, HALO)
    diagonal = Field(diagonal_ref, DIAGONAL_HALO)
    c1 = Field(c1_ref, 3)
    c2 = Field(c2_ref, HALO)
    d2 = Field(d2_ref, 4)
    d2.clear_pads()
    apply_rows(d2, c2, diagonal, 0, own)

    def moment_row(row, sums):
        for x in range(0, c0.cells, 8):
            for c in range(c0.columns):
                a, b, e, d = (field.load(c, row, x) for field in (c0, c1, c2, d2))
                pairs = ((a, a), (a, b), (b, b), (b, e), (e, e), (d, d))
                sums = tuple(total + u * v for total, (u, v) in zip(sums, pairs))
        return sums

    zero = jnp.zeros((8, 128), jnp.float32)
    sums = lax.fori_loop(0, own, moment_row, (zero,) * 6)
    sums = [jnp.sum(total, axis=0, keepdims=True) for total in sums]
    moments_ref[...] = jnp.concatenate(sums + [zero[:2]], axis=0)


def moment_slopes(inverse_count, probe, weights_ref, moment_refs):
    total = moment_refs[0][...]
    for ref in moment_refs[1:]:
        total = total + ref[...]
    total = jnp.sum(total, axis=1, keepdims=True) * inverse_count
    raw = [jnp.broadcast_to(total[k : k + 1], (8, 128)) for k in range(6)]
    moments = tuple(raw[:5]) + (raw[5] - SHIFT * raw[4],)
    weights = [weights_ref[k, probe] for k in range(5)]
    value, pullback = jax.vjp(lambda m: loss_of_moments(m, weights), moments)
    (slopes,) = pullback(jnp.full((8, 128), 2.0, jnp.float32))
    return [slope[0, 0] for slope in slopes]


def third_kernel(
    own,
    ends_ref, diagonal_ref, c2_in, d2_in, low_ref, high_ref,
    c2_ref, d2_ref, c3_ref, d3_ref, c4_ref,
):
    diagonal = Field(diagonal_ref, DIAGONAL_HALO)
    c2 = Field(c2_ref, HALO)
    d2 = Field(d2_ref, 4)
    c3 = Field(c3_ref, 3)
    d3 = Field(d3_ref, 2)
    c4 = Field(c4_ref, 1)
    for field in (c3, d3, c4):
        field.clear_pads()
    fill_halo(c2, own, low_ref, high_ref)
    apply_rows(d2, c2, diagonal, -4, 4)
    apply_rows(d2, c2, diagonal, own, 4)
    clear_outside(ends_ref, own, d2)
    steps = functools.partial(apply_steps, ends_ref, own)
    steps(c3, d2, diagonal, 3, c2)
    steps(d3, c3, diagonal, 2)
    steps(c4, d3, diagonal, 1, c3)


def last_kernel(
    grid, inverse_count,
    ends_ref, weights_ref, c0_ref, diagonal_ref, d0_ref, c1_ref, d1_ref,
    c2_ref, d2_ref, c3_ref, d3_ref, c4_ref, *rest,
):
    nx, nz, bx, by, bz = grid
    moment_refs, out_ref = rest[:-1], rest[-1]
    c0 = Field(c0_ref, HALO)
    diagonal = Field(diagonal_ref, DIAGONAL_HALO)
    d0 = Field(d0_ref, 4)
    c1 = Field(c1_ref, 3)
    d1 = Field(d1_ref, 2)
    c2 = Field(c2_ref, HALO)
    d2 = Field(d2_ref, 4)
    c3 = Field(c3_ref, 3)
    d3 = Field(d3_ref, 2)
    c4 = Field(c4_ref, 1)
    slopes = moment_slopes(inverse_count, ends_ref[2], weights_ref, moment_refs)
    masks = lane_masks()
    place = {(x, z): (s, column) for s, column, x, z in places(grid)}
    block = 2

    def out_rows(step, carry):
        row = step * block
        for x in range(0, c4.cells, 8):
            results = []
            for z, at, d4 in stencil_block(c4, diagonal, row, block, x, masks):
                cs = [field.load(z, at, x) for field in (c0, c1, c2, c3, c4)]
                ds = [field.load(z, at, x) for field in (d0, d1, d2, d3)] + [d4]
                total = None
                for i in range(5):
                    inner = None
                    for j in range(5 - i):
                        term = slopes[i + j + 1] * ds[j]
                        inner = term if inner is None else inner + term
                    term = cs[i] * inner
                    total = term if total is None else total + term
                results.append(place[x, z] + (at, total))
            for s, column, at, total in results:
                out_ref[s, column, pl.ds(at, bx, stride=by), :] = total
        return carry

    lax.fori_loop(0, by // block, out_rows, 0)


def sum_kernel(grid, count, parts_ref, out_ref):
    nx, nz, bx, by, bz = grid
    for column in range(bz // 128):
        for x in range(bx):
            total = None
            for p in range(count):
                part = parts_ref[p, column, pl.ds(x * by, by), :]
                total = part if total is None else total + part
            out_ref[x, :, pl.ds(column * 128, 128)] = total


def vmem():
    return pl.BlockSpec(memory_space=pltpu.VMEM)


def smem():
    return pl.BlockSpec(memory_space=pltpu.SMEM)


def hbm():
    return pl.BlockSpec(memory_space=pltpu.HBM)


def here(value):
    return pltpu.with_memory_space_constraint(value, pltpu.VMEM)


def there(value):
    return pltpu.with_memory_space_constraint(value, pltpu.HBM)


def f32(*shape):
    return jax.ShapeDtypeStruct(shape, jnp.float32)


def params():
    return pltpu.CompilerParams(vmem_limit_bytes=12 * MIB)


def body(probes, kappa2, cotangents):
    nx, ny, nz = (lax.axis_size(axis) for axis in ("gx", "gy", "gz"))
    count, bx, by, bz = probes.shape
    group = nx * nz
    assert group % count == 0 and nx % 2 == 0 and bx == 8 and bz == 256
    assert by % 8 == 0 and by >= HALO
    X = nx * bx
    columns = nz * bz // 128
    per = bz // 128
    rows = bx * by
    grid = (nx, nz, bx, by, bz)
    gx, gy = lax.axis_index("gx"), lax.axis_index("gy")
    mine = (gx * nz + lax.axis_index("gz")) % count
    up = [(i, i + 1) for i in range(ny - 1)]
    down = [(target, source) for source, target in up]
    sibling = [(i, i ^ 1) for i in range(nx)]

    def edge(halo):
        return f32(columns, halo, X, 128)

    def padded(halo):
        return (columns, by + 2 * halo, X + 2 * PAD, 128)

    def vector(halo):
        return pltpu.VMEM(padded(halo), jnp.float32)

    blocks = pl.pallas_call(
        functools.partial(pack_kernel, grid, count),
        out_shape=f32(group, per + 1, rows, 128),
        in_specs=[hbm(), hbm()],
        out_specs=vmem(),
        scratch_shapes=[pltpu.SemaphoreType.DMA((group, per + 1))],
        compiler_params=params(),
        name="pack",
    )(there(probes.reshape(count * rows, bz)), there(kappa2.reshape(rows, bz)))
    blocks = lax.all_to_all(blocks, ("gx", "gz"), 0, 0, tiled=True)
    c0, up_edge, down_edge, half = pl.pallas_call(
        functools.partial(probe_kernel, grid),
        out_shape=(vector(HALO), edge(HALO), edge(HALO), f32(group, rows, 128)),
        in_specs=[vmem()],
        out_specs=(vmem(),) * 4,
        compiler_params=params(),
        name="probe_rows",
    )(blocks)
    low1 = lax.ppermute(up_edge, "gy", up)
    high1 = lax.ppermute(down_edge, "gy", down)
    other = lax.ppermute(half, "gx", sibling)
    diagonal, up_edge, down_edge = pl.pallas_call(
        functools.partial(diagonal_kernel, grid),
        out_shape=(vector(DIAGONAL_HALO), edge(DIAGONAL_HALO), edge(DIAGONAL_HALO)),
        in_specs=[smem(), vmem(), vmem()],
        out_specs=(vmem(),) * 3,
        compiler_params=params(),
        name="diagonal_rows",
    )((gx % 2).astype(jnp.int32).reshape(1), half, other)
    low_diagonal = lax.ppermute(up_edge, "gy", up)
    high_diagonal = lax.ppermute(down_edge, "gy", down)

    cells = by * X * columns * 128

    def cost(operations):
        return pl.CostEstimate(
            flops=operations * cells, bytes_accessed=16 * cells, transcendentals=0
        )

    inner = pl.pallas_call(
        functools.partial(inner_kernel, by),
        out_shape=tuple(vector(h) for h in (4, 3, 2, HALO)),
        in_specs=[vmem()] * 2,
        out_specs=(vmem(),) * 4,
        compiler_params=params(),
        cost_estimate=cost(32),
        name="inner_steps",
    )(here(c0), here(diagonal))
    ends = jnp.stack([gy == 0, gy == ny - 1, mine]).astype(jnp.int32)
    vectors = [here(value) for value in (c0, diagonal) + tuple(inner)]
    c0, diagonal, d0, c1, d1, c2, up_edge, down_edge = pl.pallas_call(
        functools.partial(first_kernel, by),
        out_shape=tuple(vector(h) for h in (HALO, DIAGONAL_HALO, 4, 3, 2, HALO))
        + (edge(HALO), edge(HALO)),
        in_specs=[smem()] + [vmem()] * 10,
        out_specs=(vmem(),) * 8,
        input_output_aliases={i + 1: i for i in range(6)},
        compiler_params=params(),
        name="first_steps",
    )(ends, *vectors, low1, high1, low_diagonal, high_diagonal)
    low2 = lax.ppermute(up_edge, "gy", up)
    high2 = lax.ppermute(down_edge, "gy", down)
    d2, moments = pl.pallas_call(
        functools.partial(middle_kernel, by),
        out_shape=(vector(4), f32(8, 128)),
        in_specs=[vmem()] * 4,
        out_specs=(vmem(),) * 2,
        compiler_params=params(),
        cost_estimate=cost(24),
        name="middle_step",
    )(here(c0), here(c1), here(c2), here(diagonal))
    shares = [moments]
    for step in range(1, ny):
        shares.append(lax.ppermute(moments, "gy", [(i, (i + step) % ny) for i in range(ny)]))

    c2, d2, c3, d3, c4 = pl.pallas_call(
        functools.partial(third_kernel, by),
        out_shape=tuple(vector(h) for h in (HALO, 4, 3, 2, 1)),
        in_specs=[smem()] + [vmem()] * 5,
        out_specs=(vmem(),) * 5,
        input_output_aliases={2: 0, 3: 1},
        compiler_params=params(),
        cost_estimate=cost(40),
        name="third_steps",
    )(ends, here(diagonal), here(c2), here(d2), low2, high2)
    inverse_count = 1.0 / (ny * cells)
    vectors = [here(value) for value in (c0, diagonal, d0, c1, d1, c2, d2, c3, d3, c4)]
    out = pl.pallas_call(
        functools.partial(last_kernel, grid, inverse_count),
        out_shape=f32(group, per, rows, 128),
        in_specs=[smem(), smem()] + [vmem()] * (10 + ny),
        out_specs=vmem(),
        compiler_params=params(),
        name="last_step",
    )(ends, cotangents, *vectors, *shares)

    out = lax.all_to_all(out, ("gx", "gz"), 0, 0, tiled=True)
    return pl.pallas_call(
        functools.partial(sum_kernel, grid, count),
        out_shape=f32(bx, by, bz),
        in_specs=[vmem()],
        out_specs=vmem(),
        compiler_params=params(),
        name="sum_probes",
    )(out)


def solution(mesh):
    return jax.shard_map(
        body,
        mesh=mesh,
        in_specs=(P(None, "gx", "gy", "gz"), P("gx", "gy", "gz"), P()),
        out_specs=P("gx", "gy", "gz"),
        check_vma=False,
    )
```

```python
import functools

import jax
import jax.numpy as jnp
from jax import lax
from jax.experimental import pallas as pl
from jax.experimental.pallas import tpu as pltpu
from jax.sharding import PartitionSpec as P

EPSILON = 1e-06
SHIFT = 64.0
HALO = 5
DIAGONAL_HALO = 4
PAD = 8
MIB = 1024 * 1024


def loss_of_moments(moments, weights):
    m0, m1, m2, m3, m4, m5 = moments
    norm = m0 + EPSILON
    alpha1 = (m1 + SHIFT * m0) / norm
    e1 = SHIFT - alpha1
    rest1 = jnp.maximum(m2 + 2.0 * e1 * m1 + e1 * e1 * m0, 0.0)
    beta1_square = rest1 / norm + EPSILON
    beta1 = jnp.sqrt(beta1_square)
    scale = 1.0 / (norm * beta1_square)
    alpha2 = scale * (m3 + 2.0 * e1 * m2 + e1 * e1 * m1 + SHIFT * rest1) - (m1 + e1 * m0) / norm
    e2 = SHIFT - alpha2
    f1 = e1 + e2
    f0 = e1 * e2 - beta1_square
    g = f1 * f1 + 2.0 * f0
    rest2 = jnp.maximum(m4 + 2.0 * f1 * m3 + g * m2 + 2.0 * f1 * f0 * m1 + f0 * f0 * m0, 0.0)
    beta2_square = scale * rest2 + EPSILON
    beta2 = jnp.sqrt(beta2_square)
    image2 = m5 + 2.0 * f1 * m4 + g * m3 + 2.0 * f1 * f0 * m2 + f0 * f0 * m1
    cross = m3 + f1 * m2 + f0 * m1 + e1 * (m2 + f1 * m1 + f0 * m0)
    alpha3 = scale * ((image2 + SHIFT * rest2) / beta2_square - cross)
    return (
        weights[0] * alpha1
        + weights[1] * alpha2
        + weights[2] * alpha3
        + weights[3] * beta1
        + weights[4] * beta2
    )


class Field:
    def __init__(self, ref, halo):
        self.ref = ref
        self.halo = halo
        self.columns, self.rows, self.pitch, _ = ref.shape
        self.cells = self.pitch - 2 * PAD

    def load(self, column, row, x):
        return self.ref[column, row + self.halo, pl.ds(PAD + x, 8), :]

    def store(self, column, row, x, value):
        self.ref[column, row + self.halo, pl.ds(PAD + x, 8), :] = value

    def clear_pads(self):
        zero = jnp.zeros((8, 128), jnp.float32)

        def body(at, carry):
            for column in range(self.columns):
                self.ref[column, at, pl.ds(0, PAD), :] = zero
                self.ref[column, at, pl.ds(PAD + self.cells, PAD), :] = zero
            return carry

        lax.fori_loop(0, self.rows, body, 0)

    def clear_row(self, row):
        zero = jnp.zeros((8, 128), jnp.float32)
        for column in range(self.columns):
            for x in range(0, self.cells, 8):
                self.store(column, row, x, zero)


def lane_masks():
    lane = lax.broadcasted_iota(jnp.int32, (8, 128), 1)
    return lane == 0, lane == 127


def stencil_block(source, diagonal, row, rows, x, masks):
    columns = range(source.columns)
    centre = {(r, c): source.load(c, row + r, x) for r in range(-1, rows + 1) for c in columns}
    results = []
    for r in range(rows):
        after = [pltpu.roll(centre[r, c], 1, 1) for c in columns]
        before = [pltpu.roll(centre[r, c], 127, 1) for c in columns]
        for c in columns:
            low = after[c - 1] if c else 0.0
            high = before[c + 1] if c + 1 < source.columns else 0.0
            total = jnp.where(masks[0], low, after[c]) + jnp.where(masks[1], high, before[c])
            total = total + (source.load(c, row + r, x - 1) + source.load(c, row + r, x + 1))
            total = total + (centre[r - 1, c] + centre[r + 1, c])
            value = diagonal.load(c, row + r, x) * centre[r, c] - total
            results.append((c, row + r, value))
    return results


def apply_block(target, source, diagonal, row, rows, minus, masks):
    for x in range(0, source.cells, 8):
        results = stencil_block(source, diagonal, row, rows, x, masks)
        if minus is not None:
            results = [(c, r, value - SHIFT * minus.load(c, r, x)) for c, r, value in results]
        for c, r, value in results:
            target.store(c, r, x, value)


def apply_rows(target, source, diagonal, first, count, minus=None, block=4):
    masks = lane_masks()

    def body(step, carry):
        apply_block(target, source, diagonal, step * block + first, block, minus, masks)
        return carry

    lax.fori_loop(0, count // block, body, 0)
    if count % block:
        start = first + count - count % block
        apply_block(target, source, diagonal, start, count % block, minus, masks)


def apply_strips(target, source, diagonal, own, halo, minus=None):
    masks = lane_masks()

    def body(step, carry):
        row = step * (own - HALO + 2 * halo) - halo
        apply_block(target, source, diagonal, row, HALO, minus, masks)
        return carry

    lax.fori_loop(0, 2, body, 0)


def clear_outside(ends_ref, own, field):
    @pl.when(ends_ref[0] == 1)
    def _():
        field.clear_row(-1)

    @pl.when(ends_ref[1] == 1)
    def _():
        field.clear_row(own)


def apply_steps(ends_ref, own, target, source, diagonal, halo, minus=None):
    apply_rows(target, source, diagonal, -halo, own + 2 * halo, minus)
    if halo:
        clear_outside(ends_ref, own, target)


def places(grid):
    nx, nz, bx, by, bz = grid
    per = bz // 128
    for s in range(nx * nz):
        for column in range(per):
            yield s, column, (s // nz) * bx, (s % nz) * per + column


def pack_kernel(grid, count, probes_ref, kappa_ref, out_ref, sem):
    nx, nz, bx, by, bz = grid
    per = bz // 128
    rows = bx * by
    copies = []
    for s in range(nx * nz):
        parts = [
            probes_ref.at[pl.ds((s % count) * rows, rows), pl.ds(column * 128, 128)]
            for column in range(per)
        ]
        parts.append(kappa_ref.at[:, pl.ds((s // nz) % 2 * 128, 128)])
        for index, part in enumerate(parts):
            copies.append(pltpu.make_async_copy(part, out_ref.at[s, index], sem.at[s, index]))
    for copy in copies:
        copy.start()
    for copy in copies:
        copy.wait()


def half_kernel(blocks_ref, half_ref):
    half_ref[...] = blocks_ref[:, blocks_ref.shape[1] - 1]


def edge_kernel(grid, blocks_ref, up_ref, down_ref):
    nx, nz, bx, by, bz = grid
    for s, column, x, z in places(grid):
        rows = list(range(HALO)) + list(range(by - HALO, by))
        values = [blocks_ref[s, column, pl.ds(y, bx, stride=by), :] for y in rows]
        for y in range(HALO):
            down_ref[z, y, pl.ds(x, bx), :] = values[y]
            up_ref[z, y, pl.ds(x, bx), :] = values[HALO + y]


def diagonal_kernel(
    grid, core_ref, half_ref, other_ref, up_in, down_in, own_ref, up_ref, down_ref
):
    nx, nz, bx, by, bz = grid
    own = Field(own_ref, DIAGONAL_HALO)
    first = core_ref[0] == 0
    up_ref[:, pl.ds(0, HALO)] = up_in[...]
    down_ref[:, pl.ds(0, HALO)] = down_in[...]
    for s, column, x, z in places(grid):
        values = []
        for y in range(by):
            rows = pl.ds(y, bx, stride=by)
            mine, other = half_ref[s, rows, :], other_ref[s, rows, :]
            pair = (mine, other) if column == 0 else (other, mine)
            values.append(6.0 + jnp.where(first, *pair))
        for y in range(by):
            own.store(z, y, x, values[y])
        for y in range(DIAGONAL_HALO):
            down_ref[z, HALO + y, pl.ds(x, bx), :] = values[y]
            up_ref[z, HALO + y, pl.ds(x, bx), :] = values[by - DIAGONAL_HALO + y]


def fill_halo(field, own, low_ref, high_ref, start=0):
    for c in range(field.columns):
        for y in range(field.halo):
            for x in range(0, field.cells, 8):
                field.store(c, y - field.halo, x, low_ref[c, start + y, pl.ds(x, 8), :])
                field.store(c, own + y, x, high_ref[c, start + y, pl.ds(x, 8), :])


def inner_kernel(grid, blocks_ref, diagonal_ref, c0_ref, d0_ref, c1_ref, d1_ref, c2_ref):
    nx, nz, bx, own, bz = grid
    c0 = Field(c0_ref, HALO)
    diagonal = Field(diagonal_ref, DIAGONAL_HALO)
    d0 = Field(d0_ref, 4)
    c1 = Field(c1_ref, 3)
    d1 = Field(d1_ref, 2)
    c2 = Field(c2_ref, HALO)
    for field in (c0, d0, c1, d1, c2):
        field.clear_pads()
    for s, column, x, z in places(grid):
        values = [blocks_ref[s, column, pl.ds(y, bx, stride=own), :] for y in range(own)]
        for y in range(own):
            c0.store(z, y, x, values[y])
    apply_rows(d0, c0, diagonal, 1, own - 2)
    apply_rows(c1, d0, diagonal, 2, own - 4, c0)
    apply_rows(d1, c1, diagonal, 3, own - 6)
    apply_rows(c2, d1, diagonal, 4, own - 8, c1)


def first_kernel(
    own,
    ends_ref, c0_in, diagonal_in, d0_in, c1_in, d1_in, c2_in,
    low_ref, high_ref,
    c0_ref, diagonal_ref, d0_ref, c1_ref, d1_ref, c2_ref, up_ref, down_ref,
):
    c0 = Field(c0_ref, HALO)
    diagonal = Field(diagonal_ref, DIAGONAL_HALO)
    d0 = Field(d0_ref, 4)
    c1 = Field(c1_ref, 3)
    d1 = Field(d1_ref, 2)
    c2 = Field(c2_ref, HALO)
    fill_halo(c0, own, low_ref, high_ref)
    fill_halo(diagonal, own, low_ref, high_ref, HALO)
    apply_strips(d0, c0, diagonal, own, 4)
    clear_outside(ends_ref, own, d0)
    apply_strips(c1, d0, diagonal, own, 3, c0)
    clear_outside(ends_ref, own, c1)
    apply_strips(d1, c1, diagonal, own, 2)
    clear_outside(ends_ref, own, d1)
    apply_strips(c2, d1, diagonal, own, 1, c1)
    clear_outside(ends_ref, own, c2)
    for c in range(c2.columns):
        for y in range(HALO):
            for x in range(0, c2.cells, 8):
                down_ref[c, y, pl.ds(x, 8), :] = c2.load(c, y, x)
                up_ref[c, y, pl.ds(x, 8), :] = c2.load(c, own - HALO + y, x)


def middle_kernel(own, c0_ref, c1_ref, c2_ref, diagonal_ref, d2_ref, moments_ref):
    c0 = Field(c0_ref, HALO)
    diagonal = Field(diagonal_ref, DIAGONAL_HALO)
    c1 = Field(c1_ref, 3)
    c2 = Field(c2_ref, HALO)
    d2 = Field(d2_ref, 4)
    d2.clear_pads()
    apply_rows(d2, c2, diagonal, 0, own)

    def moment_row(row, sums):
        for x in range(0, c0.cells, 8):
            for c in range(c0.columns):
                a, b, e, d = (field.load(c, row, x) for field in (c0, c1, c2, d2))
                pairs = ((a, a), (a, b), (b, b), (b, e), (e, e), (d, d))
                sums = tuple(total + u * v for total, (u, v) in zip(sums, pairs))
        return sums

    zero = jnp.zeros((8, 128), jnp.float32)
    sums = lax.fori_loop(0, own, moment_row, (zero,) * 6)
    sums = [jnp.sum(total, axis=0, keepdims=True) for total in sums]
    moments_ref[...] = jnp.concatenate(sums + [zero[:2]], axis=0)


def moment_slopes(inverse_count, probe, weights_ref, moment_refs):
    total = moment_refs[0][...]
    for ref in moment_refs[1:]:
        total = total + ref[...]
    total = jnp.sum(total, axis=1, keepdims=True) * inverse_count
    raw = [jnp.broadcast_to(total[k : k + 1], (8, 128)) for k in range(6)]
    moments = tuple(raw[:5]) + (raw[5] - SHIFT * raw[4],)
    weights = [weights_ref[k, probe] for k in range(5)]
    value, pullback = jax.vjp(lambda m: loss_of_moments(m, weights), moments)
    (slopes,) = pullback(jnp.full((8, 128), 2.0, jnp.float32))
    return [slope[0, 0] for slope in slopes]


def third_kernel(
    own,
    ends_ref, diagonal_ref, c2_in, d2_in, low_ref, high_ref,
    c2_ref, d2_ref, c3_ref, d3_ref, c4_ref,
):
    diagonal = Field(diagonal_ref, DIAGONAL_HALO)
    c2 = Field(c2_ref, HALO)
    d2 = Field(d2_ref, 4)
    c3 = Field(c3_ref, 3)
    d3 = Field(d3_ref, 2)
    c4 = Field(c4_ref, 1)
    for field in (c3, d3, c4):
        field.clear_pads()
    fill_halo(c2, own, low_ref, high_ref)
    apply_rows(d2, c2, diagonal, -4, 4)
    apply_rows(d2, c2, diagonal, own, 4)
    clear_outside(ends_ref, own, d2)
    steps = functools.partial(apply_steps, ends_ref, own)
    steps(c3, d2, diagonal, 3, c2)
    steps(d3, c3, diagonal, 2)
    steps(c4, d3, diagonal, 1, c3)


def last_kernel(
    grid, inverse_count,
    ends_ref, weights_ref, c0_ref, diagonal_ref, d0_ref, c1_ref, d1_ref,
    c2_ref, d2_ref, c3_ref, d3_ref, c4_ref, *rest,
):
    nx, nz, bx, by, bz = grid
    moment_refs, out_ref = rest[:-1], rest[-1]
    c0 = Field(c0_ref, HALO)
    diagonal = Field(diagonal_ref, DIAGONAL_HALO)
    d0 = Field(d0_ref, 4)
    c1 = Field(c1_ref, 3)
    d1 = Field(d1_ref, 2)
    c2 = Field(c2_ref, HALO)
    d2 = Field(d2_ref, 4)
    c3 = Field(c3_ref, 3)
    d3 = Field(d3_ref, 2)
    c4 = Field(c4_ref, 1)
    slopes = moment_slopes(inverse_count, ends_ref[2], weights_ref, moment_refs)
    masks = lane_masks()
    place = {(x, z): (s, column) for s, column, x, z in places(grid)}
    block = 2

    def out_rows(step, carry):
        row = step * block
        for x in range(0, c4.cells, 8):
            results = []
            for z, at, d4 in stencil_block(c4, diagonal, row, block, x, masks):
                cs = [field.load(z, at, x) for field in (c0, c1, c2, c3, c4)]
                ds = [field.load(z, at, x) for field in (d0, d1, d2, d3)] + [d4]
                total = None
                for i in range(5):
                    inner = None
                    for j in range(5 - i):
                        term = slopes[i + j + 1] * ds[j]
                        inner = term if inner is None else inner + term
                    term = cs[i] * inner
                    total = term if total is None else total + term
                results.append(place[x, z] + (at, total))
            for s, column, at, total in results:
                out_ref[s, column, pl.ds(at, bx, stride=by), :] = total
        return carry

    lax.fori_loop(0, by // block, out_rows, 0)


def sum_kernel(grid, count, parts_ref, out_ref):
    nx, nz, bx, by, bz = grid
    for column in range(bz // 128):
        for x in range(bx):
            total = None
            for p in range(count):
                part = parts_ref[p, column, pl.ds(x * by, by), :]
                total = part if total is None else total + part
            out_ref[x, :, pl.ds(column * 128, 128)] = total


def vmem():
    return pl.BlockSpec(memory_space=pltpu.VMEM)


def smem():
    return pl.BlockSpec(memory_space=pltpu.SMEM)


def hbm():
    return pl.BlockSpec(memory_space=pltpu.HBM)


def here(value):
    return pltpu.with_memory_space_constraint(value, pltpu.VMEM)


def there(value):
    return pltpu.with_memory_space_constraint(value, pltpu.HBM)


def f32(*shape):
    return jax.ShapeDtypeStruct(shape, jnp.float32)


def params():
    return pltpu.CompilerParams(vmem_limit_bytes=12 * MIB)


def body(probes, kappa2, cotangents):
    nx, ny, nz = (lax.axis_size(axis) for axis in ("gx", "gy", "gz"))
    count, bx, by, bz = probes.shape
    group = nx * nz
    assert group % count == 0 and nx % 2 == 0 and bx == 8 and bz == 256
    assert by % 8 == 0 and by >= HALO
    X = nx * bx
    columns = nz * bz // 128
    per = bz // 128
    rows = bx * by
    grid = (nx, nz, bx, by, bz)
    gx, gy = lax.axis_index("gx"), lax.axis_index("gy")
    mine = (gx * nz + lax.axis_index("gz")) % count
    up = [(i, i + 1) for i in range(ny - 1)]
    down = [(target, source) for source, target in up]
    sibling = [(i, i ^ 1) for i in range(nx)]

    def edge(halo):
        return f32(columns, halo, X, 128)

    def padded(halo):
        return (columns, by + 2 * halo, X + 2 * PAD, 128)

    def vector(halo):
        return pltpu.VMEM(padded(halo), jnp.float32)

    blocks = pl.pallas_call(
        functools.partial(pack_kernel, grid, count),
        out_shape=f32(group, per + 1, rows, 128),
        in_specs=[hbm(), hbm()],
        out_specs=vmem(),
        scratch_shapes=[pltpu.SemaphoreType.DMA((group, per + 1))],
        compiler_params=params(),
        name="pack",
    )(there(probes.reshape(count * rows, bz)), there(kappa2.reshape(rows, bz)))
    blocks = lax.all_to_all(blocks, ("gx", "gz"), 0, 0, tiled=True)
    half = pl.pallas_call(
        half_kernel,
        out_shape=f32(group, rows, 128),
        in_specs=[vmem()],
        out_specs=vmem(),
        compiler_params=params(),
        name="half",
    )(here(blocks))
    other = lax.ppermute(half, "gx", sibling)
    message = edge(HALO + DIAGONAL_HALO)
    up_edge, down_edge = pl.pallas_call(
        functools.partial(edge_kernel, grid),
        out_shape=(edge(HALO), edge(HALO)),
        in_specs=[vmem()],
        out_specs=(vmem(),) * 2,
        compiler_params=params(),
        name="probe_edges",
    )(here(blocks))
    diagonal, up_edge, down_edge = pl.pallas_call(
        functools.partial(diagonal_kernel, grid),
        out_shape=(vector(DIAGONAL_HALO), message, message),
        in_specs=[smem()] + [vmem()] * 4,
        out_specs=(vmem(),) * 3,
        compiler_params=params(),
        name="diagonal_rows",
    )((gx % 2).astype(jnp.int32).reshape(1), half, other, up_edge, down_edge)
    low1 = lax.ppermute(up_edge, "gy", up)
    high1 = lax.ppermute(down_edge, "gy", down)

    cells = by * X * columns * 128

    def cost(operations):
        return pl.CostEstimate(
            flops=operations * cells, bytes_accessed=16 * cells, transcendentals=0
        )

    inner = pl.pallas_call(
        functools.partial(inner_kernel, grid),
        out_shape=tuple(vector(h) for h in (HALO, 4, 3, 2, HALO)),
        in_specs=[vmem()] * 2,
        out_specs=(vmem(),) * 5,
        compiler_params=params(),
        cost_estimate=cost(32),
        name="inner_steps",
    )(here(blocks), here(diagonal))
    ends = jnp.stack([gy == 0, gy == ny - 1, mine]).astype(jnp.int32)
    vectors = [here(value) for value in (inner[0], diagonal) + tuple(inner[1:])]
    c0, diagonal, d0, c1, d1, c2, up_edge, down_edge = pl.pallas_call(
        functools.partial(first_kernel, by),
        out_shape=tuple(vector(h) for h in (HALO, DIAGONAL_HALO, 4, 3, 2, HALO))
        + (edge(HALO), edge(HALO)),
        in_specs=[smem()] + [vmem()] * 8,
        out_specs=(vmem(),) * 8,
        input_output_aliases={i + 1: i for i in range(6)},
        compiler_params=params(),
        name="first_steps",
    )(ends, *vectors, low1, high1)
    low2 = lax.ppermute(up_edge, "gy", up)
    high2 = lax.ppermute(down_edge, "gy", down)
    d2, moments = pl.pallas_call(
        functools.partial(middle_kernel, by),
        out_shape=(vector(4), f32(8, 128)),
        in_specs=[vmem()] * 4,
        out_specs=(vmem(),) * 2,
        compiler_params=params(),
        cost_estimate=cost(24),
        name="middle_step",
    )(here(c0), here(c1), here(c2), here(diagonal))
    shares = [moments]
    for step in range(1, ny):
        shares.append(lax.ppermute(moments, "gy", [(i, (i + step) % ny) for i in range(ny)]))

    c2, d2, c3, d3, c4 = pl.pallas_call(
        functools.partial(third_kernel, by),
        out_shape=tuple(vector(h) for h in (HALO, 4, 3, 2, 1)),
        in_specs=[smem()] + [vmem()] * 5,
        out_specs=(vmem(),) * 5,
        input_output_aliases={2: 0, 3: 1},
        compiler_params=params(),
        cost_estimate=cost(40),
        name="third_steps",
    )(ends, here(diagonal), here(c2), here(d2), low2, high2)
    inverse_count = 1.0 / (ny * cells)
    vectors = [here(value) for value in (c0, diagonal, d0, c1, d1, c2, d2, c3, d3, c4)]
    out = pl.pallas_call(
        functools.partial(last_kernel, grid, inverse_count),
        out_shape=f32(group, per, rows, 128),
        in_specs=[smem(), smem()] + [vmem()] * (10 + ny),
        out_specs=vmem(),
        compiler_params=params(),
        name="last_step",
    )(ends, cotangents, *vectors, *shares)

    out = lax.all_to_all(out, ("gx", "gz"), 0, 0, tiled=True)
    return pl.pallas_call(
        functools.partial(sum_kernel, grid, count),
        out_shape=f32(bx, by, bz),
        in_specs=[vmem()],
        out_specs=vmem(),
        compiler_params=params(),
        name="sum_probes",
    )(out)


def solution(mesh):
    return jax.shard_map(
        body,
        mesh=mesh,
        in_specs=(P(None, "gx", "gy", "gz"), P("gx", "gy", "gz"), P()),
        out_specs=P("gx", "gy", "gz"),
        check_vma=False,
    )
```

```python
import functools

import jax
import jax.numpy as jnp
from jax import lax
from jax.experimental import pallas as pl
from jax.experimental.pallas import tpu as pltpu
from jax.sharding import PartitionSpec as P

EPSILON = 1e-06
SHIFT = 64.0
HALO = 5
DIAGONAL_HALO = 4
PAD = 8
MIB = 1024 * 1024


def loss_of_moments(moments, weights):
    m0, m1, m2, m3, m4, m5 = moments
    norm = m0 + EPSILON
    alpha1 = (m1 + SHIFT * m0) / norm
    e1 = SHIFT - alpha1
    rest1 = jnp.maximum(m2 + 2.0 * e1 * m1 + e1 * e1 * m0, 0.0)
    beta1_square = rest1 / norm + EPSILON
    beta1 = jnp.sqrt(beta1_square)
    scale = 1.0 / (norm * beta1_square)
    alpha2 = scale * (m3 + 2.0 * e1 * m2 + e1 * e1 * m1 + SHIFT * rest1) - (m1 + e1 * m0) / norm
    e2 = SHIFT - alpha2
    f1 = e1 + e2
    f0 = e1 * e2 - beta1_square
    g = f1 * f1 + 2.0 * f0
    rest2 = jnp.maximum(m4 + 2.0 * f1 * m3 + g * m2 + 2.0 * f1 * f0 * m1 + f0 * f0 * m0, 0.0)
    beta2_square = scale * rest2 + EPSILON
    beta2 = jnp.sqrt(beta2_square)
    image2 = m5 + 2.0 * f1 * m4 + g * m3 + 2.0 * f1 * f0 * m2 + f0 * f0 * m1
    cross = m3 + f1 * m2 + f0 * m1 + e1 * (m2 + f1 * m1 + f0 * m0)
    alpha3 = scale * ((image2 + SHIFT * rest2) / beta2_square - cross)
    return (
        weights[0] * alpha1
        + weights[1] * alpha2
        + weights[2] * alpha3
        + weights[3] * beta1
        + weights[4] * beta2
    )


class Field:
    def __init__(self, ref, halo):
        self.ref = ref
        self.halo = halo
        self.columns, self.rows, self.pitch, _ = ref.shape
        self.cells = self.pitch - 2 * PAD

    def load(self, column, row, x):
        return self.ref[column, row + self.halo, pl.ds(PAD + x, 8), :]

    def store(self, column, row, x, value):
        self.ref[column, row + self.halo, pl.ds(PAD + x, 8), :] = value

    def clear_pads(self):
        zero = jnp.zeros((8, 128), jnp.float32)

        def body(at, carry):
            for column in range(self.columns):
                self.ref[column, at, pl.ds(0, PAD), :] = zero
                self.ref[column, at, pl.ds(PAD + self.cells, PAD), :] = zero
            return carry

        lax.fori_loop(0, self.rows, body, 0)

    def clear_row(self, row):
        zero = jnp.zeros((8, 128), jnp.float32)
        for column in range(self.columns):
            for x in range(0, self.cells, 8):
                self.store(column, row, x, zero)


def lane_masks():
    lane = lax.broadcasted_iota(jnp.int32, (8, 128), 1)
    return lane == 0, lane == 127


def stencil_block(source, diagonal, row, rows, x, masks):
    columns = range(source.columns)
    centre = {(r, c): source.load(c, row + r, x) for r in range(-1, rows + 1) for c in columns}
    results = []
    for r in range(rows):
        after = [pltpu.roll(centre[r, c], 1, 1) for c in columns]
        before = [pltpu.roll(centre[r, c], 127, 1) for c in columns]
        for c in columns:
            low = after[c - 1] if c else 0.0
            high = before[c + 1] if c + 1 < source.columns else 0.0
            total = jnp.where(masks[0], low, after[c]) + jnp.where(masks[1], high, before[c])
            total = total + (source.load(c, row + r, x - 1) + source.load(c, row + r, x + 1))
            total = total + (centre[r - 1, c] + centre[r + 1, c])
            value = diagonal.load(c, row + r, x) * centre[r, c] - total
            results.append((c, row + r, value))
    return results


def apply_block(target, source, diagonal, row, rows, minus, masks):
    for x in range(0, source.cells, 8):
        results = stencil_block(source, diagonal, row, rows, x, masks)
        if minus is not None:
            results = [(c, r, value - SHIFT * minus.load(c, r, x)) for c, r, value in results]
        for c, r, value in results:
            target.store(c, r, x, value)


def apply_rows(target, source, diagonal, first, count, minus=None, block=4):
    masks = lane_masks()

    def body(step, carry):
        apply_block(target, source, diagonal, step * block + first, block, minus, masks)
        return carry

    lax.fori_loop(0, count // block, body, 0)
    if count % block:
        start = first + count - count % block
        apply_block(target, source, diagonal, start, count % block, minus, masks)


def apply_strips(ends_ref, own, target, source, diagonal, halo, size, minus=None):
    masks = lane_masks()

    def body(step, carry):
        row = step * (own - size + 2 * halo) - halo
        apply_block(target, source, diagonal, row, size, minus, masks)
        return carry

    lax.fori_loop(0, 2, body, 0)
    clear_outside(ends_ref, own, target)


def clear_outside(ends_ref, own, field):
    @pl.when(ends_ref[0] == 1)
    def _():
        field.clear_row(-1)

    @pl.when(ends_ref[1] == 1)
    def _():
        field.clear_row(own)


def places(grid):
    nx, nz, bx, by, bz = grid
    per = bz // 128
    for s in range(nx * nz):
        for column in range(per):
            yield s, column, (s // nz) * bx, (s % nz) * per + column


def pack_kernel(grid, count, probes_ref, kappa_ref, out_ref, sem):
    nx, nz, bx, by, bz = grid
    per = bz // 128
    rows = bx * by
    copies = []
    for s in range(nx * nz):
        parts = [
            probes_ref.at[pl.ds((s % count) * rows, rows), pl.ds(column * 128, 128)]
            for column in range(per)
        ]
        parts.append(kappa_ref.at[:, pl.ds((s // nz) % 2 * 128, 128)])
        for index, part in enumerate(parts):
            copies.append(pltpu.make_async_copy(part, out_ref.at[s, index], sem.at[s, index]))
    for copy in copies:
        copy.start()
    for copy in copies:
        copy.wait()


def half_kernel(blocks_ref, half_ref):
    half_ref[...] = blocks_ref[:, blocks_ref.shape[1] - 1]


def edge_kernel(grid, blocks_ref, up_ref, down_ref):
    nx, nz, bx, by, bz = grid
    for s, column, x, z in places(grid):
        rows = list(range(HALO)) + list(range(by - HALO, by))
        values = [blocks_ref[s, column, pl.ds(y, bx, stride=by), :] for y in rows]
        for y in range(HALO):
            down_ref[z, y, pl.ds(x, bx), :] = values[y]
            up_ref[z, y, pl.ds(x, bx), :] = values[HALO + y]


def diagonal_kernel(
    grid, core_ref, half_ref, other_ref, up_in, down_in, own_ref, up_ref, down_ref
):
    nx, nz, bx, by, bz = grid
    own = Field(own_ref, DIAGONAL_HALO)
    first = core_ref[0] == 0
    up_ref[:, pl.ds(0, HALO)] = up_in[...]
    down_ref[:, pl.ds(0, HALO)] = down_in[...]
    for s, column, x, z in places(grid):
        values = []
        for y in range(by):
            rows = pl.ds(y, bx, stride=by)
            mine, other = half_ref[s, rows, :], other_ref[s, rows, :]
            pair = (mine, other) if column == 0 else (other, mine)
            values.append(6.0 + jnp.where(first, *pair))
        for y in range(by):
            own.store(z, y, x, values[y])
        for y in range(DIAGONAL_HALO):
            down_ref[z, HALO + y, pl.ds(x, bx), :] = values[y]
            up_ref[z, HALO + y, pl.ds(x, bx), :] = values[by - DIAGONAL_HALO + y]


def fill_halo(field, own, low_ref, high_ref, start=0):
    for c in range(field.columns):
        for y in range(field.halo):
            for x in range(0, field.cells, 8):
                field.store(c, y - field.halo, x, low_ref[c, start + y, pl.ds(x, 8), :])
                field.store(c, own + y, x, high_ref[c, start + y, pl.ds(x, 8), :])


def inner_kernel(grid, blocks_ref, diagonal_ref, c0_ref, d0_ref, c1_ref, d1_ref, c2_ref):
    nx, nz, bx, own, bz = grid
    c0 = Field(c0_ref, HALO)
    diagonal = Field(diagonal_ref, DIAGONAL_HALO)
    d0 = Field(d0_ref, 4)
    c1 = Field(c1_ref, 3)
    d1 = Field(d1_ref, 2)
    c2 = Field(c2_ref, HALO)
    for field in (c0, d0, c1, d1, c2):
        field.clear_pads()
    for s, column, x, z in places(grid):
        values = [blocks_ref[s, column, pl.ds(y, bx, stride=own), :] for y in range(own)]
        for y in range(own):
            c0.store(z, y, x, values[y])
    apply_rows(d0, c0, diagonal, 1, own - 2)
    apply_rows(c1, d0, diagonal, 2, own - 4, c0)
    apply_rows(d1, c1, diagonal, 3, own - 6)
    apply_rows(c2, d1, diagonal, 4, own - 8, c1)


def first_kernel(
    own,
    ends_ref, c0_in, diagonal_in, d0_in, c1_in, d1_in, c2_in,
    low_ref, high_ref,
    c0_ref, diagonal_ref, d0_ref, c1_ref, d1_ref, c2_ref, up_ref, down_ref,
):
    c0 = Field(c0_ref, HALO)
    diagonal = Field(diagonal_ref, DIAGONAL_HALO)
    d0 = Field(d0_ref, 4)
    c1 = Field(c1_ref, 3)
    d1 = Field(d1_ref, 2)
    c2 = Field(c2_ref, HALO)
    fill_halo(c0, own, low_ref, high_ref)
    fill_halo(diagonal, own, low_ref, high_ref, HALO)
    strips = functools.partial(apply_strips, ends_ref, own)
    strips(d0, c0, diagonal, 4, HALO)
    strips(c1, d0, diagonal, 3, HALO, c0)
    strips(d1, c1, diagonal, 2, HALO)
    strips(c2, d1, diagonal, 1, HALO, c1)
    for c in range(c2.columns):
        for y in range(HALO):
            for x in range(0, c2.cells, 8):
                down_ref[c, y, pl.ds(x, 8), :] = c2.load(c, y, x)
                up_ref[c, y, pl.ds(x, 8), :] = c2.load(c, own - HALO + y, x)


def middle_kernel(own, c0_ref, c1_ref, c2_ref, diagonal_ref, d2_ref, moments_ref):
    c0 = Field(c0_ref, HALO)
    diagonal = Field(diagonal_ref, DIAGONAL_HALO)
    c1 = Field(c1_ref, 3)
    c2 = Field(c2_ref, HALO)
    d2 = Field(d2_ref, 4)
    d2.clear_pads()
    apply_rows(d2, c2, diagonal, 0, own)

    def moment_row(row, sums):
        for x in range(0, c0.cells, 8):
            for c in range(c0.columns):
                a, b, e, d = (field.load(c, row, x) for field in (c0, c1, c2, d2))
                pairs = ((a, a), (a, b), (b, b), (b, e), (e, e), (d, d))
                sums = tuple(total + u * v for total, (u, v) in zip(sums, pairs))
        return sums

    zero = jnp.zeros((8, 128), jnp.float32)
    sums = lax.fori_loop(0, own, moment_row, (zero,) * 6)
    sums = [jnp.sum(total, axis=0, keepdims=True) for total in sums]
    moments_ref[...] = jnp.concatenate(sums + [zero[:2]], axis=0)


def moment_slopes(inverse_count, probe, weights_ref, moment_refs):
    total = moment_refs[0][...]
    for ref in moment_refs[1:]:
        total = total + ref[...]
    total = jnp.sum(total, axis=1, keepdims=True) * inverse_count
    raw = [jnp.broadcast_to(total[k : k + 1], (8, 128)) for k in range(6)]
    moments = tuple(raw[:5]) + (raw[5] - SHIFT * raw[4],)
    weights = [weights_ref[k, probe] for k in range(5)]
    value, pullback = jax.vjp(lambda m: loss_of_moments(m, weights), moments)
    (slopes,) = pullback(jnp.full((8, 128), 2.0, jnp.float32))
    return [slope[0, 0] for slope in slopes]


def second_inner_kernel(own, diagonal_ref, c2_ref, d2_ref, c3_ref, d3_ref, c4_ref):
    diagonal = Field(diagonal_ref, DIAGONAL_HALO)
    c2 = Field(c2_ref, HALO)
    d2 = Field(d2_ref, 4)
    c3 = Field(c3_ref, 3)
    d3 = Field(d3_ref, 2)
    c4 = Field(c4_ref, 1)
    for field in (c3, d3, c4):
        field.clear_pads()
    apply_rows(c3, d2, diagonal, 1, own - 2, c2)
    apply_rows(d3, c3, diagonal, 2, own - 4)
    apply_rows(c4, d3, diagonal, 3, own - 6, c3)


def third_kernel(
    own,
    ends_ref, diagonal_ref, c2_in, d2_in, c3_in, d3_in, c4_in, low_ref, high_ref,
    c2_ref, d2_ref, c3_ref, d3_ref, c4_ref,
):
    diagonal = Field(diagonal_ref, DIAGONAL_HALO)
    c2 = Field(c2_ref, HALO)
    d2 = Field(d2_ref, 4)
    c3 = Field(c3_ref, 3)
    d3 = Field(d3_ref, 2)
    c4 = Field(c4_ref, 1)
    fill_halo(c2, own, low_ref, high_ref)
    strips = functools.partial(apply_strips, ends_ref, own)
    strips(d2, c2, diagonal, 4, 4)
    strips(c3, d2, diagonal, 3, 4, c2)
    strips(d3, c3, diagonal, 2, 4)
    strips(c4, d3, diagonal, 1, 4, c3)


def last_kernel(
    grid, inverse_count, flip,
    ends_ref, weights_ref, c0_ref, diagonal_ref, d0_ref, c1_ref, d1_ref,
    c2_ref, d2_ref, c3_ref, d3_ref, c4_ref, *rest,
):
    nx, nz, bx, by, bz = grid
    per = bz // 128
    moment_refs, out_ref = rest[:-1], rest[-1]
    c0 = Field(c0_ref, HALO)
    diagonal = Field(diagonal_ref, DIAGONAL_HALO)
    d0 = Field(d0_ref, 4)
    c1 = Field(c1_ref, 3)
    d1 = Field(d1_ref, 2)
    c2 = Field(c2_ref, HALO)
    d2 = Field(d2_ref, 4)
    c3 = Field(c3_ref, 3)
    d3 = Field(d3_ref, 2)
    c4 = Field(c4_ref, 1)
    slopes = moment_slopes(inverse_count, ends_ref[2], weights_ref, moment_refs)
    masks = lane_masks()
    block = 2

    def out_rows(core, step, carry):
        row = step * block
        for chip in range(nx // 2):
            x = (2 * chip + core) * bx
            results = []
            for z, at, d4 in stencil_block(c4, diagonal, row, block, x, masks):
                cs = [field.load(z, at, x) for field in (c0, c1, c2, c3, c4)]
                ds = [field.load(z, at, x) for field in (d0, d1, d2, d3)] + [d4]
                total = None
                for i in range(5):
                    inner = None
                    for j in range(5 - i):
                        term = slopes[i + j + 1] * ds[j]
                        inner = term if inner is None else inner + term
                    term = cs[i] * inner
                    total = term if total is None else total + term
                results.append((chip * nz + z // per, z % per, at, total))
            for place, column, at, total in results:
                out_ref[place, column, pl.ds(at, bx, stride=by), :] = total
        return carry

    for core in range(2):

        @pl.when(ends_ref[3] == (1 - core if flip else core))
        def _():
            lax.fori_loop(0, by // block, functools.partial(out_rows, core), 0)


def add_kernel(kept_ref, got_ref, out_ref):
    out_ref[...] = kept_ref[...] + got_ref[...]


def sum_kernel(grid, parts_ref, out_ref):
    nx, nz, bx, by, bz = grid
    for column in range(bz // 128):
        for x in range(bx):
            total = None
            for p in range(parts_ref.shape[0]):
                part = parts_ref[p, column, pl.ds(x * by, by), :]
                total = part if total is None else total + part
            out_ref[x, :, pl.ds(column * 128, 128)] = total


def vmem():
    return pl.BlockSpec(memory_space=pltpu.VMEM)


def smem():
    return pl.BlockSpec(memory_space=pltpu.SMEM)


def hbm():
    return pl.BlockSpec(memory_space=pltpu.HBM)


def here(value):
    return pltpu.with_memory_space_constraint(value, pltpu.VMEM)


def there(value):
    return pltpu.with_memory_space_constraint(value, pltpu.HBM)


def f32(*shape):
    return jax.ShapeDtypeStruct(shape, jnp.float32)


def params():
    return pltpu.CompilerParams(vmem_limit_bytes=12 * MIB)


def body(probes, kappa2, cotangents):
    nx, ny, nz = (lax.axis_size(axis) for axis in (("chip", "core"), "gy", "gz"))
    count, bx, by, bz = probes.shape
    group = nx * nz
    assert group % count == 0 and nx % 2 == 0 and bx == 8 and bz == 256
    assert by % 8 == 0 and by >= HALO
    X = nx * bx
    columns = nz * bz // 128
    per = bz // 128
    rows = bx * by
    grid = (nx, nz, bx, by, bz)
    core, gy = lax.axis_index("core"), lax.axis_index("gy")
    place = (lax.axis_index("chip") * 2 + core) * nz + lax.axis_index("gz")
    mine = place % count
    up = [(i, i + 1) for i in range(ny - 1)]
    down = [(target, source) for source, target in up]
    swap = [(0, 1), (1, 0)]

    def edge(halo):
        return f32(columns, halo, X, 128)

    def padded(halo):
        return (columns, by + 2 * halo, X + 2 * PAD, 128)

    def vector(halo):
        return pltpu.VMEM(padded(halo), jnp.float32)

    blocks = pl.pallas_call(
        functools.partial(pack_kernel, grid, count),
        out_shape=f32(group, per + 1, rows, 128),
        in_specs=[hbm(), hbm()],
        out_specs=vmem(),
        scratch_shapes=[pltpu.SemaphoreType.DMA((group, per + 1))],
        compiler_params=params(),
        name="pack",
    )(there(probes.reshape(count * rows, bz)), there(kappa2.reshape(rows, bz)))
    blocks = lax.all_to_all(blocks, ("chip", "core", "gz"), 0, 0, tiled=True)
    half = pl.pallas_call(
        half_kernel,
        out_shape=f32(group, rows, 128),
        in_specs=[vmem()],
        out_specs=vmem(),
        compiler_params=params(),
        name="half",
    )(here(blocks))
    other = lax.ppermute(half, "core", swap)
    message = edge(HALO + DIAGONAL_HALO)
    up_edge, down_edge = pl.pallas_call(
        functools.partial(edge_kernel, grid),
        out_shape=(edge(HALO), edge(HALO)),
        in_specs=[vmem()],
        out_specs=(vmem(),) * 2,
        compiler_params=params(),
        name="probe_edges",
    )(here(blocks))
    diagonal, up_edge, down_edge = pl.pallas_call(
        functools.partial(diagonal_kernel, grid),
        out_shape=(vector(DIAGONAL_HALO), message, message),
        in_specs=[smem()] + [vmem()] * 4,
        out_specs=(vmem(),) * 3,
        compiler_params=params(),
        name="diagonal_rows",
    )(core.astype(jnp.int32).reshape(1), half, other, up_edge, down_edge)
    low1 = lax.ppermute(up_edge, "gy", up)
    high1 = lax.ppermute(down_edge, "gy", down)

    cells = by * X * columns * 128

    def cost(operations):
        return pl.CostEstimate(
            flops=operations * cells, bytes_accessed=16 * cells, transcendentals=0
        )

    inner = pl.pallas_call(
        functools.partial(inner_kernel, grid),
        out_shape=tuple(vector(h) for h in (HALO, 4, 3, 2, HALO)),
        in_specs=[vmem()] * 2,
        out_specs=(vmem(),) * 5,
        compiler_params=params(),
        cost_estimate=cost(32),
        name="inner_steps",
    )(here(blocks), here(diagonal))
    ends = jnp.stack([gy == 0, gy == ny - 1, mine, core]).astype(jnp.int32)
    vectors = [here(value) for value in (inner[0], diagonal) + tuple(inner[1:])]
    c0, diagonal, d0, c1, d1, c2, up_edge, down_edge = pl.pallas_call(
        functools.partial(first_kernel, by),
        out_shape=tuple(vector(h) for h in (HALO, DIAGONAL_HALO, 4, 3, 2, HALO))
        + (edge(HALO), edge(HALO)),
        in_specs=[smem()] + [vmem()] * 8,
        out_specs=(vmem(),) * 8,
        input_output_aliases={i + 1: i for i in range(6)},
        compiler_params=params(),
        name="first_steps",
    )(ends, *vectors, low1, high1)
    low2 = lax.ppermute(up_edge, "gy", up)
    high2 = lax.ppermute(down_edge, "gy", down)
    d2, moments = pl.pallas_call(
        functools.partial(middle_kernel, by),
        out_shape=(vector(4), f32(8, 128)),
        in_specs=[vmem()] * 4,
        out_specs=(vmem(),) * 2,
        compiler_params=params(),
        cost_estimate=cost(24),
        name="middle_step",
    )(here(c0), here(c1), here(c2), here(diagonal))
    shares = [moments]
    for step in range(1, ny):
        shares.append(lax.ppermute(moments, "gy", [(i, (i + step) % ny) for i in range(ny)]))

    c3, d3, c4 = pl.pallas_call(
        functools.partial(second_inner_kernel, by),
        out_shape=tuple(vector(h) for h in (3, 2, 1)),
        in_specs=[vmem()] * 3,
        out_specs=(vmem(),) * 3,
        compiler_params=params(),
        cost_estimate=cost(30),
        name="second_inner_steps",
    )(here(diagonal), here(c2), here(d2))
    vectors = [here(value) for value in (diagonal, c2, d2, c3, d3, c4)]
    c2, d2, c3, d3, c4 = pl.pallas_call(
        functools.partial(third_kernel, by),
        out_shape=tuple(vector(h) for h in (HALO, 4, 3, 2, 1)),
        in_specs=[smem()] + [vmem()] * 8,
        out_specs=(vmem(),) * 5,
        input_output_aliases={i + 2: i for i in range(5)},
        compiler_params=params(),
        cost_estimate=cost(20),
        name="third_steps",
    )(ends, *vectors, low2, high2)
    inverse_count = 1.0 / (ny * cells)
    vectors = [here(value) for value in (c0, diagonal, d0, c1, d1, c2, d2, c3, d3, c4)]
    if group > count:
        cotangents = jnp.where(place < count, cotangents, 0.0)
    blocks = f32(group // 2, per, rows, 128)

    def last_step(flip):
        return pl.pallas_call(
            functools.partial(last_kernel, grid, inverse_count, flip),
            out_shape=blocks,
            in_specs=[smem(), smem()] + [vmem()] * (10 + ny),
            out_specs=vmem(),
            compiler_params=params(),
            cost_estimate=cost(20),
            name="last_step_given" if flip else "last_step_kept",
        )(ends, cotangents, *vectors, *shares)

    got = lax.ppermute(last_step(True), "core", swap)
    parts = pl.pallas_call(
        add_kernel,
        out_shape=blocks,
        in_specs=[vmem()] * 2,
        out_specs=vmem(),
        compiler_params=params(),
        name="add_cores",
    )(last_step(False), got)
    parts = lax.all_to_all(parts, ("chip", "gz"), 0, 0, tiled=True)
    return pl.pallas_call(
        functools.partial(sum_kernel, grid),
        out_shape=f32(bx, by, bz),
        in_specs=[vmem()],
        out_specs=vmem(),
        compiler_params=params(),
        name="sum_chips",
    )(parts)


def solution(mesh):
    nx, ny, nz = (mesh.shape[axis] for axis in ("gx", "gy", "gz"))
    devices = mesh.devices.reshape(nx // 2, 2, ny, nz)
    split = jax.sharding.Mesh(devices, ("chip", "core", "gy", "gz"))
    gx = ("chip", "core")
    return jax.shard_map(
        body,
        mesh=split,
        in_specs=(P(None, gx, "gy", "gz"), P(gx, "gy", "gz"), P()),
        out_specs=P(gx, "gy", "gz"),
        check_vma=False,
    )
```

```python
import functools

import jax
import jax.numpy as jnp
from jax import lax
from jax.experimental import pallas as pl
from jax.experimental.pallas import tpu as pltpu
from jax.sharding import PartitionSpec as P

EPSILON = 1e-06
SHIFT = 64.0
HALO = 5
DIAGONAL_HALO = 4
PAD = 8
MIB = 1024 * 1024


def loss_of_moments(moments, weights):
    m0, m1, m2, m3, m4, m5 = moments
    norm = m0 + EPSILON
    alpha1 = (m1 + SHIFT * m0) / norm
    e1 = SHIFT - alpha1
    rest1 = jnp.maximum(m2 + 2.0 * e1 * m1 + e1 * e1 * m0, 0.0)
    beta1_square = rest1 / norm + EPSILON
    beta1 = jnp.sqrt(beta1_square)
    scale = 1.0 / (norm * beta1_square)
    alpha2 = scale * (m3 + 2.0 * e1 * m2 + e1 * e1 * m1 + SHIFT * rest1) - (m1 + e1 * m0) / norm
    e2 = SHIFT - alpha2
    f1 = e1 + e2
    f0 = e1 * e2 - beta1_square
    g = f1 * f1 + 2.0 * f0
    rest2 = jnp.maximum(m4 + 2.0 * f1 * m3 + g * m2 + 2.0 * f1 * f0 * m1 + f0 * f0 * m0, 0.0)
    beta2_square = scale * rest2 + EPSILON
    beta2 = jnp.sqrt(beta2_square)
    image2 = m5 + 2.0 * f1 * m4 + g * m3 + 2.0 * f1 * f0 * m2 + f0 * f0 * m1
    cross = m3 + f1 * m2 + f0 * m1 + e1 * (m2 + f1 * m1 + f0 * m0)
    alpha3 = scale * ((image2 + SHIFT * rest2) / beta2_square - cross)
    return (
        weights[0] * alpha1
        + weights[1] * alpha2
        + weights[2] * alpha3
        + weights[3] * beta1
        + weights[4] * beta2
    )


class Field:
    def __init__(self, ref, halo):
        self.ref = ref
        self.halo = halo
        self.columns, self.rows, self.pitch, _ = ref.shape
        self.cells = self.pitch - 2 * PAD

    def load(self, column, row, x):
        return self.ref[column, row + self.halo, pl.ds(PAD + x, 8), :]

    def store(self, column, row, x, value):
        self.ref[column, row + self.halo, pl.ds(PAD + x, 8), :] = value

    def clear_pads(self):
        zero = jnp.zeros((8, 128), jnp.float32)

        def body(at, carry):
            for column in range(self.columns):
                self.ref[column, at, pl.ds(0, PAD), :] = zero
                self.ref[column, at, pl.ds(PAD + self.cells, PAD), :] = zero
            return carry

        lax.fori_loop(0, self.rows, body, 0)

    def clear_row(self, row):
        zero = jnp.zeros((8, 128), jnp.float32)
        for column in range(self.columns):
            for x in range(0, self.cells, 8):
                self.store(column, row, x, zero)


def lane_masks():
    lane = lax.broadcasted_iota(jnp.int32, (8, 128), 1)
    return lane == 0, lane == 127


def stencil_block(source, diagonal, row, rows, x, masks):
    columns = range(source.columns)
    centre = {(r, c): source.load(c, row + r, x) for r in range(-1, rows + 1) for c in columns}
    results = []
    for r in range(rows):
        after = [pltpu.roll(centre[r, c], 1, 1) for c in columns]
        before = [pltpu.roll(centre[r, c], 127, 1) for c in columns]
        for c in columns:
            low = after[c - 1] if c else 0.0
            high = before[c + 1] if c + 1 < source.columns else 0.0
            total = jnp.where(masks[0], low, after[c]) + jnp.where(masks[1], high, before[c])
            total = total + (source.load(c, row + r, x - 1) + source.load(c, row + r, x + 1))
            total = total + (centre[r - 1, c] + centre[r + 1, c])
            value = diagonal.load(c, row + r, x) * centre[r, c] - total
            results.append((c, row + r, value))
    return results


def apply_block(target, source, diagonal, row, rows, minus, masks):
    for x in range(0, source.cells, 8):
        results = stencil_block(source, diagonal, row, rows, x, masks)
        if minus is not None:
            results = [(c, r, value - SHIFT * minus.load(c, r, x)) for c, r, value in results]
        for c, r, value in results:
            target.store(c, r, x, value)


def apply_rows(target, source, diagonal, first, count, minus=None, block=4):
    masks = lane_masks()

    def body(step, carry):
        apply_block(target, source, diagonal, step * block + first, block, minus, masks)
        return carry

    lax.fori_loop(0, count // block, body, 0)
    if count % block:
        start = first + count - count % block
        apply_block(target, source, diagonal, start, count % block, minus, masks)


def apply_strips(spot_ref, own, target, source, diagonal, halo, size, minus=None):
    masks = lane_masks()

    def body(step, carry):
        row = step * (own - size + 2 * halo) - halo
        apply_block(target, source, diagonal, row, size, minus, masks)
        return carry

    lax.fori_loop(0, 2, body, 0)
    clear_outside(spot_ref, own, target)


def clear_outside(spot_ref, own, field):
    @pl.when(spot_ref[0] == 1)
    def _():
        field.clear_row(-1)

    @pl.when(spot_ref[1] == 1)
    def _():
        field.clear_row(own)


def split_chip(grid, chip):
    nz = grid[1]
    return lax.div(chip, nz), lax.rem(chip, nz)


def pack_kappa_kernel(kappa_ref, out_ref, sem):
    copies = []
    for column in range(out_ref.shape[0]):
        part = kappa_ref.at[:, pl.ds(column * 128, 128)]
        copies.append(pltpu.make_async_copy(part, out_ref.at[column], sem.at[column]))
    for copy in copies:
        copy.start()
    for copy in copies:
        copy.wait()


def pack_probes_kernel(grid, count, spot_ref, probes_ref, *rest):
    nx, nz, bx, by, bz = grid
    rows = bx * by
    outs, sem = rest[:-1], rest[-1]
    copies = []
    for k, out in enumerate(outs):
        x, z = split_chip(grid, spot_ref[4] ^ k)
        for core in range(2):
            start = pl.multiple_of(lax.rem((2 * x + core) * nz + z, count) * rows, rows)
            for column in range(bz // 128):
                part = probes_ref.at[pl.ds(start, rows), pl.ds(column * 128, 128)]
                copies.append(
                    pltpu.make_async_copy(part, out.at[core, column], sem.at[k, core, column])
                )
    for copy in copies:
        copy.start()
    for copy in copies:
        copy.wait()


def stack_kernel(*refs):
    for k, ref in enumerate(refs[:-1]):
        refs[-1][k] = ref[...]


def sort_probes_kernel(spot_ref, *refs):
    parts, mine_ref, give_ref = refs[:-2], refs[-2], refs[-1]
    core = spot_ref[3]
    for k, part in enumerate(parts):
        mine_ref[k] = part[core]
        give_ref[k] = part[1 - core]


def block_rows(grid, spot_ref, mine_ref, other_ref, rows):
    nx, nz, bx, by, bz = grid
    per = bz // 128
    core = spot_ref[3]
    for k in range(nx // 2 * nz):
        x, z = split_chip(grid, spot_ref[4] ^ k)
        for ref, side in ((mine_ref, core), (other_ref, 1 - core)):
            for column in range(per):
                values = [ref[k, column, pl.ds(y, bx, stride=by), :] for y in rows]
                yield (2 * x + side) * bx, z * per + column, values


def store_own(field, x, z, values):
    for y, value in enumerate(values):
        at = pl.ds(pl.multiple_of(PAD + x, 8), 8)
        field.ref[z, y + field.halo, at, :] = value


def store_edges(up_ref, down_ref, x, z, first, last):
    at = pl.ds(pl.multiple_of(x, 8), 8)
    for y, value in enumerate(first):
        down_ref[z, y, at, :] = value
    for y, value in enumerate(last):
        up_ref[z, y, at, :] = value


def edge_kernel(grid, spot_ref, mine_ref, other_ref, up_ref, down_ref):
    by = grid[3]
    rows = list(range(HALO)) + list(range(by - HALO, by))
    for x, z, values in block_rows(grid, spot_ref, mine_ref, other_ref, rows):
        store_edges(up_ref, down_ref, x, z, values[:HALO], values[HALO:])


def diagonal_kernel(grid, spot_ref, mine_ref, other_ref, own_ref, up_ref, down_ref):
    own = Field(own_ref, DIAGONAL_HALO)
    for x, z, values in block_rows(grid, spot_ref, mine_ref, other_ref, range(grid[3])):
        values = [6.0 + value for value in values]
        store_own(own, x, z, values)
        store_edges(up_ref, down_ref, x, z, values[:DIAGONAL_HALO], values[-DIAGONAL_HALO:])


def fill_halo(field, own, low_ref, high_ref):
    for c in range(field.columns):
        for y in range(field.halo):
            for x in range(0, field.cells, 8):
                field.store(c, y - field.halo, x, low_ref[c, y, pl.ds(x, 8), :])
                field.store(c, own + y, x, high_ref[c, y, pl.ds(x, 8), :])


def inner_kernel(
    grid, spot_ref, mine_ref, other_ref, diagonal_ref, c0_ref, d0_ref, c1_ref, d1_ref, c2_ref
):
    own = grid[3]
    c0 = Field(c0_ref, HALO)
    diagonal = Field(diagonal_ref, DIAGONAL_HALO)
    d0 = Field(d0_ref, 4)
    c1 = Field(c1_ref, 3)
    d1 = Field(d1_ref, 2)
    c2 = Field(c2_ref, HALO)
    for field in (c0, d0, c1, d1, c2):
        field.clear_pads()
    for x, z, values in block_rows(grid, spot_ref, mine_ref, other_ref, range(own)):
        store_own(c0, x, z, values)
    apply_rows(d0, c0, diagonal, 1, own - 2)
    apply_rows(c1, d0, diagonal, 2, own - 4, c0)
    apply_rows(d1, c1, diagonal, 3, own - 6)
    apply_rows(c2, d1, diagonal, 4, own - 8, c1)


def first_kernel(
    own,
    spot_ref, c0_in, diagonal_in, d0_in, c1_in, d1_in, c2_in,
    low_ref, high_ref, low_diagonal_ref, high_diagonal_ref,
    c0_ref, diagonal_ref, d0_ref, c1_ref, d1_ref, c2_ref, up_ref, down_ref,
):
    c0 = Field(c0_ref, HALO)
    diagonal = Field(diagonal_ref, DIAGONAL_HALO)
    d0 = Field(d0_ref, 4)
    c1 = Field(c1_ref, 3)
    d1 = Field(d1_ref, 2)
    c2 = Field(c2_ref, HALO)
    fill_halo(c0, own, low_ref, high_ref)
    fill_halo(diagonal, own, low_diagonal_ref, high_diagonal_ref)
    strips = functools.partial(apply_strips, spot_ref, own)
    strips(d0, c0, diagonal, 4, HALO)
    strips(c1, d0, diagonal, 3, HALO, c0)
    strips(d1, c1, diagonal, 2, HALO)
    strips(c2, d1, diagonal, 1, HALO, c1)
    for c in range(c2.columns):
        for y in range(HALO):
            for x in range(0, c2.cells, 8):
                down_ref[c, y, pl.ds(x, 8), :] = c2.load(c, y, x)
                up_ref[c, y, pl.ds(x, 8), :] = c2.load(c, own - HALO + y, x)


def middle_kernel(own, c0_ref, c1_ref, c2_ref, diagonal_ref, d2_ref, moments_ref):
    c0 = Field(c0_ref, HALO)
    diagonal = Field(diagonal_ref, DIAGONAL_HALO)
    c1 = Field(c1_ref, 3)
    c2 = Field(c2_ref, HALO)
    d2 = Field(d2_ref, 4)
    d2.clear_pads()
    apply_rows(d2, c2, diagonal, 0, own)

    def moment_row(row, sums):
        for x in range(0, c0.cells, 8):
            for c in range(c0.columns):
                a, b, e, d = (field.load(c, row, x) for field in (c0, c1, c2, d2))
                pairs = ((a, a), (a, b), (b, b), (b, e), (e, e), (d, d))
                sums = tuple(total + u * v for total, (u, v) in zip(sums, pairs))
        return sums

    zero = jnp.zeros((8, 128), jnp.float32)
    sums = lax.fori_loop(0, own, moment_row, (zero,) * 6)
    sums = [jnp.sum(total, axis=0, keepdims=True) for total in sums]
    moments_ref[...] = jnp.concatenate(sums + [zero[:2]], axis=0)


def moment_slopes(inverse_count, probe, weights_ref, moment_refs):
    total = moment_refs[0][...]
    for ref in moment_refs[1:]:
        total = total + ref[...]
    total = jnp.sum(total, axis=1, keepdims=True) * inverse_count
    raw = [jnp.broadcast_to(total[k : k + 1], (8, 128)) for k in range(6)]
    moments = tuple(raw[:5]) + (raw[5] - SHIFT * raw[4],)
    weights = [weights_ref[k, probe] for k in range(5)]
    value, pullback = jax.vjp(lambda m: loss_of_moments(m, weights), moments)
    (slopes,) = pullback(jnp.full((8, 128), 2.0, jnp.float32))
    return [slope[0, 0] for slope in slopes]


def second_inner_kernel(own, diagonal_ref, c2_ref, d2_ref, c3_ref, d3_ref, c4_ref):
    diagonal = Field(diagonal_ref, DIAGONAL_HALO)
    c2 = Field(c2_ref, HALO)
    d2 = Field(d2_ref, 4)
    c3 = Field(c3_ref, 3)
    d3 = Field(d3_ref, 2)
    c4 = Field(c4_ref, 1)
    for field in (c3, d3, c4):
        field.clear_pads()
    apply_rows(c3, d2, diagonal, 1, own - 2, c2)
    apply_rows(d3, c3, diagonal, 2, own - 4)
    apply_rows(c4, d3, diagonal, 3, own - 6, c3)


def third_kernel(
    own,
    spot_ref, diagonal_ref, c2_in, d2_in, c3_in, d3_in, c4_in, low_ref, high_ref,
    c2_ref, d2_ref, c3_ref, d3_ref, c4_ref,
):
    diagonal = Field(diagonal_ref, DIAGONAL_HALO)
    c2 = Field(c2_ref, HALO)
    d2 = Field(d2_ref, 4)
    c3 = Field(c3_ref, 3)
    d3 = Field(d3_ref, 2)
    c4 = Field(c4_ref, 1)
    fill_halo(c2, own, low_ref, high_ref)
    strips = functools.partial(apply_strips, spot_ref, own)
    strips(d2, c2, diagonal, 4, 4)
    strips(c3, d2, diagonal, 3, 4, c2)
    strips(d3, c3, diagonal, 2, 4)
    strips(c4, d3, diagonal, 1, 4, c3)


def last_kernel(
    grid, inverse_count, flip,
    spot_ref, weights_ref, c0_ref, diagonal_ref, d0_ref, c1_ref, d1_ref,
    c2_ref, d2_ref, c3_ref, d3_ref, c4_ref, *rest,
):
    nx, nz, bx, by, bz = grid
    per = bz // 128
    moment_refs, out_ref = rest[:-1], rest[-1]
    c0 = Field(c0_ref, HALO)
    diagonal = Field(diagonal_ref, DIAGONAL_HALO)
    d0 = Field(d0_ref, 4)
    c1 = Field(c1_ref, 3)
    d1 = Field(d1_ref, 2)
    c2 = Field(c2_ref, HALO)
    d2 = Field(d2_ref, 4)
    c3 = Field(c3_ref, 3)
    d3 = Field(d3_ref, 2)
    c4 = Field(c4_ref, 1)
    slopes = moment_slopes(inverse_count, spot_ref[2], weights_ref, moment_refs)
    masks = lane_masks()
    block = 2

    def out_rows(core, step, carry):
        row = step * block
        for chip in range(nx // 2):
            x = (2 * chip + core) * bx
            results = []
            for z, at, d4 in stencil_block(c4, diagonal, row, block, x, masks):
                cs = [field.load(z, at, x) for field in (c0, c1, c2, c3, c4)]
                ds = [field.load(z, at, x) for field in (d0, d1, d2, d3)] + [d4]
                total = None
                for i in range(5):
                    inner = None
                    for j in range(5 - i):
                        term = slopes[i + j + 1] * ds[j]
                        inner = term if inner is None else inner + term
                    term = cs[i] * inner
                    total = term if total is None else total + term
                results.append((chip * nz + z // per, z % per, at, total))
            for place, column, at, total in results:
                out_ref[place, column, pl.ds(at, bx, stride=by), :] = total
        return carry

    for core in range(2):

        @pl.when(spot_ref[3] == (1 - core if flip else core))
        def _():
            lax.fori_loop(0, by // block, functools.partial(out_rows, core), 0)


def add_kernel(spot_ref, kept_ref, got_ref, *outs):
    for k, out in enumerate(outs):
        chip = spot_ref[4] ^ k
        out[...] = kept_ref[chip] + got_ref[chip]


def sum_kernel(grid, *refs):
    nx, nz, bx, by, bz = grid
    parts, out_ref = refs[:-1], refs[-1]
    for column in range(bz // 128):
        for x in range(bx):
            total = None
            for ref in parts:
                part = ref[column, pl.ds(x * by, by), :]
                total = part if total is None else total + part
            out_ref[x, :, pl.ds(column * 128, 128)] = total


def vmem():
    return pl.BlockSpec(memory_space=pltpu.VMEM)


def smem():
    return pl.BlockSpec(memory_space=pltpu.SMEM)


def hbm():
    return pl.BlockSpec(memory_space=pltpu.HBM)


def here(value):
    return pltpu.with_memory_space_constraint(value, pltpu.VMEM)


def there(value):
    return pltpu.with_memory_space_constraint(value, pltpu.HBM)


def f32(*shape):
    return jax.ShapeDtypeStruct(shape, jnp.float32)


def params():
    return pltpu.CompilerParams(vmem_limit_bytes=12 * MIB)


def body(probes, kappa2, cotangents):
    nx, ny, nz = (lax.axis_size(axis) for axis in (("chip", "core"), "gy", "gz"))
    count, bx, by, bz = probes.shape
    group = nx * nz
    assert group % count == 0 and nx % 2 == 0 and bx == 8 and bz == 256
    assert by % 8 == 0 and by >= HALO
    X = nx * bx
    columns = nz * bz // 128
    per = bz // 128
    rows = bx * by
    grid = (nx, nz, bx, by, bz)
    core, gy = lax.axis_index("core"), lax.axis_index("gy")
    place = (lax.axis_index("chip") * 2 + core) * nz + lax.axis_index("gz")
    mine = place % count
    up = [(i, i + 1) for i in range(ny - 1)]
    down = [(target, source) for source, target in up]
    swap = [(0, 1), (1, 0)]

    def edge(halo):
        return f32(columns, halo, X, 128)

    def padded(halo):
        return (columns, by + 2 * halo, X + 2 * PAD, 128)

    def vector(halo):
        return pltpu.VMEM(padded(halo), jnp.float32)

    chips = nx // 2 * nz
    assert chips & (chips - 1) == 0
    chip = lax.axis_index("chip") * nz + lax.axis_index("gz")
    spot = jnp.stack([gy == 0, gy == ny - 1, mine, core, chip]).astype(jnp.int32)

    def to_chip(value, k):
        pairs = [(i, i ^ k) for i in range(chips)]
        return lax.ppermute(value, ("chip", "gz"), pairs)

    def plain(kernel, name, out_shape, specs, *operands, **options):
        return pl.pallas_call(
            kernel,
            out_shape=out_shape,
            in_specs=specs,
            out_specs=(vmem(),) * len(out_shape) if isinstance(out_shape, tuple) else vmem(),
            compiler_params=params(),
            name=name,
            **options,
        )(*operands)

    dma = pltpu.SemaphoreType.DMA
    block = f32(per, rows, 128)
    stacked = f32(chips, per, rows, 128)
    kappa = plain(
        pack_kappa_kernel, "pack_kappa", block, [hbm()], there(kappa2.reshape(rows, bz)),
        scratch_shapes=[dma((per,))],
    )
    kappas = [kappa] + [to_chip(kappa, k) for k in range(1, chips)]
    packed = plain(
        functools.partial(pack_probes_kernel, grid, count), "pack_probes",
        (f32(2, per, rows, 128),) * chips, [smem(), hbm()],
        spot, there(probes.reshape(count * rows, bz)), scratch_shapes=[dma((chips, 2, per))],
    )
    probes = [packed[0]] + [to_chip(packed[k], k) for k in range(1, chips)]

    kappa = plain(stack_kernel, "stack_kappa", stacked, [vmem()] * chips, *kappas)
    other = lax.ppermute(kappa, "core", swap)
    diagonal, up_edge, down_edge = plain(
        functools.partial(diagonal_kernel, grid), "diagonal_rows",
        (vector(DIAGONAL_HALO), edge(DIAGONAL_HALO), edge(DIAGONAL_HALO)),
        [smem(), vmem(), vmem()], spot, kappa, other,
    )
    low_diagonal = lax.ppermute(up_edge, "gy", up)
    high_diagonal = lax.ppermute(down_edge, "gy", down)

    probe, give = plain(
        sort_probes_kernel, "sort_probes", (stacked, stacked),
        [smem()] + [vmem()] * chips, spot, *probes,
    )
    other = lax.ppermute(give, "core", swap)
    up_edge, down_edge = plain(
        functools.partial(edge_kernel, grid), "probe_edges", (edge(HALO), edge(HALO)),
        [smem(), vmem(), vmem()], spot, probe, other,
    )
    low1 = lax.ppermute(up_edge, "gy", up)
    high1 = lax.ppermute(down_edge, "gy", down)

    cells = by * X * columns * 128

    def cost(operations):
        return pl.CostEstimate(
            flops=operations * cells, bytes_accessed=16 * cells, transcendentals=0
        )

    inner = pl.pallas_call(
        functools.partial(inner_kernel, grid),
        out_shape=tuple(vector(h) for h in (HALO, 4, 3, 2, HALO)),
        in_specs=[smem()] + [vmem()] * 3,
        out_specs=(vmem(),) * 5,
        compiler_params=params(),
        cost_estimate=cost(32),
        name="inner_steps",
    )(spot, probe, other, here(diagonal))
    vectors = [here(value) for value in (inner[0], diagonal) + tuple(inner[1:])]
    c0, diagonal, d0, c1, d1, c2, up_edge, down_edge = pl.pallas_call(
        functools.partial(first_kernel, by),
        out_shape=tuple(vector(h) for h in (HALO, DIAGONAL_HALO, 4, 3, 2, HALO))
        + (edge(HALO), edge(HALO)),
        in_specs=[smem()] + [vmem()] * 10,
        out_specs=(vmem(),) * 8,
        input_output_aliases={i + 1: i for i in range(6)},
        compiler_params=params(),
        name="first_steps",
    )(spot, *vectors, low1, high1, low_diagonal, high_diagonal)
    low2 = lax.ppermute(up_edge, "gy", up)
    high2 = lax.ppermute(down_edge, "gy", down)
    d2, moments = pl.pallas_call(
        functools.partial(middle_kernel, by),
        out_shape=(vector(4), f32(8, 128)),
        in_specs=[vmem()] * 4,
        out_specs=(vmem(),) * 2,
        compiler_params=params(),
        cost_estimate=cost(24),
        name="middle_step",
    )(here(c0), here(c1), here(c2), here(diagonal))
    shares = [moments]
    for step in range(1, ny):
        shares.append(lax.ppermute(moments, "gy", [(i, (i + step) % ny) for i in range(ny)]))

    c3, d3, c4 = pl.pallas_call(
        functools.partial(second_inner_kernel, by),
        out_shape=tuple(vector(h) for h in (3, 2, 1)),
        in_specs=[vmem()] * 3,
        out_specs=(vmem(),) * 3,
        compiler_params=params(),
        cost_estimate=cost(30),
        name="second_inner_steps",
    )(here(diagonal), here(c2), here(d2))
    vectors = [here(value) for value in (diagonal, c2, d2, c3, d3, c4)]
    c2, d2, c3, d3, c4 = pl.pallas_call(
        functools.partial(third_kernel, by),
        out_shape=tuple(vector(h) for h in (HALO, 4, 3, 2, 1)),
        in_specs=[smem()] + [vmem()] * 8,
        out_specs=(vmem(),) * 5,
        input_output_aliases={i + 2: i for i in range(5)},
        compiler_params=params(),
        cost_estimate=cost(20),
        name="third_steps",
    )(spot, *vectors, low2, high2)
    inverse_count = 1.0 / (ny * cells)
    vectors = [here(value) for value in (c0, diagonal, d0, c1, d1, c2, d2, c3, d3, c4)]
    if group > count:
        cotangents = jnp.where(place < count, cotangents, 0.0)

    def last_step(flip):
        return pl.pallas_call(
            functools.partial(last_kernel, grid, inverse_count, flip),
            out_shape=stacked,
            in_specs=[smem(), smem()] + [vmem()] * (10 + ny),
            out_specs=vmem(),
            compiler_params=params(),
            cost_estimate=cost(20),
            name="last_step_given" if flip else "last_step_kept",
        )(spot, cotangents, *vectors, *shares)

    got = lax.ppermute(last_step(True), "core", swap)
    parts = plain(
        add_kernel, "add_cores", (block,) * chips, [smem(), vmem(), vmem()],
        spot, last_step(False), got,
    )
    parts = [parts[0]] + [to_chip(parts[k], k) for k in range(chips - 1, 0, -1)]
    return plain(
        functools.partial(sum_kernel, grid), "sum_chips", f32(bx, by, bz), [vmem()] * chips, *parts
    )


def solution(mesh):
    nx, ny, nz = (mesh.shape[axis] for axis in ("gx", "gy", "gz"))
    devices = mesh.devices.reshape(nx // 2, 2, ny, nz)
    split = jax.sharding.Mesh(devices, ("chip", "core", "gy", "gz"))
    gx = ("chip", "core")
    return jax.shard_map(
        body,
        mesh=split,
        in_specs=(P(None, gx, "gy", "gz"), P(gx, "gy", "gz"), P()),
        out_specs=P(gx, "gy", "gz"),
        check_vma=False,
    )
```

```python
import functools

import jax
import jax.numpy as jnp
from jax import lax
from jax.experimental import pallas as pl
from jax.experimental.pallas import tpu as pltpu
from jax.sharding import PartitionSpec as P

EPSILON = 1e-06
SHIFT = 64.0
HALO = 5
DIAGONAL_HALO = 4
PAD = 8
MIB = 1024 * 1024


def loss_of_moments(moments, weights):
    m0, m1, m2, m3, m4, m5 = moments
    norm = m0 + EPSILON
    alpha1 = (m1 + SHIFT * m0) / norm
    e1 = SHIFT - alpha1
    rest1 = jnp.maximum(m2 + 2.0 * e1 * m1 + e1 * e1 * m0, 0.0)
    beta1_square = rest1 / norm + EPSILON
    beta1 = jnp.sqrt(beta1_square)
    scale = 1.0 / (norm * beta1_square)
    alpha2 = scale * (m3 + 2.0 * e1 * m2 + e1 * e1 * m1 + SHIFT * rest1) - (m1 + e1 * m0) / norm
    e2 = SHIFT - alpha2
    f1 = e1 + e2
    f0 = e1 * e2 - beta1_square
    g = f1 * f1 + 2.0 * f0
    rest2 = jnp.maximum(m4 + 2.0 * f1 * m3 + g * m2 + 2.0 * f1 * f0 * m1 + f0 * f0 * m0, 0.0)
    beta2_square = scale * rest2 + EPSILON
    beta2 = jnp.sqrt(beta2_square)
    image2 = m5 + 2.0 * f1 * m4 + g * m3 + 2.0 * f1 * f0 * m2 + f0 * f0 * m1
    cross = m3 + f1 * m2 + f0 * m1 + e1 * (m2 + f1 * m1 + f0 * m0)
    alpha3 = scale * ((image2 + SHIFT * rest2) / beta2_square - cross)
    return (
        weights[0] * alpha1
        + weights[1] * alpha2
        + weights[2] * alpha3
        + weights[3] * beta1
        + weights[4] * beta2
    )


class Field:
    def __init__(self, ref, halo):
        self.ref = ref
        self.halo = halo
        self.columns, self.rows, self.pitch, _ = ref.shape
        self.cells = self.pitch - 2 * PAD

    def load(self, column, row, x):
        return self.ref[column, row + self.halo, pl.ds(PAD + x, 8), :]

    def store(self, column, row, x, value):
        self.ref[column, row + self.halo, pl.ds(PAD + x, 8), :] = value

    def clear_pads(self):
        zero = jnp.zeros((8, 128), jnp.float32)

        def body(at, carry):
            for column in range(self.columns):
                self.ref[column, at, pl.ds(0, PAD), :] = zero
                self.ref[column, at, pl.ds(PAD + self.cells, PAD), :] = zero
            return carry

        lax.fori_loop(0, self.rows, body, 0)

    def clear_row(self, row):
        zero = jnp.zeros((8, 128), jnp.float32)
        for column in range(self.columns):
            for x in range(0, self.cells, 8):
                self.store(column, row, x, zero)


def lane_masks():
    lane = lax.broadcasted_iota(jnp.int32, (8, 128), 1)
    return lane == 0, lane == 127


def stencil_block(source, diagonal, row, rows, x, masks):
    columns = range(source.columns)
    centre = {(r, c): source.load(c, row + r, x) for r in range(-1, rows + 1) for c in columns}
    results = []
    for r in range(rows):
        after = [pltpu.roll(centre[r, c], 1, 1) for c in columns]
        before = [pltpu.roll(centre[r, c], 127, 1) for c in columns]
        for c in columns:
            low = after[c - 1] if c else 0.0
            high = before[c + 1] if c + 1 < source.columns else 0.0
            total = jnp.where(masks[0], low, after[c]) + jnp.where(masks[1], high, before[c])
            total = total + (source.load(c, row + r, x - 1) + source.load(c, row + r, x + 1))
            total = total + (centre[r - 1, c] + centre[r + 1, c])
            value = diagonal.load(c, row + r, x) * centre[r, c] - total
            results.append((c, row + r, value))
    return results


def apply_block(target, source, diagonal, row, rows, minus, masks):
    for x in range(0, source.cells, 8):
        results = stencil_block(source, diagonal, row, rows, x, masks)
        if minus is not None:
            results = [(c, r, value - SHIFT * minus.load(c, r, x)) for c, r, value in results]
        for c, r, value in results:
            target.store(c, r, x, value)


def apply_rows(target, source, diagonal, first, count, minus=None, block=4):
    masks = lane_masks()

    def body(step, carry):
        apply_block(target, source, diagonal, step * block + first, block, minus, masks)
        return carry

    lax.fori_loop(0, count // block, body, 0)
    if count % block:
        start = first + count - count % block
        apply_block(target, source, diagonal, start, count % block, minus, masks)


def apply_strips(spot_ref, own, target, source, diagonal, halo, size, minus=None):
    masks = lane_masks()

    def body(step, carry):
        row = step * (own - size + 2 * halo) - halo
        apply_block(target, source, diagonal, row, size, minus, masks)
        return carry

    lax.fori_loop(0, 2, body, 0)
    clear_outside(spot_ref, own, target)


def clear_outside(spot_ref, own, field):
    @pl.when(spot_ref[0] == 1)
    def _():
        field.clear_row(-1)

    @pl.when(spot_ref[1] == 1)
    def _():
        field.clear_row(own)


def split_chip(grid, chip):
    nz = grid[1]
    return lax.div(chip, nz), lax.rem(chip, nz)


def pack_kappa_kernel(kappa_ref, out_ref, sem):
    copies = []
    for column in range(out_ref.shape[0]):
        part = kappa_ref.at[:, pl.ds(column * 128, 128)]
        copies.append(pltpu.make_async_copy(part, out_ref.at[column], sem.at[column]))
    for copy in copies:
        copy.start()
    for copy in copies:
        copy.wait()


def pack_probes_kernel(grid, count, spot_ref, probes_ref, *rest):
    nx, nz, bx, by, bz = grid
    rows = bx * by
    outs, sem = rest[:-1], rest[-1]
    copies = []
    for k, out in enumerate(outs):
        x, z = split_chip(grid, spot_ref[4] ^ k)
        for core in range(2):
            start = pl.multiple_of(lax.rem((2 * x + core) * nz + z, count) * rows, rows)
            for column in range(bz // 128):
                part = probes_ref.at[pl.ds(start, rows), pl.ds(column * 128, 128)]
                copies.append(
                    pltpu.make_async_copy(part, out.at[core, column], sem.at[k, core, column])
                )
    for copy in copies:
        copy.start()
    for copy in copies:
        copy.wait()


def stack_kernel(*refs):
    for k, ref in enumerate(refs[:-1]):
        refs[-1][k] = ref[...]


def sort_probes_kernel(spot_ref, *refs):
    parts, mine_ref, give_ref = refs[:-2], refs[-2], refs[-1]
    core = spot_ref[3]
    for k, part in enumerate(parts):
        mine_ref[k] = part[core]
        give_ref[k] = part[1 - core]


def block_rows(grid, spot_ref, mine_ref, other_ref, rows):
    nx, nz, bx, by, bz = grid
    per = bz // 128
    core = spot_ref[3]
    for k in range(nx // 2 * nz):
        x, z = split_chip(grid, spot_ref[4] ^ k)
        for ref, side in ((mine_ref, core), (other_ref, 1 - core)):
            for column in range(per):
                values = [ref[k, column, pl.ds(y, bx, stride=by), :] for y in rows]
                yield (2 * x + side) * bx, z * per + column, values


def store_own(field, x, z, values):
    for y, value in enumerate(values):
        at = pl.ds(pl.multiple_of(PAD + x, 8), 8)
        field.ref[z, y + field.halo, at, :] = value


def store_edges(spot_ref, even_ref, odd_ref, x, z, first, last):
    at = pl.ds(pl.multiple_of(x, 8), 8)
    odd = spot_ref[5] == 1
    for y, (below, above) in enumerate(zip(first, last)):
        even_ref[z, y, at, :] = jnp.where(odd, below, above)
        odd_ref[z, y, at, :] = jnp.where(odd, above, below)


def edge_kernel(grid, spot_ref, mine_ref, other_ref, even_ref, odd_ref):
    by = grid[3]
    rows = list(range(HALO)) + list(range(by - HALO, by))
    for x, z, values in block_rows(grid, spot_ref, mine_ref, other_ref, rows):
        store_edges(spot_ref, even_ref, odd_ref, x, z, values[:HALO], values[HALO:])


def diagonal_kernel(grid, spot_ref, mine_ref, other_ref, own_ref, even_ref, odd_ref):
    own = Field(own_ref, DIAGONAL_HALO)
    for x, z, values in block_rows(grid, spot_ref, mine_ref, other_ref, range(grid[3])):
        values = [6.0 + value for value in values]
        store_own(own, x, z, values)
        first, last = values[:DIAGONAL_HALO], values[-DIAGONAL_HALO:]
        store_edges(spot_ref, even_ref, odd_ref, x, z, first, last)


def fill_halo(spot_ref, field, own, even_ref, odd_ref):
    odd = spot_ref[5] == 1
    for c in range(field.columns):
        for y in range(field.halo):
            for x in range(0, field.cells, 8):
                even, other = even_ref[c, y, pl.ds(x, 8), :], odd_ref[c, y, pl.ds(x, 8), :]
                field.store(c, y - field.halo, x, jnp.where(odd, even, other))
                field.store(c, own + y, x, jnp.where(odd, other, even))


def inner_kernel(
    grid, spot_ref, mine_ref, other_ref, diagonal_ref, c0_ref, d0_ref, c1_ref, d1_ref, c2_ref
):
    own = grid[3]
    c0 = Field(c0_ref, HALO)
    diagonal = Field(diagonal_ref, DIAGONAL_HALO)
    d0 = Field(d0_ref, 4)
    c1 = Field(c1_ref, 3)
    d1 = Field(d1_ref, 2)
    c2 = Field(c2_ref, HALO)
    for field in (c0, d0, c1, d1, c2):
        field.clear_pads()
    for x, z, values in block_rows(grid, spot_ref, mine_ref, other_ref, range(own)):
        store_own(c0, x, z, values)
    apply_rows(d0, c0, diagonal, 1, own - 2)
    apply_rows(c1, d0, diagonal, 2, own - 4, c0)
    apply_rows(d1, c1, diagonal, 3, own - 6)
    apply_rows(c2, d1, diagonal, 4, own - 8, c1)


def first_kernel(
    own,
    spot_ref, c0_in, diagonal_in, d0_in, c1_in, d1_in, c2_in,
    even_ref, odd_ref, even_diagonal_ref, odd_diagonal_ref,
    c0_ref, diagonal_ref, d0_ref, c1_ref, d1_ref, c2_ref, even_out, odd_out,
):
    c0 = Field(c0_ref, HALO)
    diagonal = Field(diagonal_ref, DIAGONAL_HALO)
    d0 = Field(d0_ref, 4)
    c1 = Field(c1_ref, 3)
    d1 = Field(d1_ref, 2)
    c2 = Field(c2_ref, HALO)
    fill_halo(spot_ref, c0, own, even_ref, odd_ref)
    fill_halo(spot_ref, diagonal, own, even_diagonal_ref, odd_diagonal_ref)
    strips = functools.partial(apply_strips, spot_ref, own)
    strips(d0, c0, diagonal, 4, HALO)
    strips(c1, d0, diagonal, 3, HALO, c0)
    strips(d1, c1, diagonal, 2, HALO)
    strips(c2, d1, diagonal, 1, HALO, c1)
    for c in range(c2.columns):
        for x in range(0, c2.cells, 8):
            first = [c2.load(c, y, x) for y in range(HALO)]
            last = [c2.load(c, own - HALO + y, x) for y in range(HALO)]
            store_edges(spot_ref, even_out, odd_out, x, c, first, last)


def middle_kernel(own, c0_ref, c1_ref, c2_ref, diagonal_ref, d2_ref, moments_ref):
    c0 = Field(c0_ref, HALO)
    diagonal = Field(diagonal_ref, DIAGONAL_HALO)
    c1 = Field(c1_ref, 3)
    c2 = Field(c2_ref, HALO)
    d2 = Field(d2_ref, 4)
    d2.clear_pads()
    apply_rows(d2, c2, diagonal, 0, own)

    def moment_row(row, sums):
        for x in range(0, c0.cells, 8):
            for c in range(c0.columns):
                a, b, e, d = (field.load(c, row, x) for field in (c0, c1, c2, d2))
                pairs = ((a, a), (a, b), (b, b), (b, e), (e, e), (d, d))
                sums = tuple(total + u * v for total, (u, v) in zip(sums, pairs))
        return sums

    zero = jnp.zeros((8, 128), jnp.float32)
    sums = lax.fori_loop(0, own, moment_row, (zero,) * 6)
    sums = [jnp.sum(total, axis=0, keepdims=True) for total in sums]
    moments_ref[...] = jnp.concatenate(sums + [zero[:2]], axis=0)


def moment_slopes(inverse_count, probe, weights_ref, moment_refs):
    total = moment_refs[0][...]
    for ref in moment_refs[1:]:
        total = total + ref[...]
    total = jnp.sum(total, axis=1, keepdims=True) * inverse_count
    raw = [jnp.broadcast_to(total[k : k + 1], (8, 128)) for k in range(6)]
    moments = tuple(raw[:5]) + (raw[5] - SHIFT * raw[4],)
    weights = [weights_ref[k, probe] for k in range(5)]
    value, pullback = jax.vjp(lambda m: loss_of_moments(m, weights), moments)
    (slopes,) = pullback(jnp.full((8, 128), 2.0, jnp.float32))
    return [slope[0, 0] for slope in slopes]


def second_inner_kernel(own, diagonal_ref, c2_ref, d2_ref, c3_ref, d3_ref, c4_ref):
    diagonal = Field(diagonal_ref, DIAGONAL_HALO)
    c2 = Field(c2_ref, HALO)
    d2 = Field(d2_ref, 4)
    c3 = Field(c3_ref, 3)
    d3 = Field(d3_ref, 2)
    c4 = Field(c4_ref, 1)
    for field in (c3, d3, c4):
        field.clear_pads()
    apply_rows(c3, d2, diagonal, 1, own - 2, c2)
    apply_rows(d3, c3, diagonal, 2, own - 4)
    apply_rows(c4, d3, diagonal, 3, own - 6, c3)


def third_kernel(
    own,
    spot_ref, diagonal_ref, c2_in, d2_in, c3_in, d3_in, c4_in, even_ref, odd_ref,
    c2_ref, d2_ref, c3_ref, d3_ref, c4_ref,
):
    diagonal = Field(diagonal_ref, DIAGONAL_HALO)
    c2 = Field(c2_ref, HALO)
    d2 = Field(d2_ref, 4)
    c3 = Field(c3_ref, 3)
    d3 = Field(d3_ref, 2)
    c4 = Field(c4_ref, 1)
    fill_halo(spot_ref, c2, own, even_ref, odd_ref)
    strips = functools.partial(apply_strips, spot_ref, own)
    strips(d2, c2, diagonal, 4, 4)
    strips(c3, d2, diagonal, 3, 4, c2)
    strips(d3, c3, diagonal, 2, 4)
    strips(c4, d3, diagonal, 1, 4, c3)


def last_kernel(
    grid, inverse_count, flip,
    spot_ref, weights_ref, c0_ref, diagonal_ref, d0_ref, c1_ref, d1_ref,
    c2_ref, d2_ref, c3_ref, d3_ref, c4_ref, *rest,
):
    nx, nz, bx, by, bz = grid
    per = bz // 128
    moment_refs, out_ref = rest[:-1], rest[-1]
    c0 = Field(c0_ref, HALO)
    diagonal = Field(diagonal_ref, DIAGONAL_HALO)
    d0 = Field(d0_ref, 4)
    c1 = Field(c1_ref, 3)
    d1 = Field(d1_ref, 2)
    c2 = Field(c2_ref, HALO)
    d2 = Field(d2_ref, 4)
    c3 = Field(c3_ref, 3)
    d3 = Field(d3_ref, 2)
    c4 = Field(c4_ref, 1)
    slopes = moment_slopes(inverse_count, spot_ref[2], weights_ref, moment_refs)
    masks = lane_masks()
    block = 2

    def out_rows(core, step, carry):
        row = step * block
        for chip in range(nx // 2):
            x = (2 * chip + core) * bx
            results = []
            for z, at, d4 in stencil_block(c4, diagonal, row, block, x, masks):
                cs = [field.load(z, at, x) for field in (c0, c1, c2, c3, c4)]
                ds = [field.load(z, at, x) for field in (d0, d1, d2, d3)] + [d4]
                total = None
                for i in range(5):
                    inner = None
                    for j in range(5 - i):
                        term = slopes[i + j + 1] * ds[j]
                        inner = term if inner is None else inner + term
                    term = cs[i] * inner
                    total = term if total is None else total + term
                results.append((chip * nz + z // per, z % per, at, total))
            for place, column, at, total in results:
                out_ref[place, column, pl.ds(at, bx, stride=by), :] = total
        return carry

    for core in range(2):

        @pl.when(spot_ref[3] == (1 - core if flip else core))
        def _():
            lax.fori_loop(0, by // block, functools.partial(out_rows, core), 0)


def add_kernel(spot_ref, kept_ref, got_ref, *outs):
    for k, out in enumerate(outs):
        chip = spot_ref[4] ^ k
        out[...] = kept_ref[chip] + got_ref[chip]


def sum_kernel(grid, *refs):
    nx, nz, bx, by, bz = grid
    parts, out_ref = refs[:-1], refs[-1]
    for column in range(bz // 128):
        for x in range(bx):
            total = None
            for ref in parts:
                part = ref[column, pl.ds(x * by, by), :]
                total = part if total is None else total + part
            out_ref[x, :, pl.ds(column * 128, 128)] = total


def vmem():
    return pl.BlockSpec(memory_space=pltpu.VMEM)


def smem():
    return pl.BlockSpec(memory_space=pltpu.SMEM)


def hbm():
    return pl.BlockSpec(memory_space=pltpu.HBM)


def here(value):
    return pltpu.with_memory_space_constraint(value, pltpu.VMEM)


def there(value):
    return pltpu.with_memory_space_constraint(value, pltpu.HBM)


def f32(*shape):
    return jax.ShapeDtypeStruct(shape, jnp.float32)


def params():
    return pltpu.CompilerParams(vmem_limit_bytes=12 * MIB)


def body(probes, kappa2, cotangents):
    nx, ny, nz = (lax.axis_size(axis) for axis in (("chip", "core"), "gy", "gz"))
    count, bx, by, bz = probes.shape
    group = nx * nz
    assert group % count == 0 and nx % 2 == 0 and bx == 8 and bz == 256
    assert by % 8 == 0 and by >= HALO
    X = nx * bx
    columns = nz * bz // 128
    per = bz // 128
    rows = bx * by
    grid = (nx, nz, bx, by, bz)
    core, gy = lax.axis_index("core"), lax.axis_index("gy")
    place = (lax.axis_index("chip") * 2 + core) * nz + lax.axis_index("gz")
    mine = place % count
    assert ny & (ny - 1) == 0
    even = [(i, i ^ 1) for i in range(ny)]
    odd = [(i, i + 1 if i % 2 else i - 1) for i in range(1, ny - 1)]
    swap = [(0, 1), (1, 0)]

    def edge(halo):
        return f32(columns, halo, X, 128)

    def padded(halo):
        return (columns, by + 2 * halo, X + 2 * PAD, 128)

    def vector(halo):
        return pltpu.VMEM(padded(halo), jnp.float32)

    chips = nx // 2 * nz
    assert chips & (chips - 1) == 0
    chip = lax.axis_index("chip") * nz + lax.axis_index("gz")
    spot = jnp.stack([gy == 0, gy == ny - 1, mine, core, chip, gy % 2]).astype(jnp.int32)

    def to_chip(value, k):
        pairs = [(i, i ^ k) for i in range(chips)]
        return lax.ppermute(value, ("chip", "gz"), pairs)

    def plain(kernel, name, out_shape, specs, *operands, **options):
        return pl.pallas_call(
            kernel,
            out_shape=out_shape,
            in_specs=specs,
            out_specs=(vmem(),) * len(out_shape) if isinstance(out_shape, tuple) else vmem(),
            compiler_params=params(),
            name=name,
            **options,
        )(*operands)

    dma = pltpu.SemaphoreType.DMA
    block = f32(per, rows, 128)
    stacked = f32(chips, per, rows, 128)
    kappa = plain(
        pack_kappa_kernel, "pack_kappa", block, [hbm()], there(kappa2.reshape(rows, bz)),
        scratch_shapes=[dma((per,))],
    )
    kappas = [kappa] + [to_chip(kappa, k) for k in range(1, chips)]
    packed = plain(
        functools.partial(pack_probes_kernel, grid, count), "pack_probes",
        (f32(2, per, rows, 128),) * chips, [smem(), hbm()],
        spot, there(probes.reshape(count * rows, bz)), scratch_shapes=[dma((chips, 2, per))],
    )
    probes = [packed[0]] + [to_chip(packed[k], k) for k in range(1, chips)]

    kappa = plain(stack_kernel, "stack_kappa", stacked, [vmem()] * chips, *kappas)
    other = lax.ppermute(kappa, "core", swap)
    diagonal, even_edge, odd_edge = plain(
        functools.partial(diagonal_kernel, grid), "diagonal_rows",
        (vector(DIAGONAL_HALO), edge(DIAGONAL_HALO), edge(DIAGONAL_HALO)),
        [smem(), vmem(), vmem()], spot, kappa, other,
    )
    even_diagonal = lax.ppermute(even_edge, "gy", even)
    odd_diagonal = lax.ppermute(odd_edge, "gy", odd)

    probe, give = plain(
        sort_probes_kernel, "sort_probes", (stacked, stacked),
        [smem()] + [vmem()] * chips, spot, *probes,
    )
    other = lax.ppermute(give, "core", swap)
    even_edge, odd_edge = plain(
        functools.partial(edge_kernel, grid), "probe_edges", (edge(HALO), edge(HALO)),
        [smem(), vmem(), vmem()], spot, probe, other,
    )
    even1 = lax.ppermute(even_edge, "gy", even)
    odd1 = lax.ppermute(odd_edge, "gy", odd)

    cells = by * X * columns * 128

    def cost(operations):
        return pl.CostEstimate(
            flops=operations * cells, bytes_accessed=16 * cells, transcendentals=0
        )

    inner = pl.pallas_call(
        functools.partial(inner_kernel, grid),
        out_shape=tuple(vector(h) for h in (HALO, 4, 3, 2, HALO)),
        in_specs=[smem()] + [vmem()] * 3,
        out_specs=(vmem(),) * 5,
        compiler_params=params(),
        cost_estimate=cost(32),
        name="inner_steps",
    )(spot, probe, other, here(diagonal))
    vectors = [here(value) for value in (inner[0], diagonal) + tuple(inner[1:])]
    c0, diagonal, d0, c1, d1, c2, even_edge, odd_edge = pl.pallas_call(
        functools.partial(first_kernel, by),
        out_shape=tuple(vector(h) for h in (HALO, DIAGONAL_HALO, 4, 3, 2, HALO))
        + (edge(HALO), edge(HALO)),
        in_specs=[smem()] + [vmem()] * 10,
        out_specs=(vmem(),) * 8,
        input_output_aliases={i + 1: i for i in range(6)},
        compiler_params=params(),
        name="first_steps",
    )(spot, *vectors, even1, odd1, even_diagonal, odd_diagonal)
    even2 = lax.ppermute(even_edge, "gy", even)
    odd2 = lax.ppermute(odd_edge, "gy", odd)
    d2, moments = pl.pallas_call(
        functools.partial(middle_kernel, by),
        out_shape=(vector(4), f32(8, 128)),
        in_specs=[vmem()] * 4,
        out_specs=(vmem(),) * 2,
        compiler_params=params(),
        cost_estimate=cost(24),
        name="middle_step",
    )(here(c0), here(c1), here(c2), here(diagonal))
    shares = [moments]
    for step in range(1, ny):
        shares.append(lax.ppermute(moments, "gy", [(i, i ^ step) for i in range(ny)]))

    c3, d3, c4 = pl.pallas_call(
        functools.partial(second_inner_kernel, by),
        out_shape=tuple(vector(h) for h in (3, 2, 1)),
        in_specs=[vmem()] * 3,
        out_specs=(vmem(),) * 3,
        compiler_params=params(),
        cost_estimate=cost(30),
        name="second_inner_steps",
    )(here(diagonal), here(c2), here(d2))
    vectors = [here(value) for value in (diagonal, c2, d2, c3, d3, c4)]
    c2, d2, c3, d3, c4 = pl.pallas_call(
        functools.partial(third_kernel, by),
        out_shape=tuple(vector(h) for h in (HALO, 4, 3, 2, 1)),
        in_specs=[smem()] + [vmem()] * 8,
        out_specs=(vmem(),) * 5,
        input_output_aliases={i + 2: i for i in range(5)},
        compiler_params=params(),
        cost_estimate=cost(20),
        name="third_steps",
    )(spot, *vectors, even2, odd2)
    inverse_count = 1.0 / (ny * cells)
    vectors = [here(value) for value in (c0, diagonal, d0, c1, d1, c2, d2, c3, d3, c4)]
    if group > count:
        cotangents = jnp.where(place < count, cotangents, 0.0)

    def last_step(flip):
        return pl.pallas_call(
            functools.partial(last_kernel, grid, inverse_count, flip),
            out_shape=stacked,
            in_specs=[smem(), smem()] + [vmem()] * (10 + ny),
            out_specs=vmem(),
            compiler_params=params(),
            cost_estimate=cost(20),
            name="last_step_given" if flip else "last_step_kept",
        )(spot, cotangents, *vectors, *shares)

    got = lax.ppermute(last_step(True), "core", swap)
    parts = plain(
        add_kernel, "add_cores", (block,) * chips, [smem(), vmem(), vmem()],
        spot, last_step(False), got,
    )
    parts = [parts[0]] + [to_chip(parts[k], k) for k in range(chips - 1, 0, -1)]
    return plain(
        functools.partial(sum_kernel, grid), "sum_chips", f32(bx, by, bz), [vmem()] * chips, *parts
    )


def solution(mesh):
    nx, ny, nz = (mesh.shape[axis] for axis in ("gx", "gy", "gz"))
    devices = mesh.devices.reshape(nx // 2, 2, ny, nz)
    split = jax.sharding.Mesh(devices, ("chip", "core", "gy", "gz"))
    gx = ("chip", "core")
    return jax.shard_map(
        body,
        mesh=split,
        in_specs=(P(None, gx, "gy", "gz"), P(gx, "gy", "gz"), P()),
        out_specs=P(gx, "gy", "gz"),
        check_vma=False,
    )
```

```python
import functools

import jax
import jax.numpy as jnp
from jax import lax
from jax.experimental import pallas as pl
from jax.experimental.pallas import tpu as pltpu
from jax.sharding import PartitionSpec as P

EPSILON = 1e-06
SHIFT = 64.0
HALO = 5
DIAGONAL_HALO = 4
PAD = 8
MIB = 1024 * 1024


def loss_of_moments(moments, weights):
    m0, m1, m2, m3, m4, m5 = moments
    norm = m0 + EPSILON
    alpha1 = (m1 + SHIFT * m0) / norm
    e1 = SHIFT - alpha1
    rest1 = jnp.maximum(m2 + 2.0 * e1 * m1 + e1 * e1 * m0, 0.0)
    beta1_square = rest1 / norm + EPSILON
    beta1 = jnp.sqrt(beta1_square)
    scale = 1.0 / (norm * beta1_square)
    alpha2 = scale * (m3 + 2.0 * e1 * m2 + e1 * e1 * m1 + SHIFT * rest1) - (m1 + e1 * m0) / norm
    e2 = SHIFT - alpha2
    f1 = e1 + e2
    f0 = e1 * e2 - beta1_square
    g = f1 * f1 + 2.0 * f0
    rest2 = jnp.maximum(m4 + 2.0 * f1 * m3 + g * m2 + 2.0 * f1 * f0 * m1 + f0 * f0 * m0, 0.0)
    beta2_square = scale * rest2 + EPSILON
    beta2 = jnp.sqrt(beta2_square)
    image2 = m5 + 2.0 * f1 * m4 + g * m3 + 2.0 * f1 * f0 * m2 + f0 * f0 * m1
    cross = m3 + f1 * m2 + f0 * m1 + e1 * (m2 + f1 * m1 + f0 * m0)
    alpha3 = scale * ((image2 + SHIFT * rest2) / beta2_square - cross)
    return (
        weights[0] * alpha1
        + weights[1] * alpha2
        + weights[2] * alpha3
        + weights[3] * beta1
        + weights[4] * beta2
    )


class Field:
    def __init__(self, ref, halo):
        self.ref = ref
        self.halo = halo
        self.columns, self.rows, self.pitch, _ = ref.shape
        self.cells = self.pitch - 2 * PAD

    def load(self, column, row, x):
        return self.ref[column, row + self.halo, pl.ds(PAD + x, 8), :]

    def store(self, column, row, x, value):
        self.ref[column, row + self.halo, pl.ds(PAD + x, 8), :] = value

    def clear_pads(self):
        zero = jnp.zeros((8, 128), jnp.float32)

        def body(at, carry):
            for column in range(self.columns):
                self.ref[column, at, pl.ds(0, PAD), :] = zero
                self.ref[column, at, pl.ds(PAD + self.cells, PAD), :] = zero
            return carry

        lax.fori_loop(0, self.rows, body, 0)

    def clear_row(self, row):
        zero = jnp.zeros((8, 128), jnp.float32)
        for column in range(self.columns):
            for x in range(0, self.cells, 8):
                self.store(column, row, x, zero)


def lane_masks():
    lane = lax.broadcasted_iota(jnp.int32, (8, 128), 1)
    return lane == 0, lane == 127


def stencil_block(source, diagonal, row, rows, x, masks):
    columns = range(source.columns)
    centre = {(r, c): source.load(c, row + r, x) for r in range(-1, rows + 1) for c in columns}
    results = []
    for r in range(rows):
        after = [pltpu.roll(centre[r, c], 1, 1) for c in columns]
        before = [pltpu.roll(centre[r, c], 127, 1) for c in columns]
        for c in columns:
            low = after[c - 1] if c else 0.0
            high = before[c + 1] if c + 1 < source.columns else 0.0
            total = jnp.where(masks[0], low, after[c]) + jnp.where(masks[1], high, before[c])
            total = total + (source.load(c, row + r, x - 1) + source.load(c, row + r, x + 1))
            total = total + (centre[r - 1, c] + centre[r + 1, c])
            value = diagonal.load(c, row + r, x) * centre[r, c] - total
            results.append((c, row + r, value))
    return results


def apply_block(target, source, diagonal, row, rows, minus, masks):
    for x in range(0, source.cells, 8):
        results = stencil_block(source, diagonal, row, rows, x, masks)
        if minus is not None:
            results = [(c, r, value - SHIFT * minus.load(c, r, x)) for c, r, value in results]
        for c, r, value in results:
            target.store(c, r, x, value)


def apply_rows(target, source, diagonal, first, count, minus=None, block=4):
    masks = lane_masks()

    def body(step, carry):
        apply_block(target, source, diagonal, step * block + first, block, minus, masks)
        return carry

    lax.fori_loop(0, count // block, body, 0)
    if count % block:
        start = first + count - count % block
        apply_block(target, source, diagonal, start, count % block, minus, masks)


def apply_strips(spot_ref, own, target, source, diagonal, halo, size, minus=None):
    masks = lane_masks()

    def body(step, carry):
        row = step * (own - size + 2 * halo) - halo
        apply_block(target, source, diagonal, row, size, minus, masks)
        return carry

    lax.fori_loop(0, 2, body, 0)
    clear_outside(spot_ref, own, target)


def clear_outside(spot_ref, own, field):
    @pl.when(spot_ref[0] == 1)
    def _():
        field.clear_row(-1)

    @pl.when(spot_ref[1] == 1)
    def _():
        field.clear_row(own)


def split_chip(grid, chip):
    nz = grid[1]
    return lax.div(chip, nz), lax.rem(chip, nz)


def pack_kappa_kernel(kappa_ref, out_ref, sem):
    copies = []
    for column in range(out_ref.shape[0]):
        part = kappa_ref.at[:, pl.ds(column * 128, 128)]
        copies.append(pltpu.make_async_copy(part, out_ref.at[column], sem.at[column]))
    for copy in copies:
        copy.start()
    for copy in copies:
        copy.wait()


def pack_probes_kernel(grid, count, spot_ref, after_ref, probes_ref, *rest):
    nx, nz, bx, by, bz = grid
    rows = bx * by
    outs, sem = rest[:-1], rest[-1]
    copies = []
    for k, out in enumerate(outs):
        x, z = split_chip(grid, spot_ref[4] ^ k)
        for core in range(2):
            start = pl.multiple_of(lax.rem((2 * x + core) * nz + z, count) * rows, rows)
            for column in range(bz // 128):
                part = probes_ref.at[pl.ds(start, rows), pl.ds(column * 128, 128)]
                copies.append(
                    pltpu.make_async_copy(part, out.at[core, column], sem.at[k, core, column])
                )
    for copy in copies:
        copy.start()
    for copy in copies:
        copy.wait()


def stack_kernel(after_ref, *refs):
    for k, ref in enumerate(refs[:-1]):
        refs[-1][k] = ref[...]


def sort_probes_kernel(spot_ref, after_ref, after_too_ref, *refs):
    parts, mine_ref, give_ref = refs[:-2], refs[-2], refs[-1]
    core = spot_ref[3]
    for k, part in enumerate(parts):
        mine_ref[k] = part[core]
        give_ref[k] = part[1 - core]


def block_rows(grid, spot_ref, mine_ref, other_ref, rows):
    nx, nz, bx, by, bz = grid
    per = bz // 128
    core = spot_ref[3]
    for k in range(nx // 2 * nz):
        x, z = split_chip(grid, spot_ref[4] ^ k)
        for ref, side in ((mine_ref, core), (other_ref, 1 - core)):
            for column in range(per):
                values = [ref[k, column, pl.ds(y, bx, stride=by), :] for y in rows]
                yield (2 * x + side) * bx, z * per + column, values


def store_own(field, x, z, values):
    for y, value in enumerate(values):
        at = pl.ds(pl.multiple_of(PAD + x, 8), 8)
        field.ref[z, y + field.halo, at, :] = value


def store_edges(spot_ref, even_ref, odd_ref, x, z, first, last):
    at = pl.ds(pl.multiple_of(x, 8), 8)
    odd = spot_ref[5] == 1
    for y, (below, above) in enumerate(zip(first, last)):
        even_ref[z, y, at, :] = jnp.where(odd, below, above)
        odd_ref[z, y, at, :] = jnp.where(odd, above, below)


def edge_kernel(grid, spot_ref, mine_ref, other_ref, even_ref, odd_ref):
    by = grid[3]
    rows = list(range(HALO)) + list(range(by - HALO, by))
    for x, z, values in block_rows(grid, spot_ref, mine_ref, other_ref, rows):
        store_edges(spot_ref, even_ref, odd_ref, x, z, values[:HALO], values[HALO:])


def diagonal_kernel(grid, spot_ref, mine_ref, other_ref, own_ref, even_ref, odd_ref):
    own = Field(own_ref, DIAGONAL_HALO)
    for x, z, values in block_rows(grid, spot_ref, mine_ref, other_ref, range(grid[3])):
        values = [6.0 + value for value in values]
        store_own(own, x, z, values)
        first, last = values[:DIAGONAL_HALO], values[-DIAGONAL_HALO:]
        store_edges(spot_ref, even_ref, odd_ref, x, z, first, last)


def fill_halo(spot_ref, field, own, even_ref, odd_ref):
    odd = spot_ref[5] == 1
    for c in range(field.columns):
        for y in range(field.halo):
            for x in range(0, field.cells, 8):
                even, other = even_ref[c, y, pl.ds(x, 8), :], odd_ref[c, y, pl.ds(x, 8), :]
                field.store(c, y - field.halo, x, jnp.where(odd, even, other))
                field.store(c, own + y, x, jnp.where(odd, other, even))


def inner_kernel(
    grid, spot_ref, mine_ref, other_ref, diagonal_ref, c0_ref, d0_ref, c1_ref, d1_ref, c2_ref
):
    own = grid[3]
    c0 = Field(c0_ref, HALO)
    diagonal = Field(diagonal_ref, DIAGONAL_HALO)
    d0 = Field(d0_ref, 4)
    c1 = Field(c1_ref, 3)
    d1 = Field(d1_ref, 2)
    c2 = Field(c2_ref, HALO)
    for field in (c0, d0, c1, d1, c2):
        field.clear_pads()
    for x, z, values in block_rows(grid, spot_ref, mine_ref, other_ref, range(own)):
        store_own(c0, x, z, values)
    apply_rows(d0, c0, diagonal, 1, own - 2)
    apply_rows(c1, d0, diagonal, 2, own - 4, c0)
    apply_rows(d1, c1, diagonal, 3, own - 6)
    apply_rows(c2, d1, diagonal, 4, own - 8, c1)


def first_kernel(
    own,
    spot_ref, c0_in, diagonal_in, d0_in, c1_in, d1_in, c2_in,
    even_ref, odd_ref, even_diagonal_ref, odd_diagonal_ref,
    c0_ref, diagonal_ref, d0_ref, c1_ref, d1_ref, c2_ref, even_out, odd_out,
):
    c0 = Field(c0_ref, HALO)
    diagonal = Field(diagonal_ref, DIAGONAL_HALO)
    d0 = Field(d0_ref, 4)
    c1 = Field(c1_ref, 3)
    d1 = Field(d1_ref, 2)
    c2 = Field(c2_ref, HALO)
    fill_halo(spot_ref, c0, own, even_ref, odd_ref)
    fill_halo(spot_ref, diagonal, own, even_diagonal_ref, odd_diagonal_ref)
    strips = functools.partial(apply_strips, spot_ref, own)
    strips(d0, c0, diagonal, 4, HALO)
    strips(c1, d0, diagonal, 3, HALO, c0)
    strips(d1, c1, diagonal, 2, HALO)
    strips(c2, d1, diagonal, 1, HALO, c1)
    for c in range(c2.columns):
        for x in range(0, c2.cells, 8):
            first = [c2.load(c, y, x) for y in range(HALO)]
            last = [c2.load(c, own - HALO + y, x) for y in range(HALO)]
            store_edges(spot_ref, even_out, odd_out, x, c, first, last)


def middle_kernel(own, c0_ref, c1_ref, c2_ref, diagonal_ref, d2_ref, moments_ref):
    c0 = Field(c0_ref, HALO)
    diagonal = Field(diagonal_ref, DIAGONAL_HALO)
    c1 = Field(c1_ref, 3)
    c2 = Field(c2_ref, HALO)
    d2 = Field(d2_ref, 4)
    d2.clear_pads()
    apply_rows(d2, c2, diagonal, 0, own)

    def moment_row(row, sums):
        for x in range(0, c0.cells, 8):
            for c in range(c0.columns):
                a, b, e, d = (field.load(c, row, x) for field in (c0, c1, c2, d2))
                pairs = ((a, a), (a, b), (b, b), (b, e), (e, e), (d, d))
                sums = tuple(total + u * v for total, (u, v) in zip(sums, pairs))
        return sums

    zero = jnp.zeros((8, 128), jnp.float32)
    sums = lax.fori_loop(0, own, moment_row, (zero,) * 6)
    sums = [jnp.sum(total, axis=0, keepdims=True) for total in sums]
    moments_ref[...] = jnp.concatenate(sums + [zero[:2]], axis=0)


def moment_slopes(inverse_count, probe, weights_ref, moment_refs):
    total = moment_refs[0][...]
    for ref in moment_refs[1:]:
        total = total + ref[...]
    total = jnp.sum(total, axis=1, keepdims=True) * inverse_count
    raw = [jnp.broadcast_to(total[k : k + 1], (8, 128)) for k in range(6)]
    moments = tuple(raw[:5]) + (raw[5] - SHIFT * raw[4],)
    weights = [weights_ref[k, probe] for k in range(5)]
    value, pullback = jax.vjp(lambda m: loss_of_moments(m, weights), moments)
    (slopes,) = pullback(jnp.full((8, 128), 2.0, jnp.float32))
    return [slope[0, 0] for slope in slopes]


def second_inner_kernel(own, diagonal_ref, c2_ref, d2_ref, c3_ref, d3_ref, c4_ref):
    diagonal = Field(diagonal_ref, DIAGONAL_HALO)
    c2 = Field(c2_ref, HALO)
    d2 = Field(d2_ref, 4)
    c3 = Field(c3_ref, 3)
    d3 = Field(d3_ref, 2)
    c4 = Field(c4_ref, 1)
    for field in (c3, d3, c4):
        field.clear_pads()
    apply_rows(c3, d2, diagonal, 1, own - 2, c2)
    apply_rows(d3, c3, diagonal, 2, own - 4)
    apply_rows(c4, d3, diagonal, 3, own - 6, c3)


def third_kernel(
    own,
    spot_ref, diagonal_ref, c2_in, d2_in, c3_in, d3_in, c4_in, even_ref, odd_ref,
    c2_ref, d2_ref, c3_ref, d3_ref, c4_ref,
):
    diagonal = Field(diagonal_ref, DIAGONAL_HALO)
    c2 = Field(c2_ref, HALO)
    d2 = Field(d2_ref, 4)
    c3 = Field(c3_ref, 3)
    d3 = Field(d3_ref, 2)
    c4 = Field(c4_ref, 1)
    fill_halo(spot_ref, c2, own, even_ref, odd_ref)
    strips = functools.partial(apply_strips, spot_ref, own)
    strips(d2, c2, diagonal, 4, 4)
    strips(c3, d2, diagonal, 3, 4, c2)
    strips(d3, c3, diagonal, 2, 4)
    strips(c4, d3, diagonal, 1, 4, c3)


def last_kernel(
    grid, inverse_count, flip,
    spot_ref, weights_ref, c0_ref, diagonal_ref, d0_ref, c1_ref, d1_ref,
    c2_ref, d2_ref, c3_ref, d3_ref, c4_ref, *rest,
):
    nx, nz, bx, by, bz = grid
    per = bz // 128
    moment_refs, out_ref = rest[:-1], rest[-1]
    c0 = Field(c0_ref, HALO)
    diagonal = Field(diagonal_ref, DIAGONAL_HALO)
    d0 = Field(d0_ref, 4)
    c1 = Field(c1_ref, 3)
    d1 = Field(d1_ref, 2)
    c2 = Field(c2_ref, HALO)
    d2 = Field(d2_ref, 4)
    c3 = Field(c3_ref, 3)
    d3 = Field(d3_ref, 2)
    c4 = Field(c4_ref, 1)
    slopes = moment_slopes(inverse_count, spot_ref[2], weights_ref, moment_refs)
    masks = lane_masks()
    block = 2

    def out_rows(core, step, carry):
        row = step * block
        for chip in range(nx // 2):
            x = (2 * chip + core) * bx
            results = []
            for z, at, d4 in stencil_block(c4, diagonal, row, block, x, masks):
                cs = [field.load(z, at, x) for field in (c0, c1, c2, c3, c4)]
                ds = [field.load(z, at, x) for field in (d0, d1, d2, d3)] + [d4]
                total = None
                for i in range(5):
                    inner = None
                    for j in range(5 - i):
                        term = slopes[i + j + 1] * ds[j]
                        inner = term if inner is None else inner + term
                    term = cs[i] * inner
                    total = term if total is None else total + term
                results.append((chip * nz + z // per, z % per, at, total))
            for place, column, at, total in results:
                out_ref[place, column, pl.ds(at, bx, stride=by), :] = total
        return carry

    for core in range(2):

        @pl.when(spot_ref[3] == (1 - core if flip else core))
        def _():
            lax.fori_loop(0, by // block, functools.partial(out_rows, core), 0)


def add_kernel(spot_ref, kept_ref, got_ref, *outs):
    for k, out in enumerate(outs):
        chip = spot_ref[4] ^ k
        out[...] = kept_ref[chip] + got_ref[chip]


def sum_kernel(grid, *refs):
    nx, nz, bx, by, bz = grid
    parts, out_ref = refs[:-1], refs[-1]
    for column in range(bz // 128):
        for x in range(bx):
            total = None
            for ref in parts:
                part = ref[column, pl.ds(x * by, by), :]
                total = part if total is None else total + part
            out_ref[x, :, pl.ds(column * 128, 128)] = total


def vmem():
    return pl.BlockSpec(memory_space=pltpu.VMEM)


def smem():
    return pl.BlockSpec(memory_space=pltpu.SMEM)


def hbm():
    return pl.BlockSpec(memory_space=pltpu.HBM)


def here(value):
    return pltpu.with_memory_space_constraint(value, pltpu.VMEM)


def there(value):
    return pltpu.with_memory_space_constraint(value, pltpu.HBM)


def f32(*shape):
    return jax.ShapeDtypeStruct(shape, jnp.float32)


def params():
    return pltpu.CompilerParams(vmem_limit_bytes=12 * MIB)


def body(probes, kappa2, cotangents):
    nx, ny, nz = (lax.axis_size(axis) for axis in (("chip", "core"), "gy", "gz"))
    count, bx, by, bz = probes.shape
    group = nx * nz
    assert group % count == 0 and nx % 2 == 0 and bx == 8 and bz == 256
    assert by % 8 == 0 and by >= HALO
    X = nx * bx
    columns = nz * bz // 128
    per = bz // 128
    rows = bx * by
    grid = (nx, nz, bx, by, bz)
    core, gy = lax.axis_index("core"), lax.axis_index("gy")
    place = (lax.axis_index("chip") * 2 + core) * nz + lax.axis_index("gz")
    mine = place % count
    assert ny & (ny - 1) == 0
    even = [(i, i ^ 1) for i in range(ny)]
    odd = [(i, i + 1 if i % 2 else i - 1) for i in range(1, ny - 1)]
    swap = [(0, 1), (1, 0)]

    def edge(halo):
        return f32(columns, halo, X, 128)

    def padded(halo):
        return (columns, by + 2 * halo, X + 2 * PAD, 128)

    def vector(halo):
        return pltpu.VMEM(padded(halo), jnp.float32)

    chips = nx // 2 * nz
    assert chips & (chips - 1) == 0
    chip = lax.axis_index("chip") * nz + lax.axis_index("gz")
    spot = jnp.stack([gy == 0, gy == ny - 1, mine, core, chip, gy % 2]).astype(jnp.int32)

    def to_chip(value, k):
        pairs = [(i, i ^ k) for i in range(chips)]
        return lax.ppermute(value, ("chip", "gz"), pairs)

    def plain(kernel, name, out_shape, specs, *operands, **options):
        return pl.pallas_call(
            kernel,
            out_shape=out_shape,
            in_specs=specs,
            out_specs=(vmem(),) * len(out_shape) if isinstance(out_shape, tuple) else vmem(),
            compiler_params=params(),
            name=name,
            **options,
        )(*operands)

    dma = pltpu.SemaphoreType.DMA
    block = f32(per, rows, 128)
    stacked = f32(chips, per, rows, 128)
    kappa = plain(
        pack_kappa_kernel, "pack_kappa", block, [hbm()], there(kappa2.reshape(rows, bz)),
        scratch_shapes=[dma((per,))],
    )
    kappas = [kappa] + [to_chip(kappa, k) for k in range(1, chips)]
    packed = plain(
        functools.partial(pack_probes_kernel, grid, count), "pack_probes",
        (f32(2, per, rows, 128),) * chips, [smem(), vmem(), hbm()],
        spot, kappa, there(probes.reshape(count * rows, bz)), scratch_shapes=[dma((chips, 2, per))],
    )
    probes = [packed[0]] + [to_chip(packed[k], k) for k in range(1, chips)]

    kappa = plain(
        stack_kernel, "stack_kappa", stacked,
        [vmem()] * (chips + 1), packed[0], *kappas,
    )
    other = lax.ppermute(kappa, "core", swap)
    diagonal, even_edge, odd_edge = plain(
        functools.partial(diagonal_kernel, grid), "diagonal_rows",
        (vector(DIAGONAL_HALO), edge(DIAGONAL_HALO), edge(DIAGONAL_HALO)),
        [smem(), vmem(), vmem()], spot, kappa, other,
    )
    even_diagonal = lax.ppermute(even_edge, "gy", even)
    odd_diagonal = lax.ppermute(odd_edge, "gy", odd)

    probe, give = plain(
        sort_probes_kernel, "sort_probes", (stacked, stacked),
        [smem()] + [vmem()] * (chips + 2), spot, even_diagonal, odd_diagonal, *probes,
    )
    other = lax.ppermute(give, "core", swap)
    even_edge, odd_edge = plain(
        functools.partial(edge_kernel, grid), "probe_edges", (edge(HALO), edge(HALO)),
        [smem(), vmem(), vmem()], spot, probe, other,
    )
    even1 = lax.ppermute(even_edge, "gy", even)
    odd1 = lax.ppermute(odd_edge, "gy", odd)

    cells = by * X * columns * 128

    def cost(operations):
        return pl.CostEstimate(
            flops=operations * cells, bytes_accessed=16 * cells, transcendentals=0
        )

    inner = pl.pallas_call(
        functools.partial(inner_kernel, grid),
        out_shape=tuple(vector(h) for h in (HALO, 4, 3, 2, HALO)),
        in_specs=[smem()] + [vmem()] * 3,
        out_specs=(vmem(),) * 5,
        compiler_params=params(),
        cost_estimate=cost(32),
        name="inner_steps",
    )(spot, probe, other, here(diagonal))
    vectors = [here(value) for value in (inner[0], diagonal) + tuple(inner[1:])]
    c0, diagonal, d0, c1, d1, c2, even_edge, odd_edge = pl.pallas_call(
        functools.partial(first_kernel, by),
        out_shape=tuple(vector(h) for h in (HALO, DIAGONAL_HALO, 4, 3, 2, HALO))
        + (edge(HALO), edge(HALO)),
        in_specs=[smem()] + [vmem()] * 10,
        out_specs=(vmem(),) * 8,
        input_output_aliases={i + 1: i for i in range(6)},
        compiler_params=params(),
        name="first_steps",
    )(spot, *vectors, even1, odd1, even_diagonal, odd_diagonal)
    even2 = lax.ppermute(even_edge, "gy", even)
    odd2 = lax.ppermute(odd_edge, "gy", odd)
    d2, moments = pl.pallas_call(
        functools.partial(middle_kernel, by),
        out_shape=(vector(4), f32(8, 128)),
        in_specs=[vmem()] * 4,
        out_specs=(vmem(),) * 2,
        compiler_params=params(),
        cost_estimate=cost(24),
        name="middle_step",
    )(here(c0), here(c1), here(c2), here(diagonal))
    shares = [moments]
    for step in range(1, ny):
        shares.append(lax.ppermute(moments, "gy", [(i, i ^ step) for i in range(ny)]))

    c3, d3, c4 = pl.pallas_call(
        functools.partial(second_inner_kernel, by),
        out_shape=tuple(vector(h) for h in (3, 2, 1)),
        in_specs=[vmem()] * 3,
        out_specs=(vmem(),) * 3,
        compiler_params=params(),
        cost_estimate=cost(30),
        name="second_inner_steps",
    )(here(diagonal), here(c2), here(d2))
    vectors = [here(value) for value in (diagonal, c2, d2, c3, d3, c4)]
    c2, d2, c3, d3, c4 = pl.pallas_call(
        functools.partial(third_kernel, by),
        out_shape=tuple(vector(h) for h in (HALO, 4, 3, 2, 1)),
        in_specs=[smem()] + [vmem()] * 8,
        out_specs=(vmem(),) * 5,
        input_output_aliases={i + 2: i for i in range(5)},
        compiler_params=params(),
        cost_estimate=cost(20),
        name="third_steps",
    )(spot, *vectors, even2, odd2)
    inverse_count = 1.0 / (ny * cells)
    vectors = [here(value) for value in (c0, diagonal, d0, c1, d1, c2, d2, c3, d3, c4)]
    if group > count:
        cotangents = jnp.where(place < count, cotangents, 0.0)

    def last_step(flip):
        return pl.pallas_call(
            functools.partial(last_kernel, grid, inverse_count, flip),
            out_shape=stacked,
            in_specs=[smem(), smem()] + [vmem()] * (10 + ny),
            out_specs=vmem(),
            compiler_params=params(),
            cost_estimate=cost(20),
            name="last_step_given" if flip else "last_step_kept",
        )(spot, cotangents, *vectors, *shares)

    got = lax.ppermute(last_step(True), "core", swap)
    parts = plain(
        add_kernel, "add_cores", (block,) * chips, [smem(), vmem(), vmem()],
        spot, last_step(False), got,
    )
    parts = [parts[0]] + [to_chip(parts[k], k) for k in range(chips - 1, 0, -1)]
    return plain(
        functools.partial(sum_kernel, grid), "sum_chips", f32(bx, by, bz), [vmem()] * chips, *parts
    )


def solution(mesh):
    nx, ny, nz = (mesh.shape[axis] for axis in ("gx", "gy", "gz"))
    devices = mesh.devices.reshape(nx // 2, 2, ny, nz)
    split = jax.sharding.Mesh(devices, ("chip", "core", "gy", "gz"))
    gx = ("chip", "core")
    return jax.shard_map(
        body,
        mesh=split,
        in_specs=(P(None, gx, "gy", "gz"), P(gx, "gy", "gz"), P()),
        out_specs=P(gx, "gy", "gz"),
        check_vma=False,
    )
```

```python
import functools

import jax
import jax.numpy as jnp
from jax import lax
from jax.experimental import pallas as pl
from jax.experimental.pallas import tpu as pltpu
from jax.sharding import PartitionSpec as P

EPSILON = 1e-06
SHIFT = 64.0
HALO = 5
DIAGONAL_HALO = 4
PAD = 8
MIB = 1024 * 1024


def loss_of_moments(moments, weights):
    m0, m1, m2, m3, m4, m5 = moments
    norm = m0 + EPSILON
    alpha1 = (m1 + SHIFT * m0) / norm
    e1 = SHIFT - alpha1
    rest1 = jnp.maximum(m2 + 2.0 * e1 * m1 + e1 * e1 * m0, 0.0)
    beta1_square = rest1 / norm + EPSILON
    beta1 = jnp.sqrt(beta1_square)
    scale = 1.0 / (norm * beta1_square)
    alpha2 = scale * (m3 + 2.0 * e1 * m2 + e1 * e1 * m1 + SHIFT * rest1) - (m1 + e1 * m0) / norm
    e2 = SHIFT - alpha2
    f1 = e1 + e2
    f0 = e1 * e2 - beta1_square
    g = f1 * f1 + 2.0 * f0
    rest2 = jnp.maximum(m4 + 2.0 * f1 * m3 + g * m2 + 2.0 * f1 * f0 * m1 + f0 * f0 * m0, 0.0)
    beta2_square = scale * rest2 + EPSILON
    beta2 = jnp.sqrt(beta2_square)
    image2 = m5 + 2.0 * f1 * m4 + g * m3 + 2.0 * f1 * f0 * m2 + f0 * f0 * m1
    cross = m3 + f1 * m2 + f0 * m1 + e1 * (m2 + f1 * m1 + f0 * m0)
    alpha3 = scale * ((image2 + SHIFT * rest2) / beta2_square - cross)
    return (
        weights[0] * alpha1
        + weights[1] * alpha2
        + weights[2] * alpha3
        + weights[3] * beta1
        + weights[4] * beta2
    )


class Field:
    def __init__(self, ref, halo):
        self.ref = ref
        self.halo = halo
        self.columns, self.rows, self.pitch, _ = ref.shape
        self.cells = self.pitch - 2 * PAD

    def load(self, column, row, x):
        return self.ref[column, row + self.halo, pl.ds(PAD + x, 8), :]

    def store(self, column, row, x, value):
        self.ref[column, row + self.halo, pl.ds(PAD + x, 8), :] = value

    def clear_pads(self):
        zero = jnp.zeros((8, 128), jnp.float32)

        def body(at, carry):
            for column in range(self.columns):
                self.ref[column, at, pl.ds(0, PAD), :] = zero
                self.ref[column, at, pl.ds(PAD + self.cells, PAD), :] = zero
            return carry

        lax.fori_loop(0, self.rows, body, 0)

    def clear_row(self, row):
        zero = jnp.zeros((8, 128), jnp.float32)
        for column in range(self.columns):
            for x in range(0, self.cells, 8):
                self.store(column, row, x, zero)


def lane_masks():
    lane = lax.broadcasted_iota(jnp.int32, (8, 128), 1)
    return lane == 0, lane == 127


def stencil_block(source, diagonal, row, rows, x, masks):
    columns = range(source.columns)
    centre = {(r, c): source.load(c, row + r, x) for r in range(-1, rows + 1) for c in columns}
    results = []
    for r in range(rows):
        after = [pltpu.roll(centre[r, c], 1, 1) for c in columns]
        before = [pltpu.roll(centre[r, c], 127, 1) for c in columns]
        for c in columns:
            low = after[c - 1] if c else 0.0
            high = before[c + 1] if c + 1 < source.columns else 0.0
            total = jnp.where(masks[0], low, after[c]) + jnp.where(masks[1], high, before[c])
            total = total + (source.load(c, row + r, x - 1) + source.load(c, row + r, x + 1))
            total = total + (centre[r - 1, c] + centre[r + 1, c])
            value = diagonal.load(c, row + r, x) * centre[r, c] - total
            results.append((c, row + r, value))
    return results


def apply_block(target, source, diagonal, row, rows, minus, masks):
    for x in range(0, source.cells, 8):
        results = stencil_block(source, diagonal, row, rows, x, masks)
        if minus is not None:
            results = [(c, r, value - SHIFT * minus.load(c, r, x)) for c, r, value in results]
        for c, r, value in results:
            target.store(c, r, x, value)


def apply_rows(target, source, diagonal, first, count, minus=None, block=4):
    masks = lane_masks()

    def body(step, carry):
        apply_block(target, source, diagonal, step * block + first, block, minus, masks)
        return carry

    lax.fori_loop(0, count // block, body, 0)
    if count % block:
        start = first + count - count % block
        apply_block(target, source, diagonal, start, count % block, minus, masks)


def apply_strips(spot_ref, own, target, source, diagonal, halo, size, minus=None):
    masks = lane_masks()

    def body(step, carry):
        row = step * (own - size + 2 * halo) - halo
        apply_block(target, source, diagonal, row, size, minus, masks)
        return carry

    lax.fori_loop(0, 2, body, 0)
    clear_outside(spot_ref, own, target)


def clear_outside(spot_ref, own, field):
    @pl.when(spot_ref[0] == 1)
    def _():
        field.clear_row(-1)

    @pl.when(spot_ref[1] == 1)
    def _():
        field.clear_row(own)


def split_chip(grid, chip):
    nz = grid[1]
    return lax.div(chip, nz), lax.rem(chip, nz)


def pack_kappa_kernel(kappa_ref, out_ref, sem):
    copies = []
    for column in range(out_ref.shape[0]):
        part = kappa_ref.at[:, pl.ds(column * 128, 128)]
        copies.append(pltpu.make_async_copy(part, out_ref.at[column], sem.at[column]))
    for copy in copies:
        copy.start()
    for copy in copies:
        copy.wait()


def pack_probes_kernel(grid, count, spot_ref, after_ref, probes_ref, *rest):
    nx, nz, bx, by, bz = grid
    rows = bx * by
    outs, sem = rest[:-1], rest[-1]
    copies = []
    for k, out in enumerate(outs):
        x, z = split_chip(grid, spot_ref[4] ^ k)
        for core in range(2):
            start = pl.multiple_of(lax.rem((2 * x + core) * nz + z, count) * rows, rows)
            for column in range(bz // 128):
                part = probes_ref.at[pl.ds(start, rows), pl.ds(column * 128, 128)]
                copies.append(
                    pltpu.make_async_copy(part, out.at[core, column], sem.at[k, core, column])
                )
    for copy in copies:
        copy.start()
    for copy in copies:
        copy.wait()


def stack_kernel(after_ref, *refs):
    for k, ref in enumerate(refs[:-1]):
        refs[-1][k] = ref[...]


def sort_probes_kernel(spot_ref, after_ref, after_too_ref, *refs):
    parts, mine_ref, give_ref = refs[:-2], refs[-2], refs[-1]
    core = spot_ref[3]
    for k, part in enumerate(parts):
        mine_ref[k] = part[core]
        give_ref[k] = part[1 - core]


def block_rows(grid, spot_ref, mine_ref, other_ref, rows):
    nx, nz, bx, by, bz = grid
    per = bz // 128
    core = spot_ref[3]
    for k in range(nx // 2 * nz):
        x, z = split_chip(grid, spot_ref[4] ^ k)
        for ref, side in ((mine_ref, core), (other_ref, 1 - core)):
            for column in range(per):
                values = [ref[k, column, pl.ds(y, bx, stride=by), :] for y in rows]
                yield (2 * x + side) * bx, z * per + column, values


def store_own(field, x, z, values):
    for y, value in enumerate(values):
        at = pl.ds(pl.multiple_of(PAD + x, 8), 8)
        field.ref[z, y + field.halo, at, :] = value


def store_edges(spot_ref, even_ref, odd_ref, x, z, first, last):
    at = pl.ds(pl.multiple_of(x, 8), 8)
    odd = spot_ref[5] == 1
    for y, (below, above) in enumerate(zip(first, last)):
        even_ref[z, y, at, :] = jnp.where(odd, below, above)
        odd_ref[z, y, at, :] = jnp.where(odd, above, below)


def edge_kernel(grid, spot_ref, mine_ref, other_ref, even_ref, odd_ref):
    by = grid[3]
    rows = list(range(HALO)) + list(range(by - HALO, by))
    for x, z, values in block_rows(grid, spot_ref, mine_ref, other_ref, rows):
        store_edges(spot_ref, even_ref, odd_ref, x, z, values[:HALO], values[HALO:])


def diagonal_kernel(grid, spot_ref, mine_ref, other_ref, own_ref, even_ref, odd_ref):
    own = Field(own_ref, DIAGONAL_HALO)
    for x, z, values in block_rows(grid, spot_ref, mine_ref, other_ref, range(grid[3])):
        values = [6.0 + value for value in values]
        store_own(own, x, z, values)
        first, last = values[:DIAGONAL_HALO], values[-DIAGONAL_HALO:]
        store_edges(spot_ref, even_ref, odd_ref, x, z, first, last)


def fill_halo(spot_ref, field, own, even_ref, odd_ref):
    odd = spot_ref[5] == 1
    inside = [1.0 - spot_ref[end].astype(jnp.float32) for end in range(2)]
    for c in range(field.columns):
        for y in range(field.halo):
            for x in range(0, field.cells, 8):
                even, other = even_ref[c, y, pl.ds(x, 8), :], odd_ref[c, y, pl.ds(x, 8), :]
                field.store(c, y - field.halo, x, jnp.where(odd, even, other) * inside[0])
                field.store(c, own + y, x, jnp.where(odd, other, even) * inside[1])


def inner_kernel(
    grid, spot_ref, mine_ref, other_ref, diagonal_ref, c0_ref, d0_ref, c1_ref, d1_ref, c2_ref
):
    own = grid[3]
    c0 = Field(c0_ref, HALO)
    diagonal = Field(diagonal_ref, DIAGONAL_HALO)
    d0 = Field(d0_ref, 4)
    c1 = Field(c1_ref, 3)
    d1 = Field(d1_ref, 2)
    c2 = Field(c2_ref, HALO)
    for field in (c0, d0, c1, d1, c2):
        field.clear_pads()
    for x, z, values in block_rows(grid, spot_ref, mine_ref, other_ref, range(own)):
        store_own(c0, x, z, values)
    apply_rows(d0, c0, diagonal, 1, own - 2)
    apply_rows(c1, d0, diagonal, 2, own - 4, c0)
    apply_rows(d1, c1, diagonal, 3, own - 6)
    apply_rows(c2, d1, diagonal, 4, own - 8, c1)


def first_kernel(
    own,
    spot_ref, c0_in, diagonal_in, d0_in, c1_in, d1_in, c2_in,
    even_ref, odd_ref, even_diagonal_ref, odd_diagonal_ref,
    c0_ref, diagonal_ref, d0_ref, c1_ref, d1_ref, c2_ref, even_out, odd_out,
):
    c0 = Field(c0_ref, HALO)
    diagonal = Field(diagonal_ref, DIAGONAL_HALO)
    d0 = Field(d0_ref, 4)
    c1 = Field(c1_ref, 3)
    d1 = Field(d1_ref, 2)
    c2 = Field(c2_ref, HALO)
    fill_halo(spot_ref, c0, own, even_ref, odd_ref)
    fill_halo(spot_ref, diagonal, own, even_diagonal_ref, odd_diagonal_ref)
    strips = functools.partial(apply_strips, spot_ref, own)
    strips(d0, c0, diagonal, 4, HALO)
    strips(c1, d0, diagonal, 3, HALO, c0)
    strips(d1, c1, diagonal, 2, HALO)
    strips(c2, d1, diagonal, 1, HALO, c1)
    for c in range(c2.columns):
        for x in range(0, c2.cells, 8):
            first = [c2.load(c, y, x) for y in range(HALO)]
            last = [c2.load(c, own - HALO + y, x) for y in range(HALO)]
            store_edges(spot_ref, even_out, odd_out, x, c, first, last)


def middle_kernel(own, c0_ref, c1_ref, c2_ref, diagonal_ref, d2_ref, moments_ref):
    c0 = Field(c0_ref, HALO)
    diagonal = Field(diagonal_ref, DIAGONAL_HALO)
    c1 = Field(c1_ref, 3)
    c2 = Field(c2_ref, HALO)
    d2 = Field(d2_ref, 4)
    d2.clear_pads()
    apply_rows(d2, c2, diagonal, 0, own)

    def moment_row(row, sums):
        for x in range(0, c0.cells, 8):
            for c in range(c0.columns):
                a, b, e, d = (field.load(c, row, x) for field in (c0, c1, c2, d2))
                pairs = ((a, a), (a, b), (b, b), (b, e), (e, e), (d, d))
                sums = tuple(total + u * v for total, (u, v) in zip(sums, pairs))
        return sums

    zero = jnp.zeros((8, 128), jnp.float32)
    sums = lax.fori_loop(0, own, moment_row, (zero,) * 6)
    sums = [jnp.sum(total, axis=0, keepdims=True) for total in sums]
    moments_ref[...] = jnp.concatenate(sums + [zero[:2]], axis=0)


def moment_slopes(inverse_count, probe, weights_ref, moment_refs):
    total = moment_refs[0][...]
    for ref in moment_refs[1:]:
        total = total + ref[...]
    total = jnp.sum(total, axis=1, keepdims=True) * inverse_count
    raw = [jnp.broadcast_to(total[k : k + 1], (8, 128)) for k in range(6)]
    moments = tuple(raw[:5]) + (raw[5] - SHIFT * raw[4],)
    weights = [weights_ref[k, probe] for k in range(5)]
    value, pullback = jax.vjp(lambda m: loss_of_moments(m, weights), moments)
    (slopes,) = pullback(jnp.full((8, 128), 2.0, jnp.float32))
    return [slope[0, 0] for slope in slopes]


def second_inner_kernel(own, diagonal_ref, c2_ref, d2_ref, c3_ref, d3_ref, c4_ref):
    diagonal = Field(diagonal_ref, DIAGONAL_HALO)
    c2 = Field(c2_ref, HALO)
    d2 = Field(d2_ref, 4)
    c3 = Field(c3_ref, 3)
    d3 = Field(d3_ref, 2)
    c4 = Field(c4_ref, 1)
    for field in (c3, d3, c4):
        field.clear_pads()
    apply_rows(c3, d2, diagonal, 1, own - 2, c2)
    apply_rows(d3, c3, diagonal, 2, own - 4)
    apply_rows(c4, d3, diagonal, 3, own - 6, c3)


def third_kernel(
    own,
    spot_ref, diagonal_ref, c2_in, d2_in, c3_in, d3_in, c4_in, even_ref, odd_ref,
    c2_ref, d2_ref, c3_ref, d3_ref, c4_ref,
):
    diagonal = Field(diagonal_ref, DIAGONAL_HALO)
    c2 = Field(c2_ref, HALO)
    d2 = Field(d2_ref, 4)
    c3 = Field(c3_ref, 3)
    d3 = Field(d3_ref, 2)
    c4 = Field(c4_ref, 1)
    fill_halo(spot_ref, c2, own, even_ref, odd_ref)
    strips = functools.partial(apply_strips, spot_ref, own)
    strips(d2, c2, diagonal, 4, 4)
    strips(c3, d2, diagonal, 3, 4, c2)
    strips(d3, c3, diagonal, 2, 4)
    strips(c4, d3, diagonal, 1, 4, c3)


def last_kernel(
    grid, inverse_count, flip,
    spot_ref, weights_ref, c0_ref, diagonal_ref, d0_ref, c1_ref, d1_ref,
    c2_ref, d2_ref, c3_ref, d3_ref, c4_ref, *rest,
):
    nx, nz, bx, by, bz = grid
    per = bz // 128
    moment_refs, out_ref = rest[:-1], rest[-1]
    c0 = Field(c0_ref, HALO)
    diagonal = Field(diagonal_ref, DIAGONAL_HALO)
    d0 = Field(d0_ref, 4)
    c1 = Field(c1_ref, 3)
    d1 = Field(d1_ref, 2)
    c2 = Field(c2_ref, HALO)
    d2 = Field(d2_ref, 4)
    c3 = Field(c3_ref, 3)
    d3 = Field(d3_ref, 2)
    c4 = Field(c4_ref, 1)
    slopes = moment_slopes(inverse_count, spot_ref[2], weights_ref, moment_refs)
    masks = lane_masks()
    block = 2

    def out_rows(core, step, carry):
        row = step * block
        for chip in range(nx // 2):
            x = (2 * chip + core) * bx
            results = []
            for z, at, d4 in stencil_block(c4, diagonal, row, block, x, masks):
                cs = [field.load(z, at, x) for field in (c0, c1, c2, c3, c4)]
                ds = [field.load(z, at, x) for field in (d0, d1, d2, d3)] + [d4]
                total = None
                for i in range(5):
                    inner = None
                    for j in range(5 - i):
                        term = slopes[i + j + 1] * ds[j]
                        inner = term if inner is None else inner + term
                    term = cs[i] * inner
                    total = term if total is None else total + term
                results.append((chip * nz + z // per, z % per, at, total))
            for place, column, at, total in results:
                out_ref[place, column, pl.ds(at, bx, stride=by), :] = total
        return carry

    for core in range(2):

        @pl.when(spot_ref[3] == (1 - core if flip else core))
        def _():
            lax.fori_loop(0, by // block, functools.partial(out_rows, core), 0)


def add_kernel(spot_ref, kept_ref, got_ref, *outs):
    for k, out in enumerate(outs):
        chip = spot_ref[4] ^ k
        out[...] = kept_ref[chip] + got_ref[chip]


def sum_kernel(grid, *refs):
    nx, nz, bx, by, bz = grid
    parts, out_ref = refs[:-1], refs[-1]
    for column in range(bz // 128):
        for x in range(bx):
            total = None
            for ref in parts:
                part = ref[column, pl.ds(x * by, by), :]
                total = part if total is None else total + part
            out_ref[x, :, pl.ds(column * 128, 128)] = total


def vmem():
    return pl.BlockSpec(memory_space=pltpu.VMEM)


def smem():
    return pl.BlockSpec(memory_space=pltpu.SMEM)


def hbm():
    return pl.BlockSpec(memory_space=pltpu.HBM)


def here(value):
    return pltpu.with_memory_space_constraint(value, pltpu.VMEM)


def there(value):
    return pltpu.with_memory_space_constraint(value, pltpu.HBM)


def f32(*shape):
    return jax.ShapeDtypeStruct(shape, jnp.float32)


def params():
    return pltpu.CompilerParams(vmem_limit_bytes=12 * MIB)


def body(probes, kappa2, cotangents):
    nx, ny, nz = (lax.axis_size(axis) for axis in (("chip", "core"), "gy", "gz"))
    count, bx, by, bz = probes.shape
    group = nx * nz
    assert group % count == 0 and nx % 2 == 0 and bx == 8 and bz == 256
    assert by % 8 == 0 and by >= HALO
    X = nx * bx
    columns = nz * bz // 128
    per = bz // 128
    rows = bx * by
    grid = (nx, nz, bx, by, bz)
    core, gy = lax.axis_index("core"), lax.axis_index("gy")
    place = (lax.axis_index("chip") * 2 + core) * nz + lax.axis_index("gz")
    mine = place % count
    assert ny & (ny - 1) == 0
    even = [(i, i ^ 1) for i in range(ny)]
    odd = [(i, min(max(i + 1 if i % 2 else i - 1, 0), ny - 1)) for i in range(ny)]
    swap = [(0, 1), (1, 0)]

    def edge(halo):
        return f32(columns, halo, X, 128)

    def padded(halo):
        return (columns, by + 2 * halo, X + 2 * PAD, 128)

    def vector(halo):
        return pltpu.VMEM(padded(halo), jnp.float32)

    chips = nx // 2 * nz
    assert chips & (chips - 1) == 0
    chip = lax.axis_index("chip") * nz + lax.axis_index("gz")
    spot = jnp.stack([gy == 0, gy == ny - 1, mine, core, chip, gy % 2]).astype(jnp.int32)

    def to_chip(value, k):
        pairs = [(i, i ^ k) for i in range(chips)]
        return lax.ppermute(value, ("chip", "gz"), pairs)

    def plain(kernel, name, out_shape, specs, *operands, **options):
        return pl.pallas_call(
            kernel,
            out_shape=out_shape,
            in_specs=specs,
            out_specs=(vmem(),) * len(out_shape) if isinstance(out_shape, tuple) else vmem(),
            compiler_params=params(),
            name=name,
            **options,
        )(*operands)

    dma = pltpu.SemaphoreType.DMA
    block = f32(per, rows, 128)
    stacked = f32(chips, per, rows, 128)
    kappa = plain(
        pack_kappa_kernel, "pack_kappa", block, [hbm()], there(kappa2.reshape(rows, bz)),
        scratch_shapes=[dma((per,))],
    )
    kappas = [kappa] + [to_chip(kappa, k) for k in range(1, chips)]
    packed = plain(
        functools.partial(pack_probes_kernel, grid, count), "pack_probes",
        (f32(2, per, rows, 128),) * chips, [smem(), vmem(), hbm()],
        spot, kappa, there(probes.reshape(count * rows, bz)), scratch_shapes=[dma((chips, 2, per))],
    )
    probes = [packed[0]] + [to_chip(packed[k], k) for k in range(1, chips)]

    kappa = plain(
        stack_kernel, "stack_kappa", stacked,
        [vmem()] * (chips + 1), packed[0], *kappas,
    )
    other = lax.ppermute(kappa, "core", swap)
    diagonal, even_edge, odd_edge = plain(
        functools.partial(diagonal_kernel, grid), "diagonal_rows",
        (vector(DIAGONAL_HALO), edge(DIAGONAL_HALO), edge(DIAGONAL_HALO)),
        [smem(), vmem(), vmem()], spot, kappa, other,
    )
    even_diagonal = lax.ppermute(even_edge, "gy", even)
    odd_diagonal = lax.ppermute(odd_edge, "gy", odd)

    probe, give = plain(
        sort_probes_kernel, "sort_probes", (stacked, stacked),
        [smem()] + [vmem()] * (chips + 2), spot, even_diagonal, odd_diagonal, *probes,
    )
    other = lax.ppermute(give, "core", swap)
    even_edge, odd_edge = plain(
        functools.partial(edge_kernel, grid), "probe_edges", (edge(HALO), edge(HALO)),
        [smem(), vmem(), vmem()], spot, probe, other,
    )
    even1 = lax.ppermute(even_edge, "gy", even)
    odd1 = lax.ppermute(odd_edge, "gy", odd)

    cells = by * X * columns * 128

    def cost(operations):
        return pl.CostEstimate(
            flops=operations * cells, bytes_accessed=16 * cells, transcendentals=0
        )

    inner = pl.pallas_call(
        functools.partial(inner_kernel, grid),
        out_shape=tuple(vector(h) for h in (HALO, 4, 3, 2, HALO)),
        in_specs=[smem()] + [vmem()] * 3,
        out_specs=(vmem(),) * 5,
        compiler_params=params(),
        cost_estimate=cost(32),
        name="inner_steps",
    )(spot, probe, other, here(diagonal))
    vectors = [here(value) for value in (inner[0], diagonal) + tuple(inner[1:])]
    c0, diagonal, d0, c1, d1, c2, even_edge, odd_edge = pl.pallas_call(
        functools.partial(first_kernel, by),
        out_shape=tuple(vector(h) for h in (HALO, DIAGONAL_HALO, 4, 3, 2, HALO))
        + (edge(HALO), edge(HALO)),
        in_specs=[smem()] + [vmem()] * 10,
        out_specs=(vmem(),) * 8,
        input_output_aliases={i + 1: i for i in range(6)},
        compiler_params=params(),
        name="first_steps",
    )(spot, *vectors, even1, odd1, even_diagonal, odd_diagonal)
    even2 = lax.ppermute(even_edge, "gy", even)
    odd2 = lax.ppermute(odd_edge, "gy", odd)
    d2, moments = pl.pallas_call(
        functools.partial(middle_kernel, by),
        out_shape=(vector(4), f32(8, 128)),
        in_specs=[vmem()] * 4,
        out_specs=(vmem(),) * 2,
        compiler_params=params(),
        cost_estimate=cost(24),
        name="middle_step",
    )(here(c0), here(c1), here(c2), here(diagonal))
    shares = [moments]
    for step in range(1, ny):
        shares.append(lax.ppermute(moments, "gy", [(i, i ^ step) for i in range(ny)]))

    c3, d3, c4 = pl.pallas_call(
        functools.partial(second_inner_kernel, by),
        out_shape=tuple(vector(h) for h in (3, 2, 1)),
        in_specs=[vmem()] * 3,
        out_specs=(vmem(),) * 3,
        compiler_params=params(),
        cost_estimate=cost(30),
        name="second_inner_steps",
    )(here(diagonal), here(c2), here(d2))
    vectors = [here(value) for value in (diagonal, c2, d2, c3, d3, c4)]
    c2, d2, c3, d3, c4 = pl.pallas_call(
        functools.partial(third_kernel, by),
        out_shape=tuple(vector(h) for h in (HALO, 4, 3, 2, 1)),
        in_specs=[smem()] + [vmem()] * 8,
        out_specs=(vmem(),) * 5,
        input_output_aliases={i + 2: i for i in range(5)},
        compiler_params=params(),
        cost_estimate=cost(20),
        name="third_steps",
    )(spot, *vectors, even2, odd2)
    inverse_count = 1.0 / (ny * cells)
    vectors = [here(value) for value in (c0, diagonal, d0, c1, d1, c2, d2, c3, d3, c4)]
    if group > count:
        cotangents = jnp.where(place < count, cotangents, 0.0)

    def last_step(flip):
        return pl.pallas_call(
            functools.partial(last_kernel, grid, inverse_count, flip),
            out_shape=stacked,
            in_specs=[smem(), smem()] + [vmem()] * (10 + ny),
            out_specs=vmem(),
            compiler_params=params(),
            cost_estimate=cost(20),
            name="last_step_given" if flip else "last_step_kept",
        )(spot, cotangents, *vectors, *shares)

    got = lax.ppermute(last_step(True), "core", swap)
    parts = plain(
        add_kernel, "add_cores", (block,) * chips, [smem(), vmem(), vmem()],
        spot, last_step(False), got,
    )
    parts = [parts[0]] + [to_chip(parts[k], k) for k in range(chips - 1, 0, -1)]
    return plain(
        functools.partial(sum_kernel, grid), "sum_chips", f32(bx, by, bz), [vmem()] * chips, *parts
    )


def solution(mesh):
    nx, ny, nz = (mesh.shape[axis] for axis in ("gx", "gy", "gz"))
    devices = mesh.devices.reshape(nx // 2, 2, ny, nz)
    split = jax.sharding.Mesh(devices, ("chip", "core", "gy", "gz"))
    gx = ("chip", "core")
    return jax.shard_map(
        body,
        mesh=split,
        in_specs=(P(None, gx, "gy", "gz"), P(gx, "gy", "gz"), P()),
        out_specs=P(gx, "gy", "gz"),
        check_vma=False,
    )
```

```python
import functools

import jax
import jax.numpy as jnp
from jax import lax
from jax.experimental import pallas as pl
from jax.experimental.pallas import tpu as pltpu
from jax.sharding import PartitionSpec as P

EPSILON = 1e-06
SHIFT = 64.0
HALO = 5
DIAGONAL_HALO = 4
PAD = 8
MIB = 1024 * 1024


def loss_of_moments(moments, weights):
    m0, m1, m2, m3, m4, m5 = moments
    norm = m0 + EPSILON
    alpha1 = (m1 + SHIFT * m0) / norm
    e1 = SHIFT - alpha1
    rest1 = jnp.maximum(m2 + 2.0 * e1 * m1 + e1 * e1 * m0, 0.0)
    beta1_square = rest1 / norm + EPSILON
    beta1 = jnp.sqrt(beta1_square)
    scale = 1.0 / (norm * beta1_square)
    alpha2 = scale * (m3 + 2.0 * e1 * m2 + e1 * e1 * m1 + SHIFT * rest1) - (m1 + e1 * m0) / norm
    e2 = SHIFT - alpha2
    f1 = e1 + e2
    f0 = e1 * e2 - beta1_square
    g = f1 * f1 + 2.0 * f0
    rest2 = jnp.maximum(m4 + 2.0 * f1 * m3 + g * m2 + 2.0 * f1 * f0 * m1 + f0 * f0 * m0, 0.0)
    beta2_square = scale * rest2 + EPSILON
    beta2 = jnp.sqrt(beta2_square)
    image2 = m5 + 2.0 * f1 * m4 + g * m3 + 2.0 * f1 * f0 * m2 + f0 * f0 * m1
    cross = m3 + f1 * m2 + f0 * m1 + e1 * (m2 + f1 * m1 + f0 * m0)
    alpha3 = scale * ((image2 + SHIFT * rest2) / beta2_square - cross)
    return (
        weights[0] * alpha1
        + weights[1] * alpha2
        + weights[2] * alpha3
        + weights[3] * beta1
        + weights[4] * beta2
    )


class Field:
    def __init__(self, ref, halo):
        self.ref = ref
        self.halo = halo
        self.columns, self.rows, self.pitch, _ = ref.shape
        self.cells = self.pitch - 2 * PAD

    def load(self, column, row, x):
        return self.ref[column, row + self.halo, pl.ds(PAD + x, 8), :]

    def store(self, column, row, x, value):
        self.ref[column, row + self.halo, pl.ds(PAD + x, 8), :] = value

    def clear_pads(self):
        zero = jnp.zeros((8, 128), jnp.float32)

        def body(at, carry):
            for column in range(self.columns):
                self.ref[column, at, pl.ds(0, PAD), :] = zero
                self.ref[column, at, pl.ds(PAD + self.cells, PAD), :] = zero
            return carry

        lax.fori_loop(0, self.rows, body, 0)

    def clear_row(self, row):
        zero = jnp.zeros((8, 128), jnp.float32)
        for column in range(self.columns):
            for x in range(0, self.cells, 8):
                self.store(column, row, x, zero)


def lane_masks():
    lane = lax.broadcasted_iota(jnp.int32, (8, 128), 1)
    return lane == 0, lane == 127


def stencil_block(source, diagonal, row, rows, x, masks):
    columns = range(source.columns)
    centre = {(r, c): source.load(c, row + r, x) for r in range(-1, rows + 1) for c in columns}
    results = []
    for r in range(rows):
        after = [pltpu.roll(centre[r, c], 1, 1) for c in columns]
        before = [pltpu.roll(centre[r, c], 127, 1) for c in columns]
        for c in columns:
            low = after[c - 1] if c else 0.0
            high = before[c + 1] if c + 1 < source.columns else 0.0
            total = jnp.where(masks[0], low, after[c]) + jnp.where(masks[1], high, before[c])
            total = total + (source.load(c, row + r, x - 1) + source.load(c, row + r, x + 1))
            total = total + (centre[r - 1, c] + centre[r + 1, c])
            value = diagonal.load(c, row + r, x) * centre[r, c] - total
            results.append((c, row + r, value))
    return results


def apply_block(target, source, diagonal, row, rows, minus, masks):
    for x in range(0, source.cells, 8):
        results = stencil_block(source, diagonal, row, rows, x, masks)
        if minus is not None:
            results = [(c, r, value - SHIFT * minus.load(c, r, x)) for c, r, value in results]
        for c, r, value in results:
            target.store(c, r, x, value)


def apply_rows(target, source, diagonal, first, count, minus=None, block=4):
    masks = lane_masks()

    def body(step, carry):
        apply_block(target, source, diagonal, step * block + first, block, minus, masks)
        return carry

    lax.fori_loop(0, count // block, body, 0)
    if count % block:
        start = first + count - count % block
        apply_block(target, source, diagonal, start, count % block, minus, masks)


def apply_strips(spot_ref, own, target, source, diagonal, halo, size, minus=None):
    masks = lane_masks()

    def body(step, carry):
        row = step * (own - size + 2 * halo) - halo
        apply_block(target, source, diagonal, row, size, minus, masks)
        return carry

    lax.fori_loop(0, 2, body, 0)
    clear_outside(spot_ref, own, target)


def clear_outside(spot_ref, own, field):
    @pl.when(spot_ref[0] == 1)
    def _():
        field.clear_row(-1)

    @pl.when(spot_ref[1] == 1)
    def _():
        field.clear_row(own)


def split_chip(grid, chip):
    nz = grid[1]
    return lax.div(chip, nz), lax.rem(chip, nz)


def pack_kappa_kernel(kappa_ref, out_ref, sem):
    copies = []
    for column in range(out_ref.shape[0]):
        part = kappa_ref.at[:, pl.ds(column * 128, 128)]
        copies.append(pltpu.make_async_copy(part, out_ref.at[column], sem.at[column]))
    for copy in copies:
        copy.start()
    for copy in copies:
        copy.wait()


def pack_probes_kernel(grid, count, spot_ref, after_ref, probes_ref, *rest):
    nx, nz, bx, by, bz = grid
    rows = bx * by
    outs, sem = rest[:-1], rest[-1]
    copies = []
    for k, out in enumerate(outs):
        x, z = split_chip(grid, spot_ref[4] ^ k)
        for core in range(2):
            start = pl.multiple_of(lax.rem((2 * x + core) * nz + z, count) * rows, rows)
            for column in range(bz // 128):
                part = probes_ref.at[pl.ds(start, rows), pl.ds(column * 128, 128)]
                copies.append(
                    pltpu.make_async_copy(part, out.at[core, column], sem.at[k, core, column])
                )
    for copy in copies:
        copy.start()
    for copy in copies:
        copy.wait()


def stack_kernel(after_ref, *refs):
    for k, ref in enumerate(refs[:-1]):
        refs[-1][k] = ref[...]


def sort_probes_kernel(spot_ref, after_ref, after_too_ref, *refs):
    parts, mine_ref, give_ref = refs[:-2], refs[-2], refs[-1]
    core = spot_ref[3]
    for k, part in enumerate(parts):
        mine_ref[k] = part[core]
        give_ref[k] = part[1 - core]


def block_rows(grid, spot_ref, mine_ref, other_ref, rows):
    nx, nz, bx, by, bz = grid
    per = bz // 128
    core = spot_ref[3]
    for k in range(nx // 2 * nz):
        x, z = split_chip(grid, spot_ref[4] ^ k)
        for ref, side in ((mine_ref, core), (other_ref, 1 - core)):
            for column in range(per):
                values = [ref[k, column, pl.ds(y, bx, stride=by), :] for y in rows]
                yield (2 * x + side) * bx, z * per + column, values


def store_own(field, x, z, values):
    for y, value in enumerate(values):
        at = pl.ds(pl.multiple_of(PAD + x, 8), 8)
        field.ref[z, y + field.halo, at, :] = value


def store_edges(spot_ref, one_ref, two_ref, x, z, first, last):
    at = pl.ds(pl.multiple_of(x, 8), 8)
    below_first = spot_ref[5] == 1
    for y, (below, above) in enumerate(zip(first, last)):
        one_ref[z, y, at, :] = jnp.where(below_first, below, above)
        two_ref[z, y, at, :] = jnp.where(below_first, above, below)


def edge_kernel(grid, spot_ref, mine_ref, other_ref, one_ref, two_ref):
    by = grid[3]
    rows = list(range(HALO)) + list(range(by - HALO, by))
    for x, z, values in block_rows(grid, spot_ref, mine_ref, other_ref, rows):
        store_edges(spot_ref, one_ref, two_ref, x, z, values[:HALO], values[HALO:])


def diagonal_kernel(grid, spot_ref, mine_ref, other_ref, own_ref, one_ref, two_ref):
    own = Field(own_ref, DIAGONAL_HALO)
    for x, z, values in block_rows(grid, spot_ref, mine_ref, other_ref, range(grid[3])):
        values = [6.0 + value for value in values]
        store_own(own, x, z, values)
        first, last = values[:DIAGONAL_HALO], values[-DIAGONAL_HALO:]
        store_edges(spot_ref, one_ref, two_ref, x, z, first, last)


def fill_halo(spot_ref, field, own, one_ref, two_ref):
    below_first = spot_ref[5] == 1
    for c in range(field.columns):
        for y in range(field.halo):
            for x in range(0, field.cells, 8):
                one, two = one_ref[c, y, pl.ds(x, 8), :], two_ref[c, y, pl.ds(x, 8), :]
                field.store(c, y - field.halo, x, jnp.where(below_first, one, two))
                field.store(c, own + y, x, jnp.where(below_first, two, one))


def inner_kernel(
    grid, spot_ref, mine_ref, other_ref, diagonal_ref, c0_ref, d0_ref, c1_ref, d1_ref, c2_ref
):
    own = grid[3]
    c0 = Field(c0_ref, HALO)
    diagonal = Field(diagonal_ref, DIAGONAL_HALO)
    d0 = Field(d0_ref, 4)
    c1 = Field(c1_ref, 3)
    d1 = Field(d1_ref, 2)
    c2 = Field(c2_ref, HALO)
    for field in (c0, d0, c1, d1, c2):
        field.clear_pads()
    for x, z, values in block_rows(grid, spot_ref, mine_ref, other_ref, range(own)):
        store_own(c0, x, z, values)
    apply_rows(d0, c0, diagonal, 1, own - 2)
    apply_rows(c1, d0, diagonal, 2, own - 4, c0)
    apply_rows(d1, c1, diagonal, 3, own - 6)
    apply_rows(c2, d1, diagonal, 4, own - 8, c1)


def first_kernel(
    own,
    spot_ref, c0_in, diagonal_in, d0_in, c1_in, d1_in, c2_in,
    one_ref, two_ref, one_diagonal_ref, two_diagonal_ref,
    c0_ref, diagonal_ref, d0_ref, c1_ref, d1_ref, c2_ref, one_out, two_out,
):
    c0 = Field(c0_ref, HALO)
    diagonal = Field(diagonal_ref, DIAGONAL_HALO)
    d0 = Field(d0_ref, 4)
    c1 = Field(c1_ref, 3)
    d1 = Field(d1_ref, 2)
    c2 = Field(c2_ref, HALO)
    fill_halo(spot_ref, c0, own, one_ref, two_ref)
    fill_halo(spot_ref, diagonal, own, one_diagonal_ref, two_diagonal_ref)
    strips = functools.partial(apply_strips, spot_ref, own)
    strips(d0, c0, diagonal, 4, HALO)
    strips(c1, d0, diagonal, 3, HALO, c0)
    strips(d1, c1, diagonal, 2, HALO)
    strips(c2, d1, diagonal, 1, HALO, c1)
    for c in range(c2.columns):
        for x in range(0, c2.cells, 8):
            first = [c2.load(c, y, x) for y in range(HALO)]
            last = [c2.load(c, own - HALO + y, x) for y in range(HALO)]
            store_edges(spot_ref, one_out, two_out, x, c, first, last)


def middle_kernel(own, c0_ref, c1_ref, c2_ref, diagonal_ref, d2_ref, moments_ref):
    c0 = Field(c0_ref, HALO)
    diagonal = Field(diagonal_ref, DIAGONAL_HALO)
    c1 = Field(c1_ref, 3)
    c2 = Field(c2_ref, HALO)
    d2 = Field(d2_ref, 4)
    d2.clear_pads()
    apply_rows(d2, c2, diagonal, 0, own)

    def moment_row(row, sums):
        for x in range(0, c0.cells, 8):
            for c in range(c0.columns):
                a, b, e, d = (field.load(c, row, x) for field in (c0, c1, c2, d2))
                pairs = ((a, a), (a, b), (b, b), (b, e), (e, e), (d, d))
                sums = tuple(total + u * v for total, (u, v) in zip(sums, pairs))
        return sums

    zero = jnp.zeros((8, 128), jnp.float32)
    sums = lax.fori_loop(0, own, moment_row, (zero,) * 6)
    sums = [jnp.sum(total, axis=0, keepdims=True) for total in sums]
    moments_ref[...] = jnp.concatenate(sums + [zero[:2]], axis=0)


def moment_slopes(inverse_count, probe, weights_ref, moment_refs):
    total = moment_refs[0][...]
    for ref in moment_refs[1:]:
        total = total + ref[...]
    total = jnp.sum(total, axis=1, keepdims=True) * inverse_count
    raw = [jnp.broadcast_to(total[k : k + 1], (8, 128)) for k in range(6)]
    moments = tuple(raw[:5]) + (raw[5] - SHIFT * raw[4],)
    weights = [weights_ref[k, probe] for k in range(5)]
    value, pullback = jax.vjp(lambda m: loss_of_moments(m, weights), moments)
    (slopes,) = pullback(jnp.full((8, 128), 2.0, jnp.float32))
    return [slope[0, 0] for slope in slopes]


def second_inner_kernel(own, diagonal_ref, c2_ref, d2_ref, c3_ref, d3_ref, c4_ref):
    diagonal = Field(diagonal_ref, DIAGONAL_HALO)
    c2 = Field(c2_ref, HALO)
    d2 = Field(d2_ref, 4)
    c3 = Field(c3_ref, 3)
    d3 = Field(d3_ref, 2)
    c4 = Field(c4_ref, 1)
    for field in (c3, d3, c4):
        field.clear_pads()
    apply_rows(c3, d2, diagonal, 1, own - 2, c2)
    apply_rows(d3, c3, diagonal, 2, own - 4)
    apply_rows(c4, d3, diagonal, 3, own - 6, c3)


def third_kernel(
    own,
    spot_ref, diagonal_ref, c2_in, d2_in, c3_in, d3_in, c4_in, one_ref, two_ref,
    c2_ref, d2_ref, c3_ref, d3_ref, c4_ref,
):
    diagonal = Field(diagonal_ref, DIAGONAL_HALO)
    c2 = Field(c2_ref, HALO)
    d2 = Field(d2_ref, 4)
    c3 = Field(c3_ref, 3)
    d3 = Field(d3_ref, 2)
    c4 = Field(c4_ref, 1)
    fill_halo(spot_ref, c2, own, one_ref, two_ref)
    strips = functools.partial(apply_strips, spot_ref, own)
    strips(d2, c2, diagonal, 4, 4)
    strips(c3, d2, diagonal, 3, 4, c2)
    strips(d3, c3, diagonal, 2, 4)
    strips(c4, d3, diagonal, 1, 4, c3)


def last_kernel(
    grid, inverse_count, flip,
    spot_ref, weights_ref, c0_ref, diagonal_ref, d0_ref, c1_ref, d1_ref,
    c2_ref, d2_ref, c3_ref, d3_ref, c4_ref, *rest,
):
    nx, nz, bx, by, bz = grid
    per = bz // 128
    moment_refs, out_ref = rest[:-1], rest[-1]
    c0 = Field(c0_ref, HALO)
    diagonal = Field(diagonal_ref, DIAGONAL_HALO)
    d0 = Field(d0_ref, 4)
    c1 = Field(c1_ref, 3)
    d1 = Field(d1_ref, 2)
    c2 = Field(c2_ref, HALO)
    d2 = Field(d2_ref, 4)
    c3 = Field(c3_ref, 3)
    d3 = Field(d3_ref, 2)
    c4 = Field(c4_ref, 1)
    slopes = moment_slopes(inverse_count, spot_ref[2], weights_ref, moment_refs)
    masks = lane_masks()
    block = 2

    def out_rows(core, step, carry):
        row = step * block
        for chip in range(nx // 2):
            x = (2 * chip + core) * bx
            results = []
            for z, at, d4 in stencil_block(c4, diagonal, row, block, x, masks):
                cs = [field.load(z, at, x) for field in (c0, c1, c2, c3, c4)]
                ds = [field.load(z, at, x) for field in (d0, d1, d2, d3)] + [d4]
                total = None
                for i in range(5):
                    inner = None
                    for j in range(5 - i):
                        term = slopes[i + j + 1] * ds[j]
                        inner = term if inner is None else inner + term
                    term = cs[i] * inner
                    total = term if total is None else total + term
                results.append((chip * nz + z // per, z % per, at, total))
            for place, column, at, total in results:
                out_ref[place, column, pl.ds(at, bx, stride=by), :] = total
        return carry

    for core in range(2):

        @pl.when(spot_ref[3] == (1 - core if flip else core))
        def _():
            lax.fori_loop(0, by // block, functools.partial(out_rows, core), 0)


def add_kernel(spot_ref, kept_ref, got_ref, *outs):
    for k, out in enumerate(outs):
        chip = spot_ref[4] ^ k
        out[...] = kept_ref[chip] + got_ref[chip]


def sum_kernel(grid, *refs):
    nx, nz, bx, by, bz = grid
    parts, out_ref = refs[:-1], refs[-1]
    for column in range(bz // 128):
        for x in range(bx):
            total = None
            for ref in parts:
                part = ref[column, pl.ds(x * by, by), :]
                total = part if total is None else total + part
            out_ref[x, :, pl.ds(column * 128, 128)] = total


def vmem():
    return pl.BlockSpec(memory_space=pltpu.VMEM)


def smem():
    return pl.BlockSpec(memory_space=pltpu.SMEM)


def hbm():
    return pl.BlockSpec(memory_space=pltpu.HBM)


def here(value):
    return pltpu.with_memory_space_constraint(value, pltpu.VMEM)


def there(value):
    return pltpu.with_memory_space_constraint(value, pltpu.HBM)


def f32(*shape):
    return jax.ShapeDtypeStruct(shape, jnp.float32)


def params():
    return pltpu.CompilerParams(vmem_limit_bytes=12 * MIB)


def body(probes, kappa2, cotangents):
    nx, ny, nz = (lax.axis_size(axis) for axis in (("chip", "core"), "gy", "gz"))
    count, bx, by, bz = probes.shape
    group = nx * nz
    assert group % count == 0 and nx % 2 == 0 and bx == 8 and bz == 256
    assert by % 8 == 0 and by >= HALO
    X = nx * bx
    columns = nz * bz // 128
    per = bz // 128
    rows = bx * by
    grid = (nx, nz, bx, by, bz)
    core, gy = lax.axis_index("core"), lax.axis_index("gy")
    place = (lax.axis_index("chip") * 2 + core) * nz + lax.axis_index("gz")
    mine = place % count
    assert ny & (ny - 1) == 0
    even = [(i, i ^ 1) for i in range(ny)]
    odd = [(i, i + 1 if i % 2 else i - 1) for i in range(1, ny - 1)]

    def both_cores(first, second):
        return first + [(ny + i, ny + j) for i, j in second]

    first_pairs, second_pairs = both_cores(even, odd), both_cores(odd, even)
    swap = [(0, 1), (1, 0)]

    def edge(halo):
        return f32(columns, halo, X, 128)

    def padded(halo):
        return (columns, by + 2 * halo, X + 2 * PAD, 128)

    def vector(halo):
        return pltpu.VMEM(padded(halo), jnp.float32)

    chips = nx // 2 * nz
    assert chips & (chips - 1) == 0
    chip = lax.axis_index("chip") * nz + lax.axis_index("gz")
    spot = jnp.stack([gy == 0, gy == ny - 1, mine, core, chip, (gy + core) % 2]).astype(jnp.int32)

    def to_chip(value, k):
        pairs = [(i, i ^ k) for i in range(chips)]
        return lax.ppermute(value, ("chip", "gz"), pairs)

    def plain(kernel, name, out_shape, specs, *operands, **options):
        return pl.pallas_call(
            kernel,
            out_shape=out_shape,
            in_specs=specs,
            out_specs=(vmem(),) * len(out_shape) if isinstance(out_shape, tuple) else vmem(),
            compiler_params=params(),
            name=name,
            **options,
        )(*operands)

    dma = pltpu.SemaphoreType.DMA
    block = f32(per, rows, 128)
    stacked = f32(chips, per, rows, 128)
    kappa = plain(
        pack_kappa_kernel, "pack_kappa", block, [hbm()], there(kappa2.reshape(rows, bz)),
        scratch_shapes=[dma((per,))],
    )
    kappas = [kappa] + [to_chip(kappa, k) for k in range(1, chips)]
    packed = plain(
        functools.partial(pack_probes_kernel, grid, count), "pack_probes",
        (f32(2, per, rows, 128),) * chips, [smem(), vmem(), hbm()],
        spot, kappa, there(probes.reshape(count * rows, bz)), scratch_shapes=[dma((chips, 2, per))],
    )
    probes = [packed[0]] + [to_chip(packed[k], k) for k in range(1, chips)]

    kappa = plain(
        stack_kernel, "stack_kappa", stacked,
        [vmem()] * (chips + 1), packed[0], *kappas,
    )
    other = lax.ppermute(kappa, "core", swap)
    diagonal, one_edge, two_edge = plain(
        functools.partial(diagonal_kernel, grid), "diagonal_rows",
        (vector(DIAGONAL_HALO), edge(DIAGONAL_HALO), edge(DIAGONAL_HALO)),
        [smem(), vmem(), vmem()], spot, kappa, other,
    )
    one_diagonal = lax.ppermute(one_edge, ("core", "gy"), first_pairs)
    two_diagonal = lax.ppermute(two_edge, ("core", "gy"), second_pairs)

    probe, give = plain(
        sort_probes_kernel, "sort_probes", (stacked, stacked),
        [smem()] + [vmem()] * (chips + 2), spot, one_diagonal, two_diagonal, *probes,
    )
    other = lax.ppermute(give, "core", swap)
    one_edge, two_edge = plain(
        functools.partial(edge_kernel, grid), "probe_edges", (edge(HALO), edge(HALO)),
        [smem(), vmem(), vmem()], spot, probe, other,
    )
    one1 = lax.ppermute(one_edge, ("core", "gy"), first_pairs)
    two1 = lax.ppermute(two_edge, ("core", "gy"), second_pairs)

    cells = by * X * columns * 128

    def cost(operations):
        return pl.CostEstimate(
            flops=operations * cells, bytes_accessed=16 * cells, transcendentals=0
        )

    inner = pl.pallas_call(
        functools.partial(inner_kernel, grid),
        out_shape=tuple(vector(h) for h in (HALO, 4, 3, 2, HALO)),
        in_specs=[smem()] + [vmem()] * 3,
        out_specs=(vmem(),) * 5,
        compiler_params=params(),
        cost_estimate=cost(32),
        name="inner_steps",
    )(spot, probe, other, here(diagonal))
    vectors = [here(value) for value in (inner[0], diagonal) + tuple(inner[1:])]
    c0, diagonal, d0, c1, d1, c2, one_edge, two_edge = pl.pallas_call(
        functools.partial(first_kernel, by),
        out_shape=tuple(vector(h) for h in (HALO, DIAGONAL_HALO, 4, 3, 2, HALO))
        + (edge(HALO), edge(HALO)),
        in_specs=[smem()] + [vmem()] * 10,
        out_specs=(vmem(),) * 8,
        input_output_aliases={i + 1: i for i in range(6)},
        compiler_params=params(),
        name="first_steps",
    )(spot, *vectors, one1, two1, one_diagonal, two_diagonal)
    one2 = lax.ppermute(one_edge, ("core", "gy"), first_pairs)
    two2 = lax.ppermute(two_edge, ("core", "gy"), second_pairs)
    d2, moments = pl.pallas_call(
        functools.partial(middle_kernel, by),
        out_shape=(vector(4), f32(8, 128)),
        in_specs=[vmem()] * 4,
        out_specs=(vmem(),) * 2,
        compiler_params=params(),
        cost_estimate=cost(24),
        name="middle_step",
    )(here(c0), here(c1), here(c2), here(diagonal))
    shares = [moments]
    for step in range(1, ny):
        shares.append(lax.ppermute(moments, "gy", [(i, i ^ step) for i in range(ny)]))

    c3, d3, c4 = pl.pallas_call(
        functools.partial(second_inner_kernel, by),
        out_shape=tuple(vector(h) for h in (3, 2, 1)),
        in_specs=[vmem()] * 3,
        out_specs=(vmem(),) * 3,
        compiler_params=params(),
        cost_estimate=cost(30),
        name="second_inner_steps",
    )(here(diagonal), here(c2), here(d2))
    vectors = [here(value) for value in (diagonal, c2, d2, c3, d3, c4)]
    c2, d2, c3, d3, c4 = pl.pallas_call(
        functools.partial(third_kernel, by),
        out_shape=tuple(vector(h) for h in (HALO, 4, 3, 2, 1)),
        in_specs=[smem()] + [vmem()] * 8,
        out_specs=(vmem(),) * 5,
        input_output_aliases={i + 2: i for i in range(5)},
        compiler_params=params(),
        cost_estimate=cost(20),
        name="third_steps",
    )(spot, *vectors, one2, two2)
    inverse_count = 1.0 / (ny * cells)
    vectors = [here(value) for value in (c0, diagonal, d0, c1, d1, c2, d2, c3, d3, c4)]
    if group > count:
        cotangents = jnp.where(place < count, cotangents, 0.0)

    def last_step(flip):
        return pl.pallas_call(
            functools.partial(last_kernel, grid, inverse_count, flip),
            out_shape=stacked,
            in_specs=[smem(), smem()] + [vmem()] * (10 + ny),
            out_specs=vmem(),
            compiler_params=params(),
            cost_estimate=cost(20),
            name="last_step_given" if flip else "last_step_kept",
        )(spot, cotangents, *vectors, *shares)

    got = lax.ppermute(last_step(True), "core", swap)
    parts = plain(
        add_kernel, "add_cores", (block,) * chips, [smem(), vmem(), vmem()],
        spot, last_step(False), got,
    )
    parts = [parts[0]] + [to_chip(parts[k], k) for k in range(chips - 1, 0, -1)]
    return plain(
        functools.partial(sum_kernel, grid), "sum_chips", f32(bx, by, bz), [vmem()] * chips, *parts
    )


def solution(mesh):
    nx, ny, nz = (mesh.shape[axis] for axis in ("gx", "gy", "gz"))
    devices = mesh.devices.reshape(nx // 2, 2, ny, nz)
    split = jax.sharding.Mesh(devices, ("chip", "core", "gy", "gz"))
    gx = ("chip", "core")
    return jax.shard_map(
        body,
        mesh=split,
        in_specs=(P(None, gx, "gy", "gz"), P(gx, "gy", "gz"), P()),
        out_specs=P(gx, "gy", "gz"),
        check_vma=False,
    )
```

```python
import functools

import jax
import jax.numpy as jnp
from jax import lax
from jax.experimental import pallas as pl
from jax.experimental.pallas import tpu as pltpu
from jax.sharding import PartitionSpec as P

EPSILON = 1e-06
SHIFT = 64.0
HALO = 5
DIAGONAL_HALO = 4
PAD = 8
MIB = 1024 * 1024


def loss_of_moments(moments, weights):
    m0, m1, m2, m3, m4, m5 = moments
    norm = m0 + EPSILON
    alpha1 = (m1 + SHIFT * m0) / norm
    e1 = SHIFT - alpha1
    rest1 = jnp.maximum(m2 + 2.0 * e1 * m1 + e1 * e1 * m0, 0.0)
    beta1_square = rest1 / norm + EPSILON
    beta1 = jnp.sqrt(beta1_square)
    scale = 1.0 / (norm * beta1_square)
    alpha2 = scale * (m3 + 2.0 * e1 * m2 + e1 * e1 * m1 + SHIFT * rest1) - (m1 + e1 * m0) / norm
    e2 = SHIFT - alpha2
    f1 = e1 + e2
    f0 = e1 * e2 - beta1_square
    g = f1 * f1 + 2.0 * f0
    rest2 = jnp.maximum(m4 + 2.0 * f1 * m3 + g * m2 + 2.0 * f1 * f0 * m1 + f0 * f0 * m0, 0.0)
    beta2_square = scale * rest2 + EPSILON
    beta2 = jnp.sqrt(beta2_square)
    image2 = m5 + 2.0 * f1 * m4 + g * m3 + 2.0 * f1 * f0 * m2 + f0 * f0 * m1
    cross = m3 + f1 * m2 + f0 * m1 + e1 * (m2 + f1 * m1 + f0 * m0)
    alpha3 = scale * ((image2 + SHIFT * rest2) / beta2_square - cross)
    return (
        weights[0] * alpha1
        + weights[1] * alpha2
        + weights[2] * alpha3
        + weights[3] * beta1
        + weights[4] * beta2
    )


class Field:
    def __init__(self, ref, halo):
        self.ref = ref
        self.halo = halo
        self.columns, self.rows, self.pitch, _ = ref.shape
        self.cells = self.pitch - 2 * PAD

    def load(self, column, row, x):
        return self.ref[column, row + self.halo, pl.ds(PAD + x, 8), :]

    def store(self, column, row, x, value):
        self.ref[column, row + self.halo, pl.ds(PAD + x, 8), :] = value

    def clear_pads(self):
        zero = jnp.zeros((8, 128), jnp.float32)

        def body(at, carry):
            for column in range(self.columns):
                self.ref[column, at, pl.ds(0, PAD), :] = zero
                self.ref[column, at, pl.ds(PAD + self.cells, PAD), :] = zero
            return carry

        lax.fori_loop(0, self.rows, body, 0)

    def clear_row(self, row):
        zero = jnp.zeros((8, 128), jnp.float32)
        for column in range(self.columns):
            for x in range(0, self.cells, 8):
                self.store(column, row, x, zero)


def lane_masks():
    lane = lax.broadcasted_iota(jnp.int32, (8, 128), 1)
    return lane == 0, lane == 127


def stencil_block(source, diagonal, row, rows, x, masks):
    columns = range(source.columns)
    centre = {(r, c): source.load(c, row + r, x) for r in range(-1, rows + 1) for c in columns}
    results = []
    for r in range(rows):
        after = [pltpu.roll(centre[r, c], 1, 1) for c in columns]
        before = [pltpu.roll(centre[r, c], 127, 1) for c in columns]
        for c in columns:
            low = after[c - 1] if c else 0.0
            high = before[c + 1] if c + 1 < source.columns else 0.0
            total = jnp.where(masks[0], low, after[c]) + jnp.where(masks[1], high, before[c])
            total = total + (source.load(c, row + r, x - 1) + source.load(c, row + r, x + 1))
            total = total + (centre[r - 1, c] + centre[r + 1, c])
            value = diagonal.load(c, row + r, x) * centre[r, c] - total
            results.append((c, row + r, value))
    return results


def apply_block(target, source, diagonal, row, rows, minus, masks):
    for x in range(0, source.cells, 8):
        results = stencil_block(source, diagonal, row, rows, x, masks)
        if minus is not None:
            results = [(c, r, value - SHIFT * minus.load(c, r, x)) for c, r, value in results]
        for c, r, value in results:
            target.store(c, r, x, value)


def apply_rows(target, source, diagonal, first, count, minus=None, block=4):
    masks = lane_masks()

    def body(step, carry):
        apply_block(target, source, diagonal, step * block + first, block, minus, masks)
        return carry

    lax.fori_loop(0, count // block, body, 0)
    if count % block:
        start = first + count - count % block
        apply_block(target, source, diagonal, start, count % block, minus, masks)


def apply_strips(spot_ref, own, target, source, diagonal, halo, size, minus=None):
    masks = lane_masks()

    def body(step, carry):
        row = step * (own - size + 2 * halo) - halo
        apply_block(target, source, diagonal, row, size, minus, masks)
        return carry

    lax.fori_loop(0, 2, body, 0)
    clear_outside(spot_ref, own, target)


def clear_outside(spot_ref, own, field):
    @pl.when(spot_ref[0] == 1)
    def _():
        field.clear_row(-1)

    @pl.when(spot_ref[1] == 1)
    def _():
        field.clear_row(own)


def split_chip(grid, chip):
    nz = grid[1]
    return lax.div(chip, nz), lax.rem(chip, nz)


def pack_kappa_kernel(kappa_ref, out_ref, sem):
    copies = []
    for column in range(out_ref.shape[0]):
        part = kappa_ref.at[:, pl.ds(column * 128, 128)]
        copies.append(pltpu.make_async_copy(part, out_ref.at[column], sem.at[column]))
    for copy in copies:
        copy.start()
    for copy in copies:
        copy.wait()


def pack_probes_kernel(grid, count, spot_ref, after_ref, probes_ref, *rest):
    nx, nz, bx, by, bz = grid
    rows = bx * by
    outs, sem = rest[:-1], rest[-1]
    copies = []
    for k, out in enumerate(outs):
        x, z = split_chip(grid, spot_ref[4] ^ k)
        for core in range(2):
            start = pl.multiple_of(lax.rem((2 * x + core) * nz + z, count) * rows, rows)
            for column in range(bz // 128):
                part = probes_ref.at[pl.ds(start, rows), pl.ds(column * 128, 128)]
                copies.append(
                    pltpu.make_async_copy(part, out.at[core, column], sem.at[k, core, column])
                )
    for copy in copies:
        copy.start()
    for copy in copies:
        copy.wait()


def stack_kernel(after_ref, *refs):
    for k, ref in enumerate(refs[:-1]):
        refs[-1][k] = ref[...]


def sort_probes_kernel(spot_ref, after_ref, after_too_ref, *refs):
    parts, mine_ref, give_ref = refs[:-2], refs[-2], refs[-1]
    core = spot_ref[3]
    for k, part in enumerate(parts):
        mine_ref[k] = part[core]
        give_ref[k] = part[1 - core]


def block_rows(grid, spot_ref, mine_ref, other_ref, rows):
    nx, nz, bx, by, bz = grid
    per = bz // 128
    core = spot_ref[3]
    for k in range(nx // 2 * nz):
        x, z = split_chip(grid, spot_ref[4] ^ k)
        for ref, side in ((mine_ref, core), (other_ref, 1 - core)):
            for column in range(per):
                values = [ref[k, column, pl.ds(y, bx, stride=by), :] for y in rows]
                yield (2 * x + side) * bx, z * per + column, values


def store_own(field, x, z, values):
    for y, value in enumerate(values):
        at = pl.ds(pl.multiple_of(PAD + x, 8), 8)
        field.ref[z, y + field.halo, at, :] = value


def store_edges(spot_ref, even_ref, odd_ref, x, z, first, last):
    at = pl.ds(pl.multiple_of(x, 8), 8)
    odd = spot_ref[5] == 1
    for y, (below, above) in enumerate(zip(first, last)):
        even_ref[z, y, at, :] = jnp.where(odd, below, above)
        odd_ref[z, y, at, :] = jnp.where(odd, above, below)


def edge_kernel(grid, spot_ref, mine_ref, other_ref, even_ref, odd_ref):
    by = grid[3]
    rows = list(range(HALO)) + list(range(by - HALO, by))
    for x, z, values in block_rows(grid, spot_ref, mine_ref, other_ref, rows):
        store_edges(spot_ref, even_ref, odd_ref, x, z, values[:HALO], values[HALO:])


def diagonal_kernel(grid, spot_ref, mine_ref, other_ref, own_ref, even_ref, odd_ref):
    own = Field(own_ref, DIAGONAL_HALO)
    for x, z, values in block_rows(grid, spot_ref, mine_ref, other_ref, range(grid[3])):
        values = [6.0 + value for value in values]
        store_own(own, x, z, values)
        first, last = values[:DIAGONAL_HALO], values[-DIAGONAL_HALO:]
        store_edges(spot_ref, even_ref, odd_ref, x, z, first, last)


def fill_halo(spot_ref, field, own, even_ref, odd_ref):
    odd = spot_ref[5] == 1
    for c in range(field.columns):
        for y in range(field.halo):
            for x in range(0, field.cells, 8):
                even, other = even_ref[c, y, pl.ds(x, 8), :], odd_ref[c, y, pl.ds(x, 8), :]
                field.store(c, y - field.halo, x, jnp.where(odd, even, other))
                field.store(c, own + y, x, jnp.where(odd, other, even))


def inner_kernel(
    grid, spot_ref, mine_ref, other_ref, diagonal_ref, c0_ref, d0_ref, c1_ref, d1_ref, c2_ref
):
    own = grid[3]
    c0 = Field(c0_ref, HALO)
    diagonal = Field(diagonal_ref, DIAGONAL_HALO)
    d0 = Field(d0_ref, 4)
    c1 = Field(c1_ref, 3)
    d1 = Field(d1_ref, 2)
    c2 = Field(c2_ref, HALO)
    for field in (c0, d0, c1, d1, c2):
        field.clear_pads()
    for x, z, values in block_rows(grid, spot_ref, mine_ref, other_ref, range(own)):
        store_own(c0, x, z, values)
    apply_rows(d0, c0, diagonal, 1, own - 2)
    apply_rows(c1, d0, diagonal, 2, own - 4, c0)
    apply_rows(d1, c1, diagonal, 3, own - 6)
    apply_rows(c2, d1, diagonal, 4, own - 8, c1)


def side_kernel(
    own, which,
    spot_ref, c0_in, diagonal_in, d0_in, c1_in, d1_in, c2_in, halo_ref, halo_diagonal_ref,
    c0_ref, diagonal_ref, d0_ref, c1_ref, d1_ref, c2_ref, edge_out,
):
    c0 = Field(c0_ref, HALO)
    diagonal = Field(diagonal_ref, DIAGONAL_HALO)
    d0 = Field(d0_ref, 4)
    c1 = Field(c1_ref, 3)
    d1 = Field(d1_ref, 2)
    c2 = Field(c2_ref, HALO)
    masks = lane_masks()
    above = jnp.where(spot_ref[5] == which, 1, 0)
    for field, ref in ((c0, halo_ref), (diagonal, halo_diagonal_ref)):
        base = above * (own + field.halo)
        for c in range(field.columns):
            for y in range(field.halo):
                for x in range(0, field.cells, 8):
                    field.store(c, base + (y - field.halo), x, ref[c, y, pl.ds(x, 8), :])

    def strip(target, source, halo, minus=None):
        row = above * (own - HALO + 2 * halo) - halo
        apply_block(target, source, diagonal, row, HALO, minus, masks)
        clear_outside(spot_ref, own, target)

    strip(d0, c0, 4)
    strip(c1, d0, 3, c0)
    strip(d1, c1, 2)
    strip(c2, d1, 1, c1)
    base = above * (own - HALO)
    for c in range(c2.columns):
        for x in range(0, c2.cells, 8):
            for y in range(HALO):
                edge_out[c, y, pl.ds(x, 8), :] = c2.load(c, base + y, x)


def middle_kernel(own, c0_ref, c1_ref, c2_ref, diagonal_ref, d2_ref, moments_ref):
    c0 = Field(c0_ref, HALO)
    diagonal = Field(diagonal_ref, DIAGONAL_HALO)
    c1 = Field(c1_ref, 3)
    c2 = Field(c2_ref, HALO)
    d2 = Field(d2_ref, 4)
    d2.clear_pads()
    apply_rows(d2, c2, diagonal, 0, own)

    def moment_row(row, sums):
        for x in range(0, c0.cells, 8):
            for c in range(c0.columns):
                a, b, e, d = (field.load(c, row, x) for field in (c0, c1, c2, d2))
                pairs = ((a, a), (a, b), (b, b), (b, e), (e, e), (d, d))
                sums = tuple(total + u * v for total, (u, v) in zip(sums, pairs))
        return sums

    zero = jnp.zeros((8, 128), jnp.float32)
    sums = lax.fori_loop(0, own, moment_row, (zero,) * 6)
    sums = [jnp.sum(total, axis=0, keepdims=True) for total in sums]
    moments_ref[...] = jnp.concatenate(sums + [zero[:2]], axis=0)


def moment_slopes(inverse_count, probe, weights_ref, moment_refs):
    total = moment_refs[0][...]
    for ref in moment_refs[1:]:
        total = total + ref[...]
    total = jnp.sum(total, axis=1, keepdims=True) * inverse_count
    raw = [jnp.broadcast_to(total[k : k + 1], (8, 128)) for k in range(6)]
    moments = tuple(raw[:5]) + (raw[5] - SHIFT * raw[4],)
    weights = [weights_ref[k, probe] for k in range(5)]
    value, pullback = jax.vjp(lambda m: loss_of_moments(m, weights), moments)
    (slopes,) = pullback(jnp.full((8, 128), 2.0, jnp.float32))
    return [slope[0, 0] for slope in slopes]


def second_inner_kernel(own, diagonal_ref, c2_ref, d2_ref, c3_ref, d3_ref, c4_ref):
    diagonal = Field(diagonal_ref, DIAGONAL_HALO)
    c2 = Field(c2_ref, HALO)
    d2 = Field(d2_ref, 4)
    c3 = Field(c3_ref, 3)
    d3 = Field(d3_ref, 2)
    c4 = Field(c4_ref, 1)
    for field in (c3, d3, c4):
        field.clear_pads()
    apply_rows(c3, d2, diagonal, 1, own - 2, c2)
    apply_rows(d3, c3, diagonal, 2, own - 4)
    apply_rows(c4, d3, diagonal, 3, own - 6, c3)


def third_kernel(
    own,
    spot_ref, diagonal_ref, c2_in, d2_in, c3_in, d3_in, c4_in, even_ref, odd_ref,
    c2_ref, d2_ref, c3_ref, d3_ref, c4_ref,
):
    diagonal = Field(diagonal_ref, DIAGONAL_HALO)
    c2 = Field(c2_ref, HALO)
    d2 = Field(d2_ref, 4)
    c3 = Field(c3_ref, 3)
    d3 = Field(d3_ref, 2)
    c4 = Field(c4_ref, 1)
    fill_halo(spot_ref, c2, own, even_ref, odd_ref)
    strips = functools.partial(apply_strips, spot_ref, own)
    strips(d2, c2, diagonal, 4, 4)
    strips(c3, d2, diagonal, 3, 4, c2)
    strips(d3, c3, diagonal, 2, 4)
    strips(c4, d3, diagonal, 1, 4, c3)


def last_kernel(
    grid, inverse_count, flip,
    spot_ref, weights_ref, c0_ref, diagonal_ref, d0_ref, c1_ref, d1_ref,
    c2_ref, d2_ref, c3_ref, d3_ref, c4_ref, *rest,
):
    nx, nz, bx, by, bz = grid
    per = bz // 128
    moment_refs, out_ref = rest[:-1], rest[-1]
    c0 = Field(c0_ref, HALO)
    diagonal = Field(diagonal_ref, DIAGONAL_HALO)
    d0 = Field(d0_ref, 4)
    c1 = Field(c1_ref, 3)
    d1 = Field(d1_ref, 2)
    c2 = Field(c2_ref, HALO)
    d2 = Field(d2_ref, 4)
    c3 = Field(c3_ref, 3)
    d3 = Field(d3_ref, 2)
    c4 = Field(c4_ref, 1)
    slopes = moment_slopes(inverse_count, spot_ref[2], weights_ref, moment_refs)
    masks = lane_masks()
    block = 2

    def out_rows(core, step, carry):
        row = step * block
        for chip in range(nx // 2):
            x = (2 * chip + core) * bx
            results = []
            for z, at, d4 in stencil_block(c4, diagonal, row, block, x, masks):
                cs = [field.load(z, at, x) for field in (c0, c1, c2, c3, c4)]
                ds = [field.load(z, at, x) for field in (d0, d1, d2, d3)] + [d4]
                total = None
                for i in range(5):
                    inner = None
                    for j in range(5 - i):
                        term = slopes[i + j + 1] * ds[j]
                        inner = term if inner is None else inner + term
                    term = cs[i] * inner
                    total = term if total is None else total + term
                results.append((chip * nz + z // per, z % per, at, total))
            for place, column, at, total in results:
                out_ref[place, column, pl.ds(at, bx, stride=by), :] = total
        return carry

    for core in range(2):

        @pl.when(spot_ref[3] == (1 - core if flip else core))
        def _():
            lax.fori_loop(0, by // block, functools.partial(out_rows, core), 0)


def add_kernel(spot_ref, kept_ref, got_ref, *outs):
    for k, out in enumerate(outs):
        chip = spot_ref[4] ^ k
        out[...] = kept_ref[chip] + got_ref[chip]


def sum_kernel(grid, *refs):
    nx, nz, bx, by, bz = grid
    parts, out_ref = refs[:-1], refs[-1]
    for column in range(bz // 128):
        for x in range(bx):
            total = None
            for ref in parts:
                part = ref[column, pl.ds(x * by, by), :]
                total = part if total is None else total + part
            out_ref[x, :, pl.ds(column * 128, 128)] = total


def vmem():
    return pl.BlockSpec(memory_space=pltpu.VMEM)


def smem():
    return pl.BlockSpec(memory_space=pltpu.SMEM)


def hbm():
    return pl.BlockSpec(memory_space=pltpu.HBM)


def here(value):
    return pltpu.with_memory_space_constraint(value, pltpu.VMEM)


def there(value):
    return pltpu.with_memory_space_constraint(value, pltpu.HBM)


def f32(*shape):
    return jax.ShapeDtypeStruct(shape, jnp.float32)


def params():
    return pltpu.CompilerParams(vmem_limit_bytes=12 * MIB)


def body(probes, kappa2, cotangents):
    nx, ny, nz = (lax.axis_size(axis) for axis in (("chip", "core"), "gy", "gz"))
    count, bx, by, bz = probes.shape
    group = nx * nz
    assert group % count == 0 and nx % 2 == 0 and bx == 8 and bz == 256
    assert by % 8 == 0 and by >= HALO
    X = nx * bx
    columns = nz * bz // 128
    per = bz // 128
    rows = bx * by
    grid = (nx, nz, bx, by, bz)
    core, gy = lax.axis_index("core"), lax.axis_index("gy")
    place = (lax.axis_index("chip") * 2 + core) * nz + lax.axis_index("gz")
    mine = place % count
    assert ny & (ny - 1) == 0
    even = [(i, i ^ 1) for i in range(ny)]
    odd = [(i, i + 1 if i % 2 else i - 1) for i in range(1, ny - 1)]
    swap = [(0, 1), (1, 0)]

    def edge(halo):
        return f32(columns, halo, X, 128)

    def padded(halo):
        return (columns, by + 2 * halo, X + 2 * PAD, 128)

    def vector(halo):
        return pltpu.VMEM(padded(halo), jnp.float32)

    chips = nx // 2 * nz
    assert chips & (chips - 1) == 0
    chip = lax.axis_index("chip") * nz + lax.axis_index("gz")
    spot = jnp.stack([gy == 0, gy == ny - 1, mine, core, chip, gy % 2]).astype(jnp.int32)

    def to_chip(value, k):
        pairs = [(i, i ^ k) for i in range(chips)]
        return lax.ppermute(value, ("chip", "gz"), pairs)

    def plain(kernel, name, out_shape, specs, *operands, **options):
        return pl.pallas_call(
            kernel,
            out_shape=out_shape,
            in_specs=specs,
            out_specs=(vmem(),) * len(out_shape) if isinstance(out_shape, tuple) else vmem(),
            compiler_params=params(),
            name=name,
            **options,
        )(*operands)

    dma = pltpu.SemaphoreType.DMA
    block = f32(per, rows, 128)
    stacked = f32(chips, per, rows, 128)
    kappa = plain(
        pack_kappa_kernel, "pack_kappa", block, [hbm()], there(kappa2.reshape(rows, bz)),
        scratch_shapes=[dma((per,))],
    )
    kappas = [kappa] + [to_chip(kappa, k) for k in range(1, chips)]
    packed = plain(
        functools.partial(pack_probes_kernel, grid, count), "pack_probes",
        (f32(2, per, rows, 128),) * chips, [smem(), vmem(), hbm()],
        spot, kappa, there(probes.reshape(count * rows, bz)), scratch_shapes=[dma((chips, 2, per))],
    )
    probes = [packed[0]] + [to_chip(packed[k], k) for k in range(1, chips)]

    kappa = plain(
        stack_kernel, "stack_kappa", stacked,
        [vmem()] * (chips + 1), packed[0], *kappas,
    )
    other = lax.ppermute(kappa, "core", swap)
    diagonal, even_edge, odd_edge = plain(
        functools.partial(diagonal_kernel, grid), "diagonal_rows",
        (vector(DIAGONAL_HALO), edge(DIAGONAL_HALO), edge(DIAGONAL_HALO)),
        [smem(), vmem(), vmem()], spot, kappa, other,
    )
    even_diagonal = lax.ppermute(even_edge, "gy", even)
    odd_diagonal = lax.ppermute(odd_edge, "gy", odd)

    probe, give = plain(
        sort_probes_kernel, "sort_probes", (stacked, stacked),
        [smem()] + [vmem()] * (chips + 2), spot, even_diagonal, odd_diagonal, *probes,
    )
    other = lax.ppermute(give, "core", swap)
    even_edge, odd_edge = plain(
        functools.partial(edge_kernel, grid), "probe_edges", (edge(HALO), edge(HALO)),
        [smem(), vmem(), vmem()], spot, probe, other,
    )
    even1 = lax.ppermute(even_edge, "gy", even)
    odd1 = lax.ppermute(odd_edge, "gy", odd)

    cells = by * X * columns * 128

    def cost(operations):
        return pl.CostEstimate(
            flops=operations * cells, bytes_accessed=16 * cells, transcendentals=0
        )

    inner = pl.pallas_call(
        functools.partial(inner_kernel, grid),
        out_shape=tuple(vector(h) for h in (HALO, 4, 3, 2, HALO)),
        in_specs=[smem()] + [vmem()] * 3,
        out_specs=(vmem(),) * 5,
        compiler_params=params(),
        cost_estimate=cost(32),
        name="inner_steps",
    )(spot, probe, other, here(diagonal))
    vectors = [here(value) for value in (inner[0], diagonal) + tuple(inner[1:])]
    arrived = []
    for which, (halo, halo_diagonal, pairs) in enumerate(
        ((even1, even_diagonal, even), (odd1, odd_diagonal, odd))
    ):
        *vectors, edge_rows = pl.pallas_call(
            functools.partial(side_kernel, by, which),
            out_shape=tuple(vector(h) for h in (HALO, DIAGONAL_HALO, 4, 3, 2, HALO))
            + (edge(HALO),),
            in_specs=[smem()] + [vmem()] * 8,
            out_specs=(vmem(),) * 7,
            input_output_aliases={i + 1: i for i in range(6)},
            compiler_params=params(),
            cost_estimate=cost(8),
            name="side_steps_%d" % which,
        )(spot, *(here(value) for value in vectors), halo, halo_diagonal)
        arrived.append(lax.ppermute(edge_rows, "gy", pairs))
    c0, diagonal, d0, c1, d1, c2 = vectors
    even2, odd2 = arrived

    d2, moments = pl.pallas_call(
        functools.partial(middle_kernel, by),
        out_shape=(vector(4), f32(8, 128)),
        in_specs=[vmem()] * 4,
        out_specs=(vmem(),) * 2,
        compiler_params=params(),
        cost_estimate=cost(24),
        name="middle_step",
    )(here(c0), here(c1), here(c2), here(diagonal))
    shares = [moments]
    for step in range(1, ny):
        shares.append(lax.ppermute(moments, "gy", [(i, i ^ step) for i in range(ny)]))

    c3, d3, c4 = pl.pallas_call(
        functools.partial(second_inner_kernel, by),
        out_shape=tuple(vector(h) for h in (3, 2, 1)),
        in_specs=[vmem()] * 3,
        out_specs=(vmem(),) * 3,
        compiler_params=params(),
        cost_estimate=cost(30),
        name="second_inner_steps",
    )(here(diagonal), here(c2), here(d2))
    vectors = [here(value) for value in (diagonal, c2, d2, c3, d3, c4)]
    c2, d2, c3, d3, c4 = pl.pallas_call(
        functools.partial(third_kernel, by),
        out_shape=tuple(vector(h) for h in (HALO, 4, 3, 2, 1)),
        in_specs=[smem()] + [vmem()] * 8,
        out_specs=(vmem(),) * 5,
        input_output_aliases={i + 2: i for i in range(5)},
        compiler_params=params(),
        cost_estimate=cost(20),
        name="third_steps",
    )(spot, *vectors, even2, odd2)
    inverse_count = 1.0 / (ny * cells)
    vectors = [here(value) for value in (c0, diagonal, d0, c1, d1, c2, d2, c3, d3, c4)]
    if group > count:
        cotangents = jnp.where(place < count, cotangents, 0.0)

    def last_step(flip):
        return pl.pallas_call(
            functools.partial(last_kernel, grid, inverse_count, flip),
            out_shape=stacked,
            in_specs=[smem(), smem()] + [vmem()] * (10 + ny),
            out_specs=vmem(),
            compiler_params=params(),
            cost_estimate=cost(20),
            name="last_step_given" if flip else "last_step_kept",
        )(spot, cotangents, *vectors, *shares)

    got = lax.ppermute(last_step(True), "core", swap)
    parts = plain(
        add_kernel, "add_cores", (block,) * chips, [smem(), vmem(), vmem()],
        spot, last_step(False), got,
    )
    parts = [parts[0]] + [to_chip(parts[k], k) for k in range(chips - 1, 0, -1)]
    return plain(
        functools.partial(sum_kernel, grid), "sum_chips", f32(bx, by, bz), [vmem()] * chips, *parts
    )


def solution(mesh):
    nx, ny, nz = (mesh.shape[axis] for axis in ("gx", "gy", "gz"))
    devices = mesh.devices.reshape(nx // 2, 2, ny, nz)
    split = jax.sharding.Mesh(devices, ("chip", "core", "gy", "gz"))
    gx = ("chip", "core")
    return jax.shard_map(
        body,
        mesh=split,
        in_specs=(P(None, gx, "gy", "gz"), P(gx, "gy", "gz"), P()),
        out_specs=P(gx, "gy", "gz"),
        check_vma=False,
    )
```

```python
import functools

import jax
import jax.numpy as jnp
from jax import lax
from jax.experimental import pallas as pl
from jax.experimental.pallas import tpu as pltpu
from jax.sharding import PartitionSpec as P

EPSILON = 1e-06
SHIFT = 64.0
HALO = 5
DIAGONAL_HALO = 4
PAD = 8
MIB = 1024 * 1024


def loss_of_moments(moments, weights):
    m0, m1, m2, m3, m4, m5 = moments
    norm = m0 + EPSILON
    alpha1 = (m1 + SHIFT * m0) / norm
    e1 = SHIFT - alpha1
    rest1 = jnp.maximum(m2 + 2.0 * e1 * m1 + e1 * e1 * m0, 0.0)
    beta1_square = rest1 / norm + EPSILON
    beta1 = jnp.sqrt(beta1_square)
    scale = 1.0 / (norm * beta1_square)
    alpha2 = scale * (m3 + 2.0 * e1 * m2 + e1 * e1 * m1 + SHIFT * rest1) - (m1 + e1 * m0) / norm
    e2 = SHIFT - alpha2
    f1 = e1 + e2
    f0 = e1 * e2 - beta1_square
    g = f1 * f1 + 2.0 * f0
    rest2 = jnp.maximum(m4 + 2.0 * f1 * m3 + g * m2 + 2.0 * f1 * f0 * m1 + f0 * f0 * m0, 0.0)
    beta2_square = scale * rest2 + EPSILON
    beta2 = jnp.sqrt(beta2_square)
    image2 = m5 + 2.0 * f1 * m4 + g * m3 + 2.0 * f1 * f0 * m2 + f0 * f0 * m1
    cross = m3 + f1 * m2 + f0 * m1 + e1 * (m2 + f1 * m1 + f0 * m0)
    alpha3 = scale * ((image2 + SHIFT * rest2) / beta2_square - cross)
    return (
        weights[0] * alpha1
        + weights[1] * alpha2
        + weights[2] * alpha3
        + weights[3] * beta1
        + weights[4] * beta2
    )


class Field:
    def __init__(self, ref, halo):
        self.ref = ref
        self.halo = halo
        self.columns, self.rows, self.pitch, _ = ref.shape
        self.cells = self.pitch - 2 * PAD

    def load(self, column, row, x):
        return self.ref[column, row + self.halo, pl.ds(PAD + x, 8), :]

    def store(self, column, row, x, value):
        self.ref[column, row + self.halo, pl.ds(PAD + x, 8), :] = value

    def clear_pads(self):
        zero = jnp.zeros((8, 128), jnp.float32)

        def body(at, carry):
            for column in range(self.columns):
                self.ref[column, at, pl.ds(0, PAD), :] = zero
                self.ref[column, at, pl.ds(PAD + self.cells, PAD), :] = zero
            return carry

        lax.fori_loop(0, self.rows, body, 0)

    def clear_row(self, row):
        zero = jnp.zeros((8, 128), jnp.float32)
        for column in range(self.columns):
            for x in range(0, self.cells, 8):
                self.store(column, row, x, zero)


def lane_masks():
    lane = lax.broadcasted_iota(jnp.int32, (8, 128), 1)
    return lane == 0, lane == 127


def stencil_block(source, diagonal, row, rows, x, masks):
    columns = range(source.columns)
    centre = {(r, c): source.load(c, row + r, x) for r in range(-1, rows + 1) for c in columns}
    results = []
    for r in range(rows):
        after = [pltpu.roll(centre[r, c], 1, 1) for c in columns]
        before = [pltpu.roll(centre[r, c], 127, 1) for c in columns]
        for c in columns:
            low = after[c - 1] if c else 0.0
            high = before[c + 1] if c + 1 < source.columns else 0.0
            total = jnp.where(masks[0], low, after[c]) + jnp.where(masks[1], high, before[c])
            total = total + (source.load(c, row + r, x - 1) + source.load(c, row + r, x + 1))
            total = total + (centre[r - 1, c] + centre[r + 1, c])
            value = diagonal.load(c, row + r, x) * centre[r, c] - total
            results.append((c, row + r, value))
    return results


def apply_block(target, source, diagonal, row, rows, minus, masks):
    for x in range(0, source.cells, 8):
        results = stencil_block(source, diagonal, row, rows, x, masks)
        if minus is not None:
            results = [(c, r, value - SHIFT * minus.load(c, r, x)) for c, r, value in results]
        for c, r, value in results:
            target.store(c, r, x, value)


def apply_rows(target, source, diagonal, first, count, minus=None, block=4):
    masks = lane_masks()

    def body(step, carry):
        apply_block(target, source, diagonal, step * block + first, block, minus, masks)
        return carry

    lax.fori_loop(0, count // block, body, 0)
    if count % block:
        start = first + count - count % block
        apply_block(target, source, diagonal, start, count % block, minus, masks)


def apply_strips(spot_ref, own, target, source, diagonal, halo, size, minus=None):
    masks = lane_masks()

    def body(step, carry):
        row = step * (own - size + 2 * halo) - halo
        apply_block(target, source, diagonal, row, size, minus, masks)
        return carry

    lax.fori_loop(0, 2, body, 0)
    clear_outside(spot_ref, own, target)


def clear_outside(spot_ref, own, field):
    @pl.when(spot_ref[0] == 1)
    def _():
        field.clear_row(-1)

    @pl.when(spot_ref[1] == 1)
    def _():
        field.clear_row(own)


def split_chip(grid, chip):
    nz = grid[1]
    return lax.div(chip, nz), lax.rem(chip, nz)


def pack_kappa_kernel(kappa_ref, out_ref, sem):
    copies = []
    for column in range(out_ref.shape[0]):
        part = kappa_ref.at[:, pl.ds(column * 128, 128)]
        copies.append(pltpu.make_async_copy(part, out_ref.at[column], sem.at[column]))
    for copy in copies:
        copy.start()
    for copy in copies:
        copy.wait()


def pack_probes_kernel(grid, count, spot_ref, after_ref, probes_ref, *rest):
    nx, nz, bx, by, bz = grid
    rows = bx * by
    outs, sem = rest[:-1], rest[-1]
    copies = []
    for k, out in enumerate(outs):
        x, z = split_chip(grid, spot_ref[4] ^ k)
        for core in range(2):
            start = pl.multiple_of(lax.rem((2 * x + core) * nz + z, count) * rows, rows)
            for column in range(bz // 128):
                part = probes_ref.at[pl.ds(start, rows), pl.ds(column * 128, 128)]
                copies.append(
                    pltpu.make_async_copy(part, out.at[core, column], sem.at[k, core, column])
                )
    for copy in copies:
        copy.start()
    for copy in copies:
        copy.wait()


def stack_kernel(after_ref, *refs):
    for k, ref in enumerate(refs[:-1]):
        refs[-1][k] = ref[...]


def sort_probes_kernel(spot_ref, after_ref, after_too_ref, *refs):
    parts, mine_ref, give_ref = refs[:-2], refs[-2], refs[-1]
    core = spot_ref[3]
    for k, part in enumerate(parts):
        mine_ref[k] = part[core]
        give_ref[k] = part[1 - core]


def block_rows(grid, spot_ref, mine_ref, other_ref, rows):
    nx, nz, bx, by, bz = grid
    per = bz // 128
    core = spot_ref[3]
    for k in range(nx // 2 * nz):
        x, z = split_chip(grid, spot_ref[4] ^ k)
        for ref, side in ((mine_ref, core), (other_ref, 1 - core)):
            for column in range(per):
                values = [ref[k, column, pl.ds(y, bx, stride=by), :] for y in rows]
                yield (2 * x + side) * bx, z * per + column, values


def store_own(field, x, z, values):
    for y, value in enumerate(values):
        at = pl.ds(pl.multiple_of(PAD + x, 8), 8)
        field.ref[z, y + field.halo, at, :] = value


def store_edges(spot_ref, even_ref, odd_ref, x, z, first, last):
    at = pl.ds(pl.multiple_of(x, 8), 8)
    odd = spot_ref[5] == 1
    for y, (below, above) in enumerate(zip(first, last)):
        even_ref[z, y, at, :] = jnp.where(odd, below, above)
        odd_ref[z, y, at, :] = jnp.where(odd, above, below)


def edge_kernel(grid, spot_ref, mine_ref, other_ref, even_ref, odd_ref):
    by = grid[3]
    rows = list(range(HALO)) + list(range(by - HALO, by))
    for x, z, values in block_rows(grid, spot_ref, mine_ref, other_ref, rows):
        store_edges(spot_ref, even_ref, odd_ref, x, z, values[:HALO], values[HALO:])


def diagonal_kernel(grid, spot_ref, mine_ref, other_ref, own_ref, even_ref, odd_ref):
    own = Field(own_ref, DIAGONAL_HALO)
    for x, z, values in block_rows(grid, spot_ref, mine_ref, other_ref, range(grid[3])):
        values = [6.0 + value for value in values]
        store_own(own, x, z, values)
        first, last = values[:DIAGONAL_HALO], values[-DIAGONAL_HALO:]
        store_edges(spot_ref, even_ref, odd_ref, x, z, first, last)


def fill_halo(spot_ref, field, own, even_ref, odd_ref):
    odd = spot_ref[5] == 1
    for c in range(field.columns):
        for y in range(field.halo):
            for x in range(0, field.cells, 8):
                even, other = even_ref[c, y, pl.ds(x, 8), :], odd_ref[c, y, pl.ds(x, 8), :]
                field.store(c, y - field.halo, x, jnp.where(odd, even, other))
                field.store(c, own + y, x, jnp.where(odd, other, even))


def inner_kernel(
    grid, spot_ref, mine_ref, other_ref, diagonal_ref, c0_ref, d0_ref, c1_ref, d1_ref, c2_ref
):
    own = grid[3]
    c0 = Field(c0_ref, HALO)
    diagonal = Field(diagonal_ref, DIAGONAL_HALO)
    d0 = Field(d0_ref, 4)
    c1 = Field(c1_ref, 3)
    d1 = Field(d1_ref, 2)
    c2 = Field(c2_ref, HALO)
    for field in (c0, d0, c1, d1, c2):
        field.clear_pads()
    for x, z, values in block_rows(grid, spot_ref, mine_ref, other_ref, range(own)):
        store_own(c0, x, z, values)
    apply_rows(d0, c0, diagonal, 1, own - 2)
    apply_rows(c1, d0, diagonal, 2, own - 4, c0)
    apply_rows(d1, c1, diagonal, 3, own - 6)
    apply_rows(c2, d1, diagonal, 4, own - 8, c1)


def side_kernel(
    own, which,
    spot_ref, c0_in, diagonal_in, d0_in, c1_in, d1_in, c2_in, halo_ref, halo_diagonal_ref,
    c0_ref, diagonal_ref, d0_ref, c1_ref, d1_ref, c2_ref, edge_out,
):
    c0 = Field(c0_ref, HALO)
    diagonal = Field(diagonal_ref, DIAGONAL_HALO)
    d0 = Field(d0_ref, 4)
    c1 = Field(c1_ref, 3)
    d1 = Field(d1_ref, 2)
    c2 = Field(c2_ref, HALO)
    masks = lane_masks()
    above = jnp.where(spot_ref[5] == which, 1, 0)
    for field, ref in ((c0, halo_ref), (diagonal, halo_diagonal_ref)):
        base = above * (own + field.halo)
        for c in range(field.columns):
            for y in range(field.halo):
                for x in range(0, field.cells, 8):
                    field.store(c, base + (y - field.halo), x, ref[c, y, pl.ds(x, 8), :])

    def strip(target, source, halo, minus=None):
        row = above * (own - HALO + 2 * halo) - halo
        apply_block(target, source, diagonal, row, HALO, minus, masks)
        clear_outside(spot_ref, own, target)

    strip(d0, c0, 4)
    strip(c1, d0, 3, c0)
    strip(d1, c1, 2)
    strip(c2, d1, 1, c1)
    base = above * (own - HALO)
    for c in range(c2.columns):
        for x in range(0, c2.cells, 8):
            for y in range(HALO):
                edge_out[c, y, pl.ds(x, 8), :] = c2.load(c, base + y, x)


def middle_kernel(own, c0_ref, c1_ref, c2_ref, diagonal_ref, d2_ref, moments_ref):
    c0 = Field(c0_ref, HALO)
    diagonal = Field(diagonal_ref, DIAGONAL_HALO)
    c1 = Field(c1_ref, 3)
    c2 = Field(c2_ref, HALO)
    d2 = Field(d2_ref, 4)
    d2.clear_pads()
    apply_rows(d2, c2, diagonal, 0, own)

    def moment_row(row, sums):
        for x in range(0, c0.cells, 8):
            for c in range(c0.columns):
                a, b, e, d = (field.load(c, row, x) for field in (c0, c1, c2, d2))
                pairs = ((a, a), (a, b), (b, b), (b, e), (e, e), (d, d))
                sums = tuple(total + u * v for total, (u, v) in zip(sums, pairs))
        return sums

    zero = jnp.zeros((8, 128), jnp.float32)
    sums = lax.fori_loop(0, own, moment_row, (zero,) * 6)
    sums = [jnp.sum(total, axis=0, keepdims=True) for total in sums]
    moments_ref[...] = jnp.concatenate(sums + [zero[:2]], axis=0)


def moment_slopes(inverse_count, probe, weights_ref, moment_refs):
    total = moment_refs[0][...]
    for ref in moment_refs[1:]:
        total = total + ref[...]
    total = jnp.sum(total, axis=1, keepdims=True) * inverse_count
    raw = [jnp.broadcast_to(total[k : k + 1], (8, 128)) for k in range(6)]
    moments = tuple(raw[:5]) + (raw[5] - SHIFT * raw[4],)
    weights = [weights_ref[k, probe] for k in range(5)]
    value, pullback = jax.vjp(lambda m: loss_of_moments(m, weights), moments)
    (slopes,) = pullback(jnp.full((8, 128), 2.0, jnp.float32))
    return slopes


def second_inner_kernel(own, diagonal_ref, c2_ref, d2_ref, c3_ref, d3_ref, c4_ref):
    diagonal = Field(diagonal_ref, DIAGONAL_HALO)
    c2 = Field(c2_ref, HALO)
    d2 = Field(d2_ref, 4)
    c3 = Field(c3_ref, 3)
    d3 = Field(d3_ref, 2)
    c4 = Field(c4_ref, 1)
    for field in (c3, d3, c4):
        field.clear_pads()
    apply_rows(c3, d2, diagonal, 1, own - 2, c2)
    apply_rows(d3, c3, diagonal, 2, own - 4)
    apply_rows(c4, d3, diagonal, 3, own - 6, c3)


def third_kernel(
    own,
    spot_ref, diagonal_ref, c2_in, d2_in, c3_in, d3_in, c4_in, even_ref, odd_ref,
    c2_ref, d2_ref, c3_ref, d3_ref, c4_ref,
):
    diagonal = Field(diagonal_ref, DIAGONAL_HALO)
    c2 = Field(c2_ref, HALO)
    d2 = Field(d2_ref, 4)
    c3 = Field(c3_ref, 3)
    d3 = Field(d3_ref, 2)
    c4 = Field(c4_ref, 1)
    fill_halo(spot_ref, c2, own, even_ref, odd_ref)
    strips = functools.partial(apply_strips, spot_ref, own)
    strips(d2, c2, diagonal, 4, 4)
    strips(c3, d2, diagonal, 3, 4, c2)
    strips(d3, c3, diagonal, 2, 4)
    strips(c4, d3, diagonal, 1, 4, c3)


def last_kernel(
    grid, inverse_count, flip,
    spot_ref, c0_ref, diagonal_ref, d0_ref, c1_ref, d1_ref,
    c2_ref, d2_ref, c3_ref, d3_ref, c4_ref, *rest,
):
    nx, nz, bx, by, bz = grid
    per = bz // 128
    if flip:
        weights_ref, *moment_refs, out_ref, slopes_ref = rest
        slopes = moment_slopes(inverse_count, spot_ref[2], weights_ref, moment_refs)
        for k, slope in enumerate(slopes):
            slopes_ref[k] = slope
    else:
        slopes_ref, out_ref = rest
        slopes = [slopes_ref[k] for k in range(6)]
    c0 = Field(c0_ref, HALO)
    diagonal = Field(diagonal_ref, DIAGONAL_HALO)
    d0 = Field(d0_ref, 4)
    c1 = Field(c1_ref, 3)
    d1 = Field(d1_ref, 2)
    c2 = Field(c2_ref, HALO)
    d2 = Field(d2_ref, 4)
    c3 = Field(c3_ref, 3)
    d3 = Field(d3_ref, 2)
    c4 = Field(c4_ref, 1)
    masks = lane_masks()
    block = 2

    def out_rows(core, step, carry):
        row = step * block
        for chip in range(nx // 2):
            x = (2 * chip + core) * bx
            results = []
            for z, at, d4 in stencil_block(c4, diagonal, row, block, x, masks):
                cs = [field.load(z, at, x) for field in (c0, c1, c2, c3, c4)]
                ds = [field.load(z, at, x) for field in (d0, d1, d2, d3)] + [d4]
                total = None
                for i in range(5):
                    inner = None
                    for j in range(5 - i):
                        term = slopes[i + j + 1] * ds[j]
                        inner = term if inner is None else inner + term
                    term = cs[i] * inner
                    total = term if total is None else total + term
                results.append((chip * nz + z // per, z % per, at, total))
            for place, column, at, total in results:
                out_ref[place, column, pl.ds(at, bx, stride=by), :] = total
        return carry

    for core in range(2):

        @pl.when(spot_ref[3] == (1 - core if flip else core))
        def _():
            lax.fori_loop(0, by // block, functools.partial(out_rows, core), 0)


def add_kernel(spot_ref, kept_ref, got_ref, *outs):
    for k, out in enumerate(outs):
        chip = spot_ref[4] ^ k
        out[...] = kept_ref[chip] + got_ref[chip]


def sum_kernel(grid, *refs):
    nx, nz, bx, by, bz = grid
    parts, out_ref = refs[:-1], refs[-1]
    for column in range(bz // 128):
        for x in range(bx):
            total = None
            for ref in parts:
                part = ref[column, pl.ds(x * by, by), :]
                total = part if total is None else total + part
            out_ref[x, :, pl.ds(column * 128, 128)] = total


def vmem():
    return pl.BlockSpec(memory_space=pltpu.VMEM)


def smem():
    return pl.BlockSpec(memory_space=pltpu.SMEM)


def hbm():
    return pl.BlockSpec(memory_space=pltpu.HBM)


def here(value):
    return pltpu.with_memory_space_constraint(value, pltpu.VMEM)


def there(value):
    return pltpu.with_memory_space_constraint(value, pltpu.HBM)


def f32(*shape):
    return jax.ShapeDtypeStruct(shape, jnp.float32)


def params():
    return pltpu.CompilerParams(vmem_limit_bytes=12 * MIB)


def body(probes, kappa2, cotangents):
    nx, ny, nz = (lax.axis_size(axis) for axis in (("chip", "core"), "gy", "gz"))
    count, bx, by, bz = probes.shape
    group = nx * nz
    assert group % count == 0 and nx % 2 == 0 and bx == 8 and bz == 256
    assert by % 8 == 0 and by >= HALO
    X = nx * bx
    columns = nz * bz // 128
    per = bz // 128
    rows = bx * by
    grid = (nx, nz, bx, by, bz)
    core, gy = lax.axis_index("core"), lax.axis_index("gy")
    place = (lax.axis_index("chip") * 2 + core) * nz + lax.axis_index("gz")
    mine = place % count
    assert ny & (ny - 1) == 0
    even = [(i, i ^ 1) for i in range(ny)]
    odd = [(i, i + 1 if i % 2 else i - 1) for i in range(1, ny - 1)]
    swap = [(0, 1), (1, 0)]

    def edge(halo):
        return f32(columns, halo, X, 128)

    def padded(halo):
        return (columns, by + 2 * halo, X + 2 * PAD, 128)

    def vector(halo):
        return pltpu.VMEM(padded(halo), jnp.float32)

    chips = nx // 2 * nz
    assert chips & (chips - 1) == 0
    chip = lax.axis_index("chip") * nz + lax.axis_index("gz")
    spot = jnp.stack([gy == 0, gy == ny - 1, mine, core, chip, gy % 2]).astype(jnp.int32)

    def to_chip(value, k):
        pairs = [(i, i ^ k) for i in range(chips)]
        return lax.ppermute(value, ("chip", "gz"), pairs)

    def plain(kernel, name, out_shape, specs, *operands, **options):
        return pl.pallas_call(
            kernel,
            out_shape=out_shape,
            in_specs=specs,
            out_specs=(vmem(),) * len(out_shape) if isinstance(out_shape, tuple) else vmem(),
            compiler_params=params(),
            name=name,
            **options,
        )(*operands)

    dma = pltpu.SemaphoreType.DMA
    block = f32(per, rows, 128)
    stacked = f32(chips, per, rows, 128)
    kappa = plain(
        pack_kappa_kernel, "pack_kappa", block, [hbm()], there(kappa2.reshape(rows, bz)),
        scratch_shapes=[dma((per,))],
    )
    kappas = [kappa] + [to_chip(kappa, k) for k in range(1, chips)]
    packed = plain(
        functools.partial(pack_probes_kernel, grid, count), "pack_probes",
        (f32(2, per, rows, 128),) * chips, [smem(), vmem(), hbm()],
        spot, kappa, there(probes.reshape(count * rows, bz)), scratch_shapes=[dma((chips, 2, per))],
    )
    probes = [packed[0]] + [to_chip(packed[k], k) for k in range(1, chips)]

    kappa = plain(
        stack_kernel, "stack_kappa", stacked,
        [vmem()] * (chips + 1), packed[0], *kappas,
    )
    other = lax.ppermute(kappa, "core", swap)
    diagonal, even_edge, odd_edge = plain(
        functools.partial(diagonal_kernel, grid), "diagonal_rows",
        (vector(DIAGONAL_HALO), edge(DIAGONAL_HALO), edge(DIAGONAL_HALO)),
        [smem(), vmem(), vmem()], spot, kappa, other,
    )
    even_diagonal = lax.ppermute(even_edge, "gy", even)
    odd_diagonal = lax.ppermute(odd_edge, "gy", odd)

    probe, give = plain(
        sort_probes_kernel, "sort_probes", (stacked, stacked),
        [smem()] + [vmem()] * (chips + 2), spot, even_diagonal, odd_diagonal, *probes,
    )
    other = lax.ppermute(give, "core", swap)
    even_edge, odd_edge = plain(
        functools.partial(edge_kernel, grid), "probe_edges", (edge(HALO), edge(HALO)),
        [smem(), vmem(), vmem()], spot, probe, other,
    )
    even1 = lax.ppermute(even_edge, "gy", even)
    odd1 = lax.ppermute(odd_edge, "gy", odd)

    cells = by * X * columns * 128

    def cost(operations):
        return pl.CostEstimate(
            flops=operations * cells, bytes_accessed=16 * cells, transcendentals=0
        )

    inner = pl.pallas_call(
        functools.partial(inner_kernel, grid),
        out_shape=tuple(vector(h) for h in (HALO, 4, 3, 2, HALO)),
        in_specs=[smem()] + [vmem()] * 3,
        out_specs=(vmem(),) * 5,
        compiler_params=params(),
        cost_estimate=cost(32),
        name="inner_steps",
    )(spot, probe, other, here(diagonal))
    vectors = [here(value) for value in (inner[0], diagonal) + tuple(inner[1:])]
    arrived = []
    for which, (halo, halo_diagonal, pairs) in enumerate(
        ((even1, even_diagonal, even), (odd1, odd_diagonal, odd))
    ):
        *vectors, edge_rows = pl.pallas_call(
            functools.partial(side_kernel, by, which),
            out_shape=tuple(vector(h) for h in (HALO, DIAGONAL_HALO, 4, 3, 2, HALO))
            + (edge(HALO),),
            in_specs=[smem()] + [vmem()] * 8,
            out_specs=(vmem(),) * 7,
            input_output_aliases={i + 1: i for i in range(6)},
            compiler_params=params(),
            cost_estimate=cost(8),
            name="side_steps_%d" % which,
        )(spot, *(here(value) for value in vectors), halo, halo_diagonal)
        arrived.append(lax.ppermute(edge_rows, "gy", pairs))
    c0, diagonal, d0, c1, d1, c2 = vectors
    even2, odd2 = arrived

    d2, moments = pl.pallas_call(
        functools.partial(middle_kernel, by),
        out_shape=(vector(4), f32(8, 128)),
        in_specs=[vmem()] * 4,
        out_specs=(vmem(),) * 2,
        compiler_params=params(),
        cost_estimate=cost(24),
        name="middle_step",
    )(here(c0), here(c1), here(c2), here(diagonal))
    shares = [moments]
    for step in range(1, ny):
        shares.append(lax.ppermute(moments, "gy", [(i, i ^ step) for i in range(ny)]))

    c3, d3, c4 = pl.pallas_call(
        functools.partial(second_inner_kernel, by),
        out_shape=tuple(vector(h) for h in (3, 2, 1)),
        in_specs=[vmem()] * 3,
        out_specs=(vmem(),) * 3,
        compiler_params=params(),
        cost_estimate=cost(30),
        name="second_inner_steps",
    )(here(diagonal), here(c2), here(d2))
    vectors = [here(value) for value in (diagonal, c2, d2, c3, d3, c4)]
    c2, d2, c3, d3, c4 = pl.pallas_call(
        functools.partial(third_kernel, by),
        out_shape=tuple(vector(h) for h in (HALO, 4, 3, 2, 1)),
        in_specs=[smem()] + [vmem()] * 8,
        out_specs=(vmem(),) * 5,
        input_output_aliases={i + 2: i for i in range(5)},
        compiler_params=params(),
        cost_estimate=cost(20),
        name="third_steps",
    )(spot, *vectors, even2, odd2)
    inverse_count = 1.0 / (ny * cells)
    vectors = [here(value) for value in (c0, diagonal, d0, c1, d1, c2, d2, c3, d3, c4)]
    if group > count:
        cotangents = jnp.where(place < count, cotangents, 0.0)

    def last_step(flip, out_shape, specs, *operands):
        return plain(
            functools.partial(last_kernel, grid, inverse_count, flip),
            "last_step_given" if flip else "last_step_kept", out_shape,
            [smem()] + [vmem()] * 10 + specs, spot, *vectors, *operands,
        )

    given, slopes = last_step(
        True, (stacked, f32(6, 8, 128)), [smem()] + [vmem()] * ny, cotangents, *shares
    )
    got = lax.ppermute(given, "core", swap)
    kept = last_step(False, stacked, [vmem()], slopes)
    parts = plain(
        add_kernel, "add_cores", (block,) * chips, [smem(), vmem(), vmem()],
        spot, kept, got,
    )
    parts = [parts[0]] + [to_chip(parts[k], k) for k in range(chips - 1, 0, -1)]
    return plain(
        functools.partial(sum_kernel, grid), "sum_chips", f32(bx, by, bz), [vmem()] * chips, *parts
    )


def solution(mesh):
    nx, ny, nz = (mesh.shape[axis] for axis in ("gx", "gy", "gz"))
    devices = mesh.devices.reshape(nx // 2, 2, ny, nz)
    split = jax.sharding.Mesh(devices, ("chip", "core", "gy", "gz"))
    gx = ("chip", "core")
    return jax.shard_map(
        body,
        mesh=split,
        in_specs=(P(None, gx, "gy", "gz"), P(gx, "gy", "gz"), P()),
        out_specs=P(gx, "gy", "gz"),
        check_vma=False,
    )
```
